128 devices in a mesh: row: 16 (over x_hi, z, core), col: 8 (over y, x_lo).
Axes of the slice: x: 4 (x_hi: 2, x_lo: 2; x = x_hi * 2 + x_lo), y: 4, z: 4, core: 2. Of those that a mesh axis runs over, the one named last changes fastest.
Arguments:
- image_embed: float32 [16384, 1152], P(('row', 'col')), may hold values from -6 to 6
- text_embed: float32 [16384, 1152], P(('row', 'col')), may hold values from -6 to 6
- exponent_of_sharpness: float32 [1], replicated, may hold values from 3 to 3.7
- bias: float32 [1], replicated, may hold values from -6 to -4
Outputs:
- loss_value: float32 [], replicated
- grad_image: float32 [16384, 1152], P(('row', 'col'))
- grad_text: float32 [16384, 1152], P(('row', 'col'))
The draws below stay inside these ranges and needn't reach their ends.
All inputs are finite; a program needn't handle non-finite values.
Results may differ from the reference program's by a relative error of at most 0.0011.
Values may be sent and summed in bfloat16 or wider, within the bound.
No kernel may reach another device: no remote copies, remote signals or barrier semaphores. Data moves between devices by JAX's collectives and lax.ppermute only.
A program may use at most 128 MiB of HBM per device.

```python
import jax
import jax.numpy as jnp
from jax import lax

D = 1152
IMG_DEV = 128
BATCH = 16384
N_COL = 8


def shared_base(key):
    return jnp.clip(jax.random.normal(key, (BATCH, D), jnp.float32), -6.0, 6.0)


def common_direction(key):
    signs = jax.random.randint(jax.random.fold_in(key, 5), (1, D), 0, 2).astype(jnp.float32)
    return (2.0 * signs - 1.0) * D ** (-0.5)


def alignment(top):
    return top * (jnp.arange(BATCH, dtype=jnp.float32) / BATCH)[:, None]


def draw_image_embed(key, part):
    base = shared_base(key)
    direction = common_direction(key)
    return base * D ** (-0.5) + alignment(0.2) * direction


def draw_text_embed(key, part):
    base = shared_base(key)
    direction = common_direction(key)
    key = jax.random.fold_in(key, 23)
    noise_key = jax.random.fold_in(key, 0)
    noise = jax.random.normal(noise_key, (BATCH, D), jnp.float32)
    tied = alignment(0.35)
    mixed = jnp.clip(tied * base + jnp.sqrt(1.0 - tied * tied) * noise, -6.0, 6.0)
    return mixed * D ** (-0.5) + 0.3 * direction


def setup_inputs(seed: int = 0) -> dict:
    key_list = jax.random.split(jax.random.key(seed), 5)
    return {
        "image_embed": draw_image_embed(jax.random.fold_in(key_list[4], 71), 0),
        "text_embed": draw_text_embed(jax.random.fold_in(key_list[4], 71), 0),
        "exponent_of_sharpness": jnp.clip(jax.random.uniform(key_list[2], (1,), jnp.float32, 3.0, 3.7), 3.0, 3.7),
        "bias": jnp.clip(jax.random.uniform(key_list[3], (1,), jnp.float32, -6.0, -4.0), -6.0, -4.0),
    }


def normalize(raw):
    sumsq = lax.optimization_barrier(jnp.sum(raw * raw, axis=1, keepdims=True))
    scale_rows = lax.rsqrt(sumsq + 1e-06)
    return (raw * scale_rows, scale_rows)

def couple_contributions(picture_first_entry, sentence_first_entry, picture_ordinals, sentence_ordinals, sharpness_factor, beginning_position):
    similarity_entries = lax.dot_general(picture_first_entry, sentence_first_entry, (((1,), (1,)), ((), ())), preferred_element_type=jnp.float32)
    similarity_grid = sharpness_factor * similarity_entries + beginning_position
    matching_indicator = picture_ordinals[:, None] == sentence_ordinals[None, :]
    penalty_piece = jnp.sum(jnp.where(matching_indicator, jax.nn.softplus(-similarity_grid), jax.nn.softplus(similarity_grid)))
    coefficient_piece = (sharpness_factor * (jax.nn.sigmoid(similarity_grid) - matching_indicator.astype(jnp.float32))).astype(jnp.bfloat16)
    return (coefficient_piece, penalty_piece)

def finish(unit, scale_rows, summed):
    return (summed - unit * lax.optimization_barrier(jnp.sum(unit * summed, axis=1, keepdims=True))) * scale_rows

def reference(image_embed, text_embed, exponent_of_sharpness, bias):
    img_unit, img_scale = normalize(image_embed)
    txt_unit, txt_scale = normalize(text_embed)
    picture_first_entry = img_unit.astype(jnp.bfloat16)
    sentence_first_entry = txt_unit.astype(jnp.bfloat16)
    sharpness_factor = jnp.exp(exponent_of_sharpness[0])
    beginning_position = bias[0]
    block_rows = IMG_DEV * N_COL
    blocks = BATCH // block_rows
    img_blocks = picture_first_entry.reshape(blocks, block_rows, D)
    sentence_ordinals = jnp.arange(BATCH, dtype=jnp.int32)

    def visit(state_now, item):
        txt_sum, loss_now = state_now
        picture_tile, block_index = item
        picture_ordinals = block_index * block_rows + jnp.arange(block_rows, dtype=jnp.int32)
        coefficient_piece, penalty_piece = couple_contributions(picture_tile, sentence_first_entry, picture_ordinals, sentence_ordinals, sharpness_factor, beginning_position)
        img_part = jnp.dot(coefficient_piece, sentence_first_entry, preferred_element_type=jnp.float32)
        txt_sum = txt_sum + lax.dot_general(coefficient_piece, picture_tile, (((0,), (0,)), ((), ())), preferred_element_type=jnp.float32)
        return ((txt_sum, loss_now + penalty_piece), img_part)
    start_state = (jnp.zeros((BATCH, D), jnp.float32), jnp.zeros((), jnp.float32))
    (txt_sum, loss_sum), img_parts = lax.scan(visit, start_state, (img_blocks, jnp.arange(blocks, dtype=jnp.int32)))
    img_sum = img_parts.reshape(BATCH, D)
    loss_value = loss_sum / BATCH
    return (loss_value, finish(img_unit, img_scale, img_sum), finish(txt_unit, txt_scale, txt_sum))
```

```python
import jax
import jax.numpy as jnp
from jax import lax
from jax.experimental import pallas as pl
from jax.experimental.pallas import tpu as pltpu
from jax.sharding import PartitionSpec as P

VMEM = pl.BlockSpec(memory_space=pltpu.VMEM)
SMEM = pl.BlockSpec(memory_space=pltpu.SMEM)
MIB = 1024 * 1024
BLOCK = 256
TINY = 1.1754944e-38
AXES = ("row", "col")
ROWS, COLS = 16, 8
ONE_CHIP, TWO_CHIPS, FOUR_CHIPS = 0.5, 0.25, 0.125
PARTNERS = {"x": ((0, 1), (8, 1)), "a": ((0, 2), (2, 0)), "b": ((0, 6), (6, 0))}


def exchange(x, bits_of_core):
    pairs = []
    for row in range(ROWS):
        for col in range(COLS):
            row_bits, col_bits = bits_of_core[row & 1]
            pairs.append((row * COLS + col, (row ^ row_bits) * COLS + (col ^ col_bits)))
    return lax.ppermute(x, AXES, pairs)


def move(x, step):
    return exchange(x, PARTNERS[step])


def swap(x, row_bits=1, col_bits=0):
    return exchange(x, ((row_bits, col_bits),) * 2)


def which_core():
    pairs = []
    for row in range(0, ROWS, 2):
        for col in range(COLS):
            pairs.append((row * COLS + col, (row + 1) * COLS + col))
    flag = lax.ppermute(jnp.ones((8, 128), jnp.float32), AXES, pairs)
    return flag[0, :1].astype(jnp.int32)


def encode(x, shift):
    y = x * shift
    y2 = y * y
    y4 = y2 * y2
    return (y4 * y2 * (y * jnp.abs(y))).astype(jnp.bfloat16)


def decode(e, shift):
    f = e.astype(jnp.float32)
    size = jnp.exp2(jnp.log2(jnp.maximum(jnp.abs(f), TINY)) * 0.125)
    return jnp.where(f < 0.0, -size, size) * (1.0 / shift)


def row_scale(raw):
    return lax.rsqrt(jnp.sum(raw * raw, axis=1, keepdims=True) + 1e-06)


def by_core(core_ref, work):
    pl.when(core_ref[0] == 0)(lambda: work(True))
    pl.when(core_ref[0] != 0)(lambda: work(False))


def normalize_kernel(img_ref, txt_ref, low_ref):
    own = img_ref.shape[0]
    for k, ref in enumerate((txt_ref, img_ref)):
        raw = ref[...]
        low_ref[k * own : (k + 1) * own] = (raw * row_scale(raw)).astype(jnp.bfloat16)


def normalize(img, txt):
    own, features = img.shape
    return pl.pallas_call(
        normalize_kernel,
        out_shape=jax.ShapeDtypeStruct((2 * own, features), jnp.bfloat16),
        in_specs=[VMEM, VMEM],
        out_specs=VMEM,
        compiler_params=pltpu.CompilerParams(vmem_limit_bytes=6 * MIB),
        name="normalize",
    )(img, txt)


def own_kind_kernel(core_ref, mine_ref, other_ref, out_ref):
    own = mine_ref.shape[0] // 2

    def work(is_first):
        rows = slice(0, own) if is_first else slice(own, 2 * own)
        out_ref[:own] = mine_ref[rows]
        out_ref[own:] = other_ref[rows]

    by_core(core_ref, work)


def pack_kernel(*refs):
    out_ref = refs[-1]
    start = 0
    for ref in refs[:-1]:
        out_ref[start : start + ref.shape[0]] = ref[...]
        start += ref.shape[0]


def pack(*pieces):
    shape = (sum(p.shape[0] for p in pieces), pieces[0].shape[1])
    return pl.pallas_call(
        pack_kernel,
        out_shape=jax.ShapeDtypeStruct(shape, pieces[0].dtype),
        in_specs=[VMEM] * len(pieces),
        out_specs=VMEM,
        compiler_params=pltpu.CompilerParams(vmem_limit_bytes=8 * MIB),
        name="pack",
    )(*pieces)


def tile_body(pair, first, on_first, sharp_ref, bias_ref, img_ref, txt_ref, copy_ref, before_ref, weights_refs, part_ref, loss_ref):
    rows = img_ref.shape[0]
    cols = txt_ref.shape[0]
    sharp = jnp.exp(jnp.full((1, cols), sharp_ref[0], jnp.float32))
    bias = bias_ref[0]

    def products(c):
        return lax.dot_general(
            img_ref[c * BLOCK : (c + 1) * BLOCK],
            txt_ref[...],
            (((1,), (1,)), ((), ())),
            preferred_element_type=jnp.float32,
        )

    loss = jnp.zeros((8, cols), jnp.float32)
    following = products(0)
    for c in range(rows // BLOCK):
        current = following
        if (c + 1) * BLOCK < rows:
            following = products(c + 1)
        logits = current * sharp + bias
        grown = jnp.exp(logits)
        one_more = 1.0 + grown
        weights = sharp * (grown / one_more)
        span = slice(c * BLOCK, (c + 1) * BLOCK)
        low = weights.astype(jnp.bfloat16)
        start = 0
        for ref in weights_refs:
            ref[span] = low[:, start : start + ref.shape[1]]
            start += ref.shape[1]
        logs = jnp.log(one_more[: BLOCK // 2] * one_more[BLOCK // 2 :])
        loss = loss + jnp.sum(logs.reshape(BLOCK // 16, 8, cols), axis=0)
        if first:
            copy_ref[span] = img_ref[span]
        if c == 0 and first and on_first:
            row_ids = lax.broadcasted_iota(jnp.int32, (pair, pair), 0)
            col_ids = lax.broadcasted_iota(jnp.int32, (pair, pair), 1)
            wanted = jnp.where(row_ids < pair // 2, row_ids + pair // 2, row_ids - pair // 2)
            same = wanted == col_ids
            corner = weights[:pair, :pair] - jnp.where(same, sharp[:, :pair], 0.0)
            weights_refs[0][:pair, :pair] = corner.astype(jnp.bfloat16)
            matched = jnp.where(same, logits[:pair, :pair], 0.0)
            matched = jnp.sum(matched.reshape(pair // 8, 8, pair), axis=0)
        part = None if first else before_ref[span]
        start = 0
        for ref in weights_refs:
            more = jnp.dot(
                ref[span], txt_ref[start : start + ref.shape[1]], preferred_element_type=jnp.float32
            )
            part = more if part is None else part + more
            start += ref.shape[1]
        part_ref[span] = part
    loss_ref[...] = loss
    if first and on_first:
        loss_ref[:, :pair] = loss[:, :pair] - matched


def first_tile_kernel(pair, core_ref, sharp_ref, bias_ref, near_ref, received_ref, far_ref, img_ref, weights_ref, part_ref, loss_ref):
    def work(is_first):
        img, txt = (received_ref, near_ref) if is_first else (far_ref, received_ref)
        tile_body(
            pair, True, is_first, sharp_ref, bias_ref, img, txt, img_ref, None, (weights_ref,), part_ref, loss_ref
        )

    by_core(core_ref, work)


def second_tile_kernel(core_ref, sharp_ref, bias_ref, far_ref, received_ref, img_ref, before_ref, left_ref, right_ref, part_ref, loss_ref):
    def work(is_first):
        txt = far_ref if is_first else received_ref
        weights = (left_ref, right_ref)
        tile_body(
            0, False, is_first, sharp_ref, bias_ref, img_ref, txt, None, before_ref, weights, part_ref, loss_ref
        )

    by_core(core_ref, work)


def tile_call(kernel, name, scalars, arrays, outs):
    rows, features = arrays[0].shape
    return pl.pallas_call(
        kernel,
        out_shape=outs,
        in_specs=[SMEM] * len(scalars) + [VMEM] * len(arrays),
        out_specs=(VMEM,) * len(outs),
        compiler_params=pltpu.CompilerParams(vmem_limit_bytes=24 * MIB),
        cost_estimate=pl.CostEstimate(
            flops=4 * rows * rows * features,
            bytes_accessed=4 * rows * features + 2 * rows * rows,
            transcendentals=3 * rows * rows,
        ),
        name=name,
    )(*scalars, *arrays)


def small_call(kernel, name, core, arrays, outs):
    size = sum(x.size * x.dtype.itemsize for x in (*arrays, *outs))
    return pl.pallas_call(
        kernel,
        out_shape=outs,
        in_specs=[SMEM] + [VMEM] * len(arrays),
        out_specs=(VMEM,) * len(outs),
        compiler_params=pltpu.CompilerParams(vmem_limit_bytes=size + 4 * MIB),
        name=name,
    )(core, *arrays)


def opposite_kernel(core_ref, txt_ref, img_ref, received_ref, a_ref, b_ref):
    pair = a_ref.shape[0]

    def work(is_first):
        for k, ref in enumerate((a_ref, b_ref)):
            rows = slice(k * pair, (k + 1) * pair)
            value = txt_ref[rows] + decode(received_ref[rows], ONE_CHIP) if is_first else img_ref[rows]
            ref[...] = encode(value, ONE_CHIP)

    by_core(core_ref, work)


def far_kernel(core_ref, txt_ref, img_ref, received_ref, through_ref, a_ref, b_ref):
    pair = a_ref.shape[0]

    def work(is_first):
        for k, ref in enumerate((a_ref, b_ref)):
            rows = slice(k * pair, (k + 1) * pair)
            if is_first:
                value = txt_ref[rows] + decode(received_ref[rows], ONE_CHIP)
            else:
                value = img_ref[2 * pair + k * pair : 3 * pair + k * pair]
            if k == 0:
                value = value + decode(through_ref[...], ONE_CHIP)
            ref[...] = encode(value, TWO_CHIPS)

    by_core(core_ref, work)


def near_kernel(core_ref, txt_ref, received_ref, low_ref, high_ref, through_ref, a_ref, b_ref, own_ref, x_ref):
    pair = a_ref.shape[0]

    def work(is_first):
        for k in range(4):
            rows = slice(k * pair, (k + 1) * pair)
            if is_first:
                value = txt_ref[rows] + decode(received_ref[rows], ONE_CHIP)
            elif k < 2:
                value = decode(low_ref[rows], ONE_CHIP)
            else:
                value = decode(high_ref[(k - 2) * pair : (k - 1) * pair], ONE_CHIP)
            if k == 0:
                own_ref[...] = value
            elif k == 1:
                x_ref[...] = value
            elif k == 2:
                a_ref[...] = encode(value, TWO_CHIPS)
            else:
                b_ref[...] = encode(value + decode(through_ref[...], ONE_CHIP), TWO_CHIPS)

    by_core(core_ref, work)


def across_kernel(core_ref, kept_ref, a_ref, b_ref, out_ref):
    total = kept_ref[...] + decode(a_ref[...], TWO_CHIPS) + decode(b_ref[...], TWO_CHIPS)
    out_ref[...] = encode(total, FOUR_CHIPS)


def gather_sums_kernel(core_ref, kept_ref, a_ref, b_ref, x_ref, keep_ref, give_ref):
    own = keep_ref.shape[0]
    for start, ref in ((0, keep_ref), (own, give_ref)):
        rows = slice(start, start + own)
        total = kept_ref[rows] + decode(x_ref[rows], FOUR_CHIPS)
        ref[...] = total + decode(a_ref[rows], TWO_CHIPS) + decode(b_ref[rows], TWO_CHIPS)


def finish_kernel(core_ref, img_ref, txt_ref, kept_ref, received_ref, grad_img_ref, grad_txt_ref):
    def side(raw_ref, sum_ref, grad_ref):
        raw = raw_ref[...]
        scale = row_scale(raw)
        unit = raw * scale
        summed = sum_ref[...]
        grad_ref[...] = (summed - unit * jnp.sum(unit * summed, axis=1, keepdims=True)) * scale

    @pl.when(core_ref[0] == 0)
    def _():
        side(img_ref, received_ref, grad_img_ref)
        side(txt_ref, kept_ref, grad_txt_ref)

    @pl.when(core_ref[0] != 0)
    def _():
        side(img_ref, kept_ref, grad_img_ref)
        side(txt_ref, received_ref, grad_txt_ref)


def finish(core, img, txt, kept, received):
    grad = jax.ShapeDtypeStruct(img.shape, jnp.float32)
    return pl.pallas_call(
        finish_kernel,
        out_shape=(grad, grad),
        in_specs=[SMEM] + [VMEM] * 4,
        out_specs=(VMEM, VMEM),
        compiler_params=pltpu.CompilerParams(vmem_limit_bytes=8 * MIB),
        name="finish",
    )(core, img, txt, kept, received)


def transposed_product(weights, img):
    return lax.dot_general(
        weights, img, (((0,), (0,)), ((), ())), preferred_element_type=jnp.float32
    )


def body(image_embed, text_embed, exponent_of_sharpness, bias):
    own, features = image_embed.shape
    pair = 2 * own
    count = 4 * pair
    batch = own * ROWS * COLS
    core = which_core()
    on_first = core[0] == 0
    half = jax.ShapeDtypeStruct((own, features), jnp.float32)
    piece = jax.ShapeDtypeStruct((pair, features), jnp.bfloat16)
    whole = jax.ShapeDtypeStruct((pair, features), jnp.float32)
    part = jax.ShapeDtypeStruct((count, features), jnp.float32)
    losses = jax.ShapeDtypeStruct((8, count), jnp.float32)

    mine = normalize(image_embed, text_embed)
    (low,) = small_call(own_kind_kernel, "own_kind", core, (mine, swap(mine)), (piece,))
    slot_x = move(low, "x")
    slot_1, slot_3 = move(low, "a"), move(low, "b")
    slot_x1, slot_x3 = move(slot_x, "a"), move(slot_x, "b")
    slot_2 = move(slot_1, "b")
    slot_x1, slot_x3, low, slot_x, slot_1, slot_3 = lax.optimization_barrier(
        (slot_x1, slot_x3, low, slot_x, slot_1, slot_3)
    )
    slot_x2 = move(slot_x3, "a")
    near = pack(low, slot_x, slot_1, slot_3)
    near_received = swap(near)
    far = pack(slot_2, slot_x2, slot_x1, slot_x3)
    far_received = swap(far)

    scalars = (core, exponent_of_sharpness, bias)
    img, near_weights, img_part, near_loss = tile_call(
        lambda *refs: first_tile_kernel(pair, *refs),
        "tile_first",
        scalars,
        (near, near_received, far),
        (
            jax.ShapeDtypeStruct((count, features), jnp.bfloat16),
            jax.ShapeDtypeStruct((count, count), jnp.bfloat16),
            part,
            losses,
        ),
    )
    half_weights = jax.ShapeDtypeStruct((count, count // 2), jnp.bfloat16)
    opposite_weights, far_weights, img_part, far_loss = tile_call(
        second_tile_kernel,
        "tile_second",
        scalars,
        (far, far_received, img, img_part),
        (half_weights, half_weights, part, losses),
    )
    loss = jnp.sum((near_loss + far_loss).reshape(8, -1, 128), axis=1)

    loss = loss + swap(loss)
    opposite_part = transposed_product(opposite_weights, img)
    sent = encode(jnp.where(on_first, img_part[2 * pair :], opposite_part), ONE_CHIP)
    sent, far_weights = lax.optimization_barrier((sent, far_weights))
    high_received = swap(sent)
    far_part = transposed_product(far_weights, img)
    sent = encode(jnp.where(on_first, img_part[: 2 * pair], far_part), ONE_CHIP)
    high_received, sent, loss = lax.optimization_barrier((high_received, sent, loss))

    a, b = small_call(
        opposite_kernel, "opposite", core, (opposite_part, img_part, high_received), (piece, piece)
    )
    a, b, sent, near_weights = lax.optimization_barrier((a, b, sent, near_weights))
    through_a, through_b = move(a, "a"), move(b, "b")
    low_received = swap(sent)
    near_part = transposed_product(near_weights, img)
    sent = encode(near_part, ONE_CHIP)
    loss = loss + swap(loss, 0, 1)
    loss = loss + swap(loss, 8, 1)
    through_a, through_b, low_received, sent, loss = lax.optimization_barrier(
        (through_a, through_b, low_received, sent, loss)
    )

    a, b = small_call(
        far_kernel, "far", core, (far_part, img_part, low_received, through_b), (piece, piece)
    )
    a, b, sent = lax.optimization_barrier((a, b, sent))
    from_a, from_b = move(a, "a"), move(b, "b")
    near_received = swap(sent)
    loss = loss + swap(loss, 0, 2)
    a, b, kept, kept_x = small_call(
        near_kernel,
        "near",
        core,
        (near_part, near_received, low_received, high_received, through_a),
        (piece, piece, whole, whole),
    )
    a, b, kept, kept_x, loss = lax.optimization_barrier((a, b, kept, kept_x, loss))
    loss = loss + swap(loss, 0, 6)
    from_a, from_b, a, b, loss = lax.optimization_barrier((from_a, from_b, a, b, loss))

    near_a, near_b = move(a, "a"), move(b, "b")
    (crossing,) = small_call(across_kernel, "across", core, (kept_x, from_a, from_b), (piece,))
    crossed = move(crossing, "x")
    loss = loss + swap(loss, 2, 0)
    loss = loss + swap(loss, 6, 0)
    near_a, near_b, loss = lax.optimization_barrier((near_a, near_b, loss))
    keep, give = small_call(
        gather_sums_kernel, "gather_sums", core, (kept, near_a, near_b, crossed), (half, half)
    )
    grad_image, grad_text = finish(core, image_embed, text_embed, keep, swap(give))
    return (jnp.sum(loss) / batch, grad_image, grad_text)


def solution(mesh):
    in_specs = (P(("row", "col"), None), P(("row", "col"), None), P(), P())
    out_specs = (P(), P(("row", "col"), None), P(("row", "col"), None))
    return jax.shard_map(body, mesh=mesh, in_specs=in_specs, out_specs=out_specs, check_vma=False)
```

```python
import jax
import jax.numpy as jnp
from jax import lax
from jax.experimental import pallas as pl
from jax.experimental.pallas import tpu as pltpu
from jax.sharding import PartitionSpec as P

VMEM = pl.BlockSpec(memory_space=pltpu.VMEM)
SMEM = pl.BlockSpec(memory_space=pltpu.SMEM)
HBM = pl.BlockSpec(memory_space=pltpu.HBM)
MIB = 1024 * 1024
BLOCK = 256
TINY = 1.1754944e-38
AXES = ("row", "col")
ROWS, COLS = 16, 8
ONE_CHIP, TWO_CHIPS, FOUR_CHIPS = 0.5, 0.25, 0.125
PARTNERS = {"x": ((0, 1), (8, 1)), "a": ((0, 2), (2, 0)), "b": ((0, 6), (6, 0))}


def exchange(x, bits_of_core):
    pairs = []
    for row in range(ROWS):
        for col in range(COLS):
            row_bits, col_bits = bits_of_core[row & 1]
            pairs.append((row * COLS + col, (row ^ row_bits) * COLS + (col ^ col_bits)))
    return lax.ppermute(x, AXES, pairs)


def move(x, step):
    return exchange(x, PARTNERS[step])


def swap(x, row_bits=1, col_bits=0):
    return exchange(x, ((row_bits, col_bits),) * 2)


def encode(x, shift):
    y = x * shift
    y2 = y * y
    y4 = y2 * y2
    return (y4 * y2 * (y * jnp.abs(y))).astype(jnp.bfloat16)


def decode(e, shift):
    f = e.astype(jnp.float32)
    size = jnp.exp2(jnp.log2(jnp.maximum(jnp.abs(f), TINY)) * 0.125)
    return jnp.where(f < 0.0, -size, size) * (1.0 / shift)


def row_scale(raw):
    return lax.rsqrt(jnp.sum(raw * raw, axis=1, keepdims=True) + 1e-06)


def by_core(core_ref, work):
    pl.when(core_ref[0] == 0)(lambda: work(True))
    pl.when(core_ref[0] != 0)(lambda: work(False))


def normalize_kernel(core_ref, img_ref, txt_ref, keep_ref, give_ref, raw_ref, sems):
    copies = [
        pltpu.make_async_copy(source, raw_ref.at[k], sems.at[k])
        for k, source in enumerate((txt_ref, img_ref))
    ]
    for copy in copies:
        copy.start()

    def low(k):
        raw = raw_ref[k]
        return (raw * row_scale(raw)).astype(jnp.bfloat16)

    for k, copy in enumerate(copies):
        copy.wait()

        def work(is_first, k=k):
            ref = keep_ref if (k == 0) == is_first else give_ref
            ref[...] = low(k)

        by_core(core_ref, work)


def normalize(core, img, txt):
    low = jax.ShapeDtypeStruct(img.shape, jnp.bfloat16)
    return pl.pallas_call(
        normalize_kernel,
        out_shape=(low, low),
        in_specs=[SMEM, HBM, HBM],
        out_specs=(VMEM, VMEM),
        scratch_shapes=[pltpu.VMEM((2, *img.shape), jnp.float32), pltpu.SemaphoreType.DMA((2,))],
        compiler_params=pltpu.CompilerParams(vmem_limit_bytes=6 * MIB),
        name="normalize",
    )(core, img, txt)


def pack_kernel(*refs):
    out_ref = refs[-1]
    start = 0
    for ref in refs[:-1]:
        out_ref[start : start + ref.shape[0]] = ref[...]
        start += ref.shape[0]


def pack(*pieces):
    shape = (sum(p.shape[0] for p in pieces), pieces[0].shape[1])
    return pl.pallas_call(
        pack_kernel,
        out_shape=jax.ShapeDtypeStruct(shape, pieces[0].dtype),
        in_specs=[VMEM] * len(pieces),
        out_specs=VMEM,
        compiler_params=pltpu.CompilerParams(vmem_limit_bytes=8 * MIB),
        name="pack",
    )(*pieces)


def half_kernel(k, in_ref, out_ref):
    rows = out_ref.shape[0]
    out_ref[...] = in_ref[k * rows : (k + 1) * rows]


def half_of(x, k):
    return pl.pallas_call(
        lambda *refs: half_kernel(k, *refs),
        out_shape=jax.ShapeDtypeStruct((x.shape[0] // 2, x.shape[1]), x.dtype),
        in_specs=[VMEM],
        out_specs=VMEM,
        compiler_params=pltpu.CompilerParams(vmem_limit_bytes=4 * MIB),
        name="half_of",
    )(x)


def tile_body(pair, first, on_first, sharp_ref, bias_ref, img_ref, txt_ref, copy_ref, before_ref, weights_ref, part_ref, loss_ref):
    rows = img_ref.shape[0]
    cols = txt_ref.shape[0]
    sharp = jnp.exp(jnp.full((1, cols), jnp.max(sharp_ref[...]), jnp.float32))
    bias = jnp.max(bias_ref[...])

    def products(c):
        return lax.dot_general(
            img_ref[c * BLOCK : (c + 1) * BLOCK],
            txt_ref[...],
            (((1,), (1,)), ((), ())),
            preferred_element_type=jnp.float32,
        )

    loss = jnp.zeros((8, cols), jnp.float32)
    following = products(0)
    for c in range(rows // BLOCK):
        current = following
        if (c + 1) * BLOCK < rows:
            following = products(c + 1)
        logits = current * sharp + bias
        grown = jnp.exp(logits)
        one_more = 1.0 + grown
        weights = sharp * (grown / one_more)
        span = slice(c * BLOCK, (c + 1) * BLOCK)
        weights_ref[span] = weights.astype(jnp.bfloat16)
        logs = jnp.log(one_more[: BLOCK // 2] * one_more[BLOCK // 2 :])
        loss = loss + jnp.sum(logs.reshape(BLOCK // 16, 8, cols), axis=0)
        if first:
            copy_ref[span] = img_ref[span]
        if c == 0 and first and on_first:
            row_ids = lax.broadcasted_iota(jnp.int32, (pair, pair), 0)
            col_ids = lax.broadcasted_iota(jnp.int32, (pair, pair), 1)
            wanted = jnp.where(row_ids < pair // 2, row_ids + pair // 2, row_ids - pair // 2)
            same = wanted == col_ids
            corner = weights[:pair, :pair] - jnp.where(same, sharp[:, :pair], 0.0)
            weights_ref[:pair, :pair] = corner.astype(jnp.bfloat16)
            matched = jnp.where(same, logits[:pair, :pair], 0.0)
            matched = jnp.sum(matched.reshape(pair // 8, 8, pair), axis=0)
        part = jnp.dot(weights_ref[span], txt_ref[...], preferred_element_type=jnp.float32)
        if not first:
            part = part + before_ref[span]
        part_ref[span] = part
    loss_ref[...] = loss
    if first and on_first:
        loss_ref[:, :pair] = loss[:, :pair] - matched


def first_tile_kernel(pair, core_ref, sharp_ref, bias_ref, near_ref, received_ref, far_ref, img_ref, weights_ref, part_ref, loss_ref):
    def work(is_first):
        img, txt = (received_ref, near_ref) if is_first else (far_ref, received_ref)
        tile_body(
            pair, True, is_first, sharp_ref, bias_ref, img, txt, img_ref, None, weights_ref, part_ref, loss_ref
        )

    by_core(core_ref, work)


def second_tile_kernel(core_ref, sharp_ref, bias_ref, far_ref, received_ref, img_ref, before_ref, weights_ref, part_ref, loss_ref):
    def work(is_first):
        txt = far_ref if is_first else received_ref
        tile_body(
            0, False, is_first, sharp_ref, bias_ref, img_ref, txt, None, before_ref, weights_ref, part_ref, loss_ref
        )

    by_core(core_ref, work)


def tile_call(kernel, name, scalars, arrays, outs):
    rows, features = arrays[0].shape
    return pl.pallas_call(
        kernel,
        out_shape=outs,
        in_specs=[SMEM] + [VMEM] * (len(scalars) - 1 + len(arrays)),
        out_specs=(VMEM,) * len(outs),
        compiler_params=pltpu.CompilerParams(vmem_limit_bytes=24 * MIB),
        cost_estimate=pl.CostEstimate(
            flops=4 * rows * rows * features,
            bytes_accessed=4 * rows * features + 2 * rows * rows,
            transcendentals=3 * rows * rows,
        ),
        name=name,
    )(*scalars, *arrays)


def small_call(kernel, name, core, arrays, outs):
    size = sum(x.size * x.dtype.itemsize for x in (*arrays, *outs))
    return pl.pallas_call(
        kernel,
        out_shape=outs,
        in_specs=[SMEM] + [VMEM] * len(arrays),
        out_specs=(VMEM,) * len(outs),
        compiler_params=pltpu.CompilerParams(vmem_limit_bytes=size + 4 * MIB),
        name=name,
    )(core, *arrays)


def opposite_kernel(core_ref, txt_ref, img_ref, received_ref, a_ref, b_ref):
    half = a_ref.shape[0]

    def work(is_first):
        for k, ref in enumerate((a_ref, b_ref)):
            rows = slice(k * half, (k + 1) * half)
            if is_first:
                value = txt_ref[rows] + decode(received_ref[rows], ONE_CHIP)
            else:
                value = img_ref[6 * half + k * half : 7 * half + k * half]
            ref[...] = encode(value, ONE_CHIP)

    by_core(core_ref, work)


def second_kernel(core_ref, txt_ref, img_ref, received_ref, out_ref):
    rows = slice(0, out_ref.shape[0])

    def work(is_first):
        value = txt_ref[rows] + decode(received_ref[rows], ONE_CHIP) if is_first else img_ref[rows]
        out_ref[...] = encode(value, TWO_CHIPS)

    by_core(core_ref, work)


def far_kernel(core_ref, txt_ref, img_ref, received_ref, from_a_ref, from_b_ref, x_ref, b_ref):
    half = x_ref.shape[0] // 2

    def work(is_first):
        def base(i):
            rows = slice(i * half, (i + 1) * half)
            if is_first:
                return txt_ref[rows] + decode(received_ref[rows], ONE_CHIP)
            return img_ref[rows]

        x_ref[:half] = encode(base(2), TWO_CHIPS)
        x_ref[half:] = encode(base(3) + decode(from_b_ref[...], ONE_CHIP), TWO_CHIPS)
        b_ref[:half] = encode(base(4) + decode(from_a_ref[...], ONE_CHIP), TWO_CHIPS)
        b_ref[half:] = encode(base(5), TWO_CHIPS)

    by_core(core_ref, work)


def base_kernel(core_ref, txt_ref, received_ref, own_ref, rest_ref, out_ref):
    pair = own_ref.shape[0]

    def work(is_first):
        for k in range(4):
            rows = slice(k * pair, (k + 1) * pair)
            if is_first:
                out_ref[rows] = txt_ref[rows] + decode(received_ref[rows], ONE_CHIP)
            elif k == 0:
                out_ref[rows] = decode(own_ref[...], ONE_CHIP)
            else:
                out_ref[rows] = decode(rest_ref[(k - 1) * pair : k * pair], ONE_CHIP)

    by_core(core_ref, work)


def near_kernel(k, core_ref, base_ref, received_ref, out_ref):
    pair = out_ref.shape[0]
    value = base_ref[k * pair : (k + 1) * pair] + decode(received_ref[...], TWO_CHIPS)
    out_ref[...] = encode(value, FOUR_CHIPS)


def gather_sums_kernel(core_ref, base_ref, a_ref, b_ref, x_ref, keep_ref, give_ref):
    own = keep_ref.shape[0]
    for start, ref in ((0, keep_ref), (own, give_ref)):
        rows = slice(start, start + own)
        total = base_ref[rows] + decode(x_ref[rows], FOUR_CHIPS)
        ref[...] = total + decode(a_ref[rows], FOUR_CHIPS) + decode(b_ref[rows], FOUR_CHIPS)


def finish_kernel(core_ref, img_ref, txt_ref, kept_ref, received_ref, grad_img_ref, grad_txt_ref):
    def side(raw_ref, sum_ref, grad_ref):
        raw = raw_ref[...]
        scale = row_scale(raw)
        unit = raw * scale
        summed = sum_ref[...]
        grad_ref[...] = (summed - unit * jnp.sum(unit * summed, axis=1, keepdims=True)) * scale

    @pl.when(core_ref[0] == 0)
    def _():
        side(img_ref, received_ref, grad_img_ref)
        side(txt_ref, kept_ref, grad_txt_ref)

    @pl.when(core_ref[0] != 0)
    def _():
        side(img_ref, kept_ref, grad_img_ref)
        side(txt_ref, received_ref, grad_txt_ref)


def finish(core, img, txt, kept, received):
    grad = jax.ShapeDtypeStruct(img.shape, jnp.float32)
    return pl.pallas_call(
        finish_kernel,
        out_shape=(grad, grad),
        in_specs=[SMEM] + [VMEM] * 4,
        out_specs=(VMEM, VMEM),
        compiler_params=pltpu.CompilerParams(vmem_limit_bytes=8 * MIB),
        name="finish",
    )(core, img, txt, kept, received)


def transposed_product(weights, img):
    return lax.dot_general(
        weights, img, (((0,), (0,)), ((), ())), preferred_element_type=jnp.float32
    )


def body(image_embed, text_embed, exponent_of_sharpness, bias):
    own, features = image_embed.shape
    pair = 2 * own
    count = 4 * pair
    batch = own * ROWS * COLS
    core = (lax.axis_index("row") & 1).reshape(1)
    on_first = core[0] == 0

    def array(rows, dtype, columns=features):
        return jax.ShapeDtypeStruct((rows, columns), dtype)

    low_half, low_piece = array(own, jnp.bfloat16), array(pair, jnp.bfloat16)

    keep, give = normalize(core, image_embed, text_embed)
    low = pack(keep, swap(give))
    slot_x, slot_1, slot_3 = move(low, "x"), move(low, "a"), move(low, "b")
    slot_2, slot_x3, slot_x1 = move(slot_3, "a"), move(slot_x, "b"), move(slot_1, "x")
    near = pack(low, slot_x, slot_1, slot_3)
    near_received = swap(near)
    sharpness = jnp.broadcast_to(exponent_of_sharpness.reshape(1, 1), (8, 128))
    shift = jnp.broadcast_to(bias.reshape(1, 1), (8, 128))
    slot_x3, sharpness, shift = lax.optimization_barrier((slot_x3, sharpness, shift))
    x2_a = move(half_of(slot_x3, 0), "a")
    x2_b = move(half_of(slot_x1, 1), "b")
    far = pack(slot_2, slot_x1, slot_x3, x2_a, x2_b)
    far_received = swap(far)

    scalars = (core, sharpness, shift)
    part, losses = array(count, jnp.float32), array(8, jnp.float32, count)
    img, near_weights, img_part, near_loss = tile_call(
        lambda *refs: first_tile_kernel(pair, *refs),
        "tile_first",
        scalars,
        (near, near_received, far),
        (array(count, jnp.bfloat16), array(count, jnp.bfloat16, count), part, losses),
    )
    far_weights, img_part, far_loss = tile_call(
        second_tile_kernel,
        "tile_second",
        scalars,
        (far, far_received, img, img_part),
        (array(count, jnp.bfloat16, count), part, losses),
    )
    loss = jnp.sum((near_loss + far_loss).reshape(8, -1, 128), axis=1)

    loss = loss + swap(loss)
    opposite_part = transposed_product(far_weights[:, 3 * pair :], img)
    sent = encode(jnp.where(on_first, img_part[:pair], opposite_part), ONE_CHIP)
    sent, far_weights = lax.optimization_barrier((sent, far_weights))
    own_received = swap(sent)
    far_part = transposed_product(far_weights[:, : 3 * pair], img)
    sent = encode(jnp.where(on_first, img_part[pair:], far_part), ONE_CHIP)
    loss = loss + swap(loss, 0, 1)
    own_received, sent, loss = lax.optimization_barrier((own_received, sent, loss))

    a, b = small_call(
        opposite_kernel, "opposite", core, (opposite_part, img_part, own_received), (low_half, low_half)
    )
    a, b, sent, near_weights = lax.optimization_barrier((a, b, sent, near_weights))
    from_a, from_b = move(a, "a"), move(b, "b")
    rest_received = swap(sent)
    near_part = transposed_product(near_weights, img)
    sent = encode(near_part, ONE_CHIP)
    loss = loss + swap(loss, 8, 1)
    (second,) = small_call(
        second_kernel, "second", core, (far_part, img_part, rest_received), (low_piece,)
    )
    from_a, from_b, second, sent, loss = lax.optimization_barrier((from_a, from_b, second, sent, loss))

    second_received = move(second, "a")
    x, b = small_call(
        far_kernel, "far", core, (far_part, img_part, rest_received, from_a, from_b), (low_piece,) * 2
    )
    x, b, sent = lax.optimization_barrier((x, b, sent))
    from_x, from_b = move(x, "x"), move(b, "b")
    near_received = swap(sent)
    (base,) = small_call(
        base_kernel, "base", core, (near_part, near_received, own_received, rest_received), (part,)
    )
    base, loss = lax.optimization_barrier((base, loss))
    loss = loss + swap(loss, 0, 2)
    second_received, base, loss = lax.optimization_barrier((second_received, base, loss))

    def near_slot(k, received):
        (out,) = small_call(
            lambda *refs: near_kernel(k, *refs), "near", core, (base, received), (low_piece,)
        )
        return out

    from_b, from_x, from_a = (
        move(near_slot(3, second_received), "b"),
        move(near_slot(1, from_b), "x"),
        move(near_slot(2, from_x), "a"),
    )
    loss = loss + swap(loss, 0, 6)
    loss = loss + swap(loss, 2, 0)
    from_x, from_a, from_b, loss = lax.optimization_barrier((from_x, from_a, from_b, loss))
    loss = loss + swap(loss, 6, 0)
    keep, give = small_call(
        gather_sums_kernel, "gather_sums", core, (base, from_a, from_b, from_x), (array(own, jnp.float32),) * 2
    )
    grad_image, grad_text = finish(core, image_embed, text_embed, keep, swap(give))
    return (jnp.sum(loss) / batch, grad_image, grad_text)


def solution(mesh):
    in_specs = (P(("row", "col"), None), P(("row", "col"), None), P(), P())
    out_specs = (P(), P(("row", "col"), None), P(("row", "col"), None))
    return jax.shard_map(body, mesh=mesh, in_specs=in_specs, out_specs=out_specs, check_vma=False)
```

```python
import jax
import jax.numpy as jnp
from jax import lax
from jax.experimental import pallas as pl
from jax.experimental.pallas import tpu as pltpu
from jax.sharding import PartitionSpec as P

VMEM = pl.BlockSpec(memory_space=pltpu.VMEM)
SMEM = pl.BlockSpec(memory_space=pltpu.SMEM)
HBM = pl.BlockSpec(memory_space=pltpu.HBM)
MIB = 1024 * 1024
TINY = 1.1754944e-38
AXES = ("row", "col")
ROWS, COLS = 16, 8
ONE_CHIP, TWO_CHIPS, FOUR_CHIPS = 0.5, 0.25, 0.125
PARTNERS = {"x": ((0, 1), (8, 1)), "a": ((0, 2), (2, 0)), "b": ((0, 6), (6, 0))}


def exchange(x, bits_of_core):
    pairs = []
    for row in range(ROWS):
        for col in range(COLS):
            row_bits, col_bits = bits_of_core[row & 1]
            pairs.append((row * COLS + col, (row ^ row_bits) * COLS + (col ^ col_bits)))
    return lax.ppermute(x, AXES, pairs)


def move(x, step):
    return exchange(x, PARTNERS[step])


def swap(x, row_bits=1, col_bits=0):
    return exchange(x, ((row_bits, col_bits),) * 2)


def encode(x, shift):
    y = x * shift
    y2 = y * y
    y4 = y2 * y2
    return (y4 * y2 * (y * jnp.abs(y))).astype(jnp.bfloat16)


def decode(e, shift):
    f = e.astype(jnp.float32)
    size = jnp.exp2(jnp.log2(jnp.maximum(jnp.abs(f), TINY)) * 0.125)
    return jnp.where(f < 0.0, -size, size) * (1.0 / shift)


def row_scale(raw):
    return lax.rsqrt(jnp.sum(raw * raw, axis=1, keepdims=True) + 1e-06)


def by_core(core_ref, work):
    pl.when(core_ref[0] == 0)(lambda: work(True))
    pl.when(core_ref[0] != 0)(lambda: work(False))


def normalize_kernel(core_ref, img_ref, txt_ref, keep_ref, give_ref, raw_ref, sems):
    copies = [
        pltpu.make_async_copy(source, raw_ref.at[k], sems.at[k])
        for k, source in enumerate((txt_ref, img_ref))
    ]
    for copy in copies:
        copy.start()

    def low(k):
        raw = raw_ref[k]
        return (raw * row_scale(raw)).astype(jnp.bfloat16)

    for k, copy in enumerate(copies):
        copy.wait()

        def work(is_first, k=k):
            ref = keep_ref if (k == 0) == is_first else give_ref
            ref[...] = low(k)

        by_core(core_ref, work)


def normalize(core, img, txt):
    low = jax.ShapeDtypeStruct(img.shape, jnp.bfloat16)
    return pl.pallas_call(
        normalize_kernel,
        out_shape=(low, low),
        in_specs=[SMEM, HBM, HBM],
        out_specs=(VMEM, VMEM),
        scratch_shapes=[pltpu.VMEM((2, *img.shape), jnp.float32), pltpu.SemaphoreType.DMA((2,))],
        compiler_params=pltpu.CompilerParams(vmem_limit_bytes=6 * MIB),
        name="normalize",
    )(core, img, txt)


def pack_kernel(*refs):
    out_ref = refs[-1]
    start = 0
    for ref in refs[:-1]:
        out_ref[start : start + ref.shape[0]] = ref[...]
        start += ref.shape[0]


def pack(*pieces):
    shape = (sum(p.shape[0] for p in pieces), pieces[0].shape[1])
    return pl.pallas_call(
        pack_kernel,
        out_shape=jax.ShapeDtypeStruct(shape, pieces[0].dtype),
        in_specs=[VMEM] * len(pieces),
        out_specs=VMEM,
        compiler_params=pltpu.CompilerParams(vmem_limit_bytes=8 * MIB),
        name="pack",
    )(*pieces)


def half_kernel(k, in_ref, out_ref):
    rows = out_ref.shape[0]
    out_ref[...] = in_ref[k * rows : (k + 1) * rows]


def half_of(x, k):
    return pl.pallas_call(
        lambda *refs: half_kernel(k, *refs),
        out_shape=jax.ShapeDtypeStruct((x.shape[0] // 2, x.shape[1]), x.dtype),
        in_specs=[VMEM],
        out_specs=VMEM,
        compiler_params=pltpu.CompilerParams(vmem_limit_bytes=4 * MIB),
        name="half_of",
    )(x)


def run_tiles(pair, sharp_ref, bias_ref, jobs):
    sharp_scalar = jnp.max(sharp_ref[...])
    bias = jnp.max(bias_ref[...])
    steps = [(job, k) for job in jobs for k in range(len(job[1]))]

    def products(step):
        job, k = step
        return lax.dot_general(
            job[0][...], job[1][k][0][...], (((1,), (1,)), ((), ())), preferred_element_type=jnp.float32
        )

    loss = jnp.zeros((8, 128), jnp.float32)
    following = products(steps[0])
    for i, (job, k) in enumerate(steps):
        current = following
        if i + 1 < len(steps):
            following = products(steps[i + 1])
        _, blocks, before, out, corner = job
        texts, weights_out = blocks[k]
        rows, cols = current.shape
        sharp = jnp.exp(jnp.full((1, cols), sharp_scalar, jnp.float32))
        logits = current * sharp + bias
        grown = jnp.exp(logits)
        one_more = 1.0 + grown
        weights = sharp * (grown / one_more)
        weights_out[...] = weights.astype(jnp.bfloat16)
        logs = jnp.log(one_more[: rows // 2] * one_more[rows // 2 :])
        logs = jnp.sum(logs.reshape(rows // 16, 8, cols), axis=0)
        if corner:
            row_ids = lax.broadcasted_iota(jnp.int32, (pair, pair), 0)
            col_ids = lax.broadcasted_iota(jnp.int32, (pair, pair), 1)
            wanted = jnp.where(row_ids < pair // 2, row_ids + pair // 2, row_ids - pair // 2)
            same = wanted == col_ids
            own = weights[:pair, :pair] - jnp.where(same, sharp[:, :pair], 0.0)
            weights_out[:pair, :pair] = own.astype(jnp.bfloat16)
            matched = jnp.where(same, logits[:pair, :pair], 0.0)
            matched = jnp.sum(matched.reshape(pair // 8, 8, pair), axis=0)
            for start in range(0, pair, 128):
                loss = loss - matched[:, start : start + 128]
        for start in range(0, cols, 128):
            loss = loss + logs[:, start : start + 128]
        part = jnp.dot(weights_out[...], texts[...], preferred_element_type=jnp.float32)
        if k == 0:
            total = part if before is None else part + before[...]
        else:
            total = total + part
        if k == len(blocks) - 1:
            out[...] = total
    return loss


def row_blocks(ref, size, rows=None):
    return [ref.at[pl.ds(start, size)] for start in range(0, rows or ref.shape[0], size)]


def near_tile_kernel(core_ref, sharp_ref, bias_ref, near_ref, near_received_ref, far_ref, img_ref, weights_ref, part_ref, loss_ref):
    pair = far_ref.shape[0] // 3

    def work(is_first):
        if is_first:
            images, texts = row_blocks(near_received_ref, pair, 3 * pair), near_ref
        else:
            images = [near_ref.at[pl.ds(3 * pair, pair)]] + row_blocks(far_ref, pair)[1:]
            texts = near_received_ref
        jobs = []
        for k, rows in enumerate(images):
            span = pl.ds(k * pair, pair)
            img_ref[span] = rows[...]
            jobs.append((rows, [(texts, weights_ref.at[span])], None, part_ref.at[span], is_first and k == 0))
        loss_ref[...] = run_tiles(pair, sharp_ref, bias_ref, jobs)

    by_core(core_ref, work)


def far_tile_kernel(core_ref, sharp_ref, bias_ref, near_ref, near_received_ref, far_ref, far_received_ref, img_ref, before_ref, far_weights_ref, part_ref, near_tail_ref, far_tail_ref, part_tail_ref, loss_ref):
    pair = far_ref.shape[0] // 3
    half = pair // 2

    def work(is_first):
        if is_first:
            near_texts, far_texts = near_ref, far_ref
            tail = far_received_ref.at[pl.ds(0, half)]
        else:
            near_texts, far_texts = near_received_ref, far_received_ref
            tail = far_ref.at[pl.ds(half, half)]
        jobs = []
        for k, rows in enumerate(row_blocks(img_ref, pair)):
            span = pl.ds(k * pair, pair)
            jobs.append((rows, [(far_texts, far_weights_ref.at[span])], before_ref.at[span], part_ref.at[span], False))
        jobs.append((tail, [(near_texts, near_tail_ref), (far_texts, far_tail_ref)], None, part_tail_ref, False))
        loss_ref[...] = run_tiles(pair, sharp_ref, bias_ref, jobs)

    by_core(core_ref, work)


def last_tile_kernel(
    core_ref, sharp_ref, bias_ref, near_ref, near_received_ref, far_ref, far_received_ref, last_ref, last_received_ref,
    img_ref, before_ref, before_tail_ref, near_half_ref, far_half_ref,
    last_weights_ref, part_ref, img_tail_ref, near_tail_ref, far_tail_ref, last_tail_ref, part_tail_ref, loss_ref,
):
    pair = last_ref.shape[0]
    half = pair // 2
    low, high = pl.ds(0, half), pl.ds(half, half)

    def work(is_first):
        if is_first:
            near_texts, far_texts, last_texts = near_ref, far_ref, last_ref
            second, last = far_received_ref.at[low], last_received_ref.at[low]
        else:
            near_texts, far_texts, last_texts = near_received_ref, far_received_ref, last_received_ref
            second, last = far_ref.at[high], last_ref.at[high]
        img_tail_ref[low] = second[...]
        img_tail_ref[high] = last[...]
        near_tail_ref[low] = near_half_ref[...]
        far_tail_ref[low] = far_half_ref[...]
        jobs = []
        for k, rows in enumerate(row_blocks(img_ref, pair)):
            span = pl.ds(k * pair, pair)
            jobs.append((rows, [(last_texts, last_weights_ref.at[span])], before_ref.at[span], part_ref.at[span], False))
        jobs.append((second, [(last_texts, last_tail_ref.at[low])], before_tail_ref, part_tail_ref.at[low], False))
        blocks = [
            (near_texts, near_tail_ref.at[high]),
            (far_texts, far_tail_ref.at[high]),
            (last_texts, last_tail_ref.at[high]),
        ]
        jobs.append((last, blocks, None, part_tail_ref.at[high], False))
        loss_ref[...] = run_tiles(pair, sharp_ref, bias_ref, jobs)

    by_core(core_ref, work)


def tile_call(kernel, name, pairs, scalars, arrays, outs):
    features = arrays[0].shape[1]
    return pl.pallas_call(
        kernel,
        out_shape=outs,
        in_specs=[SMEM] + [VMEM] * (len(scalars) - 1 + len(arrays)),
        out_specs=(VMEM,) * len(outs),
        compiler_params=pltpu.CompilerParams(vmem_limit_bytes=16 * MIB),
        cost_estimate=pl.CostEstimate(
            flops=4 * pairs * features,
            bytes_accessed=sum(2 * x.size for x in arrays),
            transcendentals=3 * pairs,
        ),
        name=name,
    )(*scalars, *arrays)


def small_call(kernel, name, core, arrays, outs):
    size = sum(x.size * x.dtype.itemsize for x in (*arrays, *outs))
    return pl.pallas_call(
        kernel,
        out_shape=outs,
        in_specs=[SMEM] + [VMEM] * len(arrays),
        out_specs=(VMEM,) * len(outs),
        compiler_params=pltpu.CompilerParams(vmem_limit_bytes=size + 4 * MIB),
        name=name,
    )(core, *arrays)


def opposite_kernel(core_ref, txt_ref, img_ref, received_ref, a_ref, b_ref):
    half = a_ref.shape[0]
    low, high = slice(0, half), slice(half, 2 * half)

    def work(is_first):
        if is_first:
            a_ref[...] = encode(txt_ref[low] + decode(received_ref[low], ONE_CHIP), ONE_CHIP)
            b_ref[...] = encode(txt_ref[high] + decode(received_ref[high], ONE_CHIP), ONE_CHIP)
        else:
            a_ref[...] = received_ref[high]
            b_ref[...] = encode(img_ref[high], ONE_CHIP)

    by_core(core_ref, work)


def second_kernel(core_ref, txt_ref, txt_received_ref, img_ref, img_received_ref, out_ref):
    half = out_ref.shape[0] // 2
    low, high = slice(0, half), slice(half, 2 * half)

    def work(is_first):
        if is_first:
            out_ref[low] = encode(txt_ref[low] + decode(txt_received_ref[low], ONE_CHIP), TWO_CHIPS)
            out_ref[high] = encode(txt_ref[high] + decode(txt_received_ref[high], ONE_CHIP), TWO_CHIPS)
        else:
            out_ref[low] = encode(decode(img_received_ref[low], ONE_CHIP), TWO_CHIPS)
            out_ref[high] = encode(img_ref[low], TWO_CHIPS)

    by_core(core_ref, work)


def far_kernel(core_ref, txt_ref, img_ref, received_ref, from_a_ref, from_b_ref, x_ref, b_ref):
    half = x_ref.shape[0] // 2

    def work(is_first):
        def base(i):
            rows = slice(i * half, (i + 1) * half)
            if is_first:
                return txt_ref[rows] + decode(received_ref[rows], ONE_CHIP)
            return img_ref[rows]

        x_ref[:half] = encode(base(2), TWO_CHIPS)
        x_ref[half:] = encode(base(3) + decode(from_b_ref[...], ONE_CHIP), TWO_CHIPS)
        b_ref[:half] = encode(base(4) + decode(from_a_ref[...], ONE_CHIP), TWO_CHIPS)
        b_ref[half:] = encode(base(5), TWO_CHIPS)

    by_core(core_ref, work)


def base_kernel(core_ref, txt_ref, received_ref, img_ref, img_received_ref, out_ref):
    pair = out_ref.shape[0] // 4

    def work(is_first):
        for k in range(4):
            rows = slice(k * pair, (k + 1) * pair)
            if is_first:
                out_ref[rows] = txt_ref[rows] + decode(received_ref[rows], ONE_CHIP)
            elif k < 3:
                out_ref[rows] = decode(img_received_ref[rows], ONE_CHIP)
            else:
                out_ref[rows] = img_ref[:pair]

    by_core(core_ref, work)


def near_kernel(k, core_ref, base_ref, received_ref, out_ref):
    pair = out_ref.shape[0]
    value = base_ref[k * pair : (k + 1) * pair] + decode(received_ref[...], TWO_CHIPS)
    out_ref[...] = encode(value, FOUR_CHIPS)


def gather_sums_kernel(core_ref, base_ref, a_ref, b_ref, x_ref, keep_ref, give_ref):
    own = keep_ref.shape[0]
    for start, ref in ((0, keep_ref), (own, give_ref)):
        rows = slice(start, start + own)
        total = base_ref[rows] + decode(x_ref[rows], FOUR_CHIPS)
        ref[...] = total + decode(a_ref[rows], FOUR_CHIPS) + decode(b_ref[rows], FOUR_CHIPS)


def finish_kernel(batch, core_ref, img_ref, txt_ref, kept_ref, received_ref, loss_parts_ref, loss_ref, grad_img_ref, grad_txt_ref):
    loss_ref[...] = jnp.full((1, 1), jnp.sum(loss_parts_ref[...]) * (1.0 / batch), jnp.float32)

    def side(raw_ref, sum_ref, grad_ref):
        raw = raw_ref[...]
        scale = row_scale(raw)
        unit = raw * scale
        summed = sum_ref[...]
        grad_ref[...] = (summed - unit * jnp.sum(unit * summed, axis=1, keepdims=True)) * scale

    def work(is_first):
        side(img_ref, received_ref if is_first else kept_ref, grad_img_ref)
        side(txt_ref, kept_ref if is_first else received_ref, grad_txt_ref)

    by_core(core_ref, work)


def transposed_product(weights, img):
    return lax.dot_general(
        weights, img, (((0,), (0,)), ((), ())), preferred_element_type=jnp.float32
    )


def body(image_embed, text_embed, exponent_of_sharpness, bias):
    own, features = image_embed.shape
    pair = 2 * own
    batch = own * ROWS * COLS
    core = lax.axis_index("row") & 1
    core, on_first = lax.optimization_barrier((core.reshape(1), core == 0))

    def array(rows, dtype, columns=features):
        return jax.ShapeDtypeStruct((rows, columns), dtype)

    low_half, low_piece = array(own, jnp.bfloat16), array(pair, jnp.bfloat16)

    keep, give = normalize(core, image_embed, text_embed)
    low = pack(keep, swap(give))
    slot_x, slot_1, slot_3 = move(low, "x"), move(low, "a"), move(low, "b")
    slot_2, slot_x3, slot_x1 = move(slot_3, "a"), move(slot_x, "b"), move(slot_1, "x")
    near = pack(low, slot_x, slot_1, slot_3)
    near_received = swap(near)
    sharpness = jnp.broadcast_to(exponent_of_sharpness.reshape(1, 1), (8, 128))
    shift = jnp.broadcast_to(bias.reshape(1, 1), (8, 128))
    slot_x3, sharpness, shift = lax.optimization_barrier((slot_x3, sharpness, shift))
    last_a = move(half_of(slot_x3, 0), "a")
    last_b = move(half_of(slot_x1, 1), "b")
    far = pack(slot_2, slot_x1, slot_x3)
    far_received = swap(far)

    scalars = (core, sharpness, shift)
    losses = array(8, jnp.float32, 128)
    wide, three = 4 * pair, 3 * pair
    img, near_weights, part, near_loss = tile_call(
        near_tile_kernel,
        "tile_near",
        three * wide,
        scalars,
        (near, near_received, far),
        (array(three, jnp.bfloat16), array(three, jnp.bfloat16, wide), array(three, jnp.float32), losses),
    )
    last_a, last_b, part = lax.optimization_barrier((last_a, last_b, part))
    last = pack(last_a, last_b)
    last_received = swap(last)
    far_weights, part, near_half, far_half, part_half, far_loss = tile_call(
        far_tile_kernel,
        "tile_far",
        three * three + own * (wide + three),
        scalars,
        (near, near_received, far, far_received, img, part),
        (
            array(three, jnp.bfloat16, three),
            array(three, jnp.float32),
            array(own, jnp.bfloat16, wide),
            array(own, jnp.bfloat16, three),
            array(own, jnp.float32),
            losses,
        ),
    )
    last_weights, img_part, img_tail, near_tail, far_tail, last_tail, img_part_tail, last_loss = tile_call(
        last_tile_kernel,
        "tile_last",
        (three + own) * pair + own * 2 * wide,
        scalars,
        (near, near_received, far, far_received, last, last_received, img, part, part_half, near_half, far_half),
        (
            array(three, jnp.bfloat16, pair),
            array(three, jnp.float32),
            array(pair, jnp.bfloat16),
            array(pair, jnp.bfloat16, wide),
            array(pair, jnp.bfloat16, three),
            array(pair, jnp.bfloat16, pair),
            array(pair, jnp.float32),
            losses,
        ),
    )
    loss = near_loss + far_loss + last_loss

    def text_sums(weights, tail):
        return transposed_product(weights, img) + transposed_product(tail, img_tail)

    loss = loss + swap(loss)
    opposite_part = text_sums(last_weights, last_tail)
    sent = encode(jnp.where(on_first, img_part_tail, opposite_part), ONE_CHIP)
    sent, far_weights, far_tail = lax.optimization_barrier((sent, far_weights, far_tail))
    tail_received = swap(sent)
    far_part = text_sums(far_weights, far_tail)
    sent = encode(jnp.where(on_first, img_part, far_part), ONE_CHIP)
    loss = loss + swap(loss, 0, 1)
    tail_received, sent, loss = lax.optimization_barrier((tail_received, sent, loss))

    a, b = small_call(
        opposite_kernel, "opposite", core, (opposite_part, img_part_tail, tail_received), (low_half, low_half)
    )
    a, b, sent, near_weights, near_tail = lax.optimization_barrier((a, b, sent, near_weights, near_tail))
    from_a, from_b = move(a, "a"), move(b, "b")
    rest_received = swap(sent)
    near_part = text_sums(near_weights, near_tail)
    sent = encode(near_part, ONE_CHIP)
    loss = loss + swap(loss, 8, 1)
    (second,) = small_call(
        second_kernel, "second", core, (far_part, rest_received, img_part_tail, tail_received), (low_piece,)
    )
    from_a, from_b, second, sent, loss = lax.optimization_barrier((from_a, from_b, second, sent, loss))

    second_received = move(second, "a")
    x, b = small_call(
        far_kernel, "far", core, (far_part, img_part, rest_received, from_a, from_b), (low_piece,) * 2
    )
    x, b, sent = lax.optimization_barrier((x, b, sent))
    from_x, from_b = move(x, "x"), move(b, "b")
    near_received = swap(sent)
    (base,) = small_call(
        base_kernel, "base", core, (near_part, near_received, img_part, rest_received), (array(wide, jnp.float32),)
    )
    base, loss = lax.optimization_barrier((base, loss))
    loss = loss + swap(loss, 0, 2)
    second_received, base, loss = lax.optimization_barrier((second_received, base, loss))

    def near_slot(k, received):
        (out,) = small_call(
            lambda *refs: near_kernel(k, *refs), "near", core, (base, received), (low_piece,)
        )
        return out

    from_b, from_x, from_a = (
        move(near_slot(3, second_received), "b"),
        move(near_slot(1, from_b), "x"),
        move(near_slot(2, from_x), "a"),
    )
    loss = loss + swap(loss, 0, 6)
    loss = loss + swap(loss, 2, 0)
    from_x, from_a, from_b, loss = lax.optimization_barrier((from_x, from_a, from_b, loss))
    loss = loss + swap(loss, 6, 0)
    keep, give = small_call(
        gather_sums_kernel, "gather_sums", core, (base, from_a, from_b, from_x), (array(own, jnp.float32),) * 2
    )
    grad = array(own, jnp.float32)
    loss_value, grad_image, grad_text = small_call(
        lambda *refs: finish_kernel(batch, *refs),
        "finish",
        core,
        (image_embed, text_embed, keep, swap(give), loss),
        (array(1, jnp.float32, 1), grad, grad),
    )
    return (loss_value.reshape(()), grad_image, grad_text)


def solution(mesh):
    in_specs = (P(("row", "col"), None), P(("row", "col"), None), P(), P())
    out_specs = (P(), P(("row", "col"), None), P(("row", "col"), None))
    return jax.shard_map(body, mesh=mesh, in_specs=in_specs, out_specs=out_specs, check_vma=False)
```

```python
import jax
import jax.numpy as jnp
from jax import lax
from jax.experimental import pallas as pl
from jax.experimental.pallas import tpu as pltpu
from jax.sharding import PartitionSpec as P

VMEM = pl.BlockSpec(memory_space=pltpu.VMEM)
SMEM = pl.BlockSpec(memory_space=pltpu.SMEM)
HBM = pl.BlockSpec(memory_space=pltpu.HBM)
MIB = 1024 * 1024
TINY = 1.1754944e-38
AXES = ("row", "col")
ROWS, COLS = 16, 8
ONE_CHIP, TWO_CHIPS, FOUR_CHIPS = 0.5, 0.25, 0.125
PARTNERS = {"x": ((0, 1), (8, 1)), "a": ((0, 2), (2, 0)), "b": ((0, 6), (6, 0))}


def exchange(x, bits_of_core):
    pairs = []
    for row in range(ROWS):
        for col in range(COLS):
            row_bits, col_bits = bits_of_core[row & 1]
            pairs.append((row * COLS + col, (row ^ row_bits) * COLS + (col ^ col_bits)))
    return lax.ppermute(x, AXES, pairs)


def move(x, step):
    return exchange(x, PARTNERS[step])


def swap(x, row_bits=1, col_bits=0):
    return exchange(x, ((row_bits, col_bits),) * 2)


def encode(x, shift):
    y = x * shift
    y2 = y * y
    y4 = y2 * y2
    return (y4 * y2 * (y * jnp.abs(y))).astype(jnp.bfloat16)


def decode(e, shift):
    f = e.astype(jnp.float32)
    size = jnp.exp2(jnp.log2(jnp.maximum(jnp.abs(f), TINY)) * 0.125)
    return jnp.where(f < 0.0, -size, size) * (1.0 / shift)


def row_scale(raw):
    return lax.rsqrt(jnp.sum(raw * raw, axis=1, keepdims=True) + 1e-06)


def by_core(core_ref, work):
    pl.when(core_ref[0] == 0)(lambda: work(True))
    pl.when(core_ref[0] != 0)(lambda: work(False))


def normalize_kernel(core_ref, img_ref, txt_ref, keep_ref, give_ref, raw_ref, sems):
    copies = [
        pltpu.make_async_copy(source, raw_ref.at[k], sems.at[k])
        for k, source in enumerate((txt_ref, img_ref))
    ]
    for copy in copies:
        copy.start()

    def low(k):
        raw = raw_ref[k]
        return (raw * row_scale(raw)).astype(jnp.bfloat16)

    for k, copy in enumerate(copies):
        copy.wait()

        def work(is_first, k=k):
            ref = keep_ref if (k == 0) == is_first else give_ref
            ref[...] = low(k)

        by_core(core_ref, work)


def normalize(core, img, txt):
    low = jax.ShapeDtypeStruct(img.shape, jnp.bfloat16)
    return pl.pallas_call(
        normalize_kernel,
        out_shape=(low, low),
        in_specs=[SMEM, HBM, HBM],
        out_specs=(VMEM, VMEM),
        scratch_shapes=[pltpu.VMEM((2, *img.shape), jnp.float32), pltpu.SemaphoreType.DMA((2,))],
        compiler_params=pltpu.CompilerParams(vmem_limit_bytes=6 * MIB),
        name="normalize",
    )(core, img, txt)


def pack_kernel(*refs):
    out_ref = refs[-1]
    start = 0
    for ref in refs[:-1]:
        out_ref[start : start + ref.shape[0]] = ref[...]
        start += ref.shape[0]


def pack(*pieces):
    shape = (sum(p.shape[0] for p in pieces), pieces[0].shape[1])
    return pl.pallas_call(
        pack_kernel,
        out_shape=jax.ShapeDtypeStruct(shape, pieces[0].dtype),
        in_specs=[VMEM] * len(pieces),
        out_specs=VMEM,
        compiler_params=pltpu.CompilerParams(vmem_limit_bytes=8 * MIB),
        name="pack",
    )(*pieces)


def half_kernel(k, in_ref, out_ref):
    rows = out_ref.shape[0]
    out_ref[...] = in_ref[k * rows : (k + 1) * rows]


def half_of(x, k):
    return pl.pallas_call(
        lambda *refs: half_kernel(k, *refs),
        out_shape=jax.ShapeDtypeStruct((x.shape[0] // 2, x.shape[1]), x.dtype),
        in_specs=[VMEM],
        out_specs=VMEM,
        compiler_params=pltpu.CompilerParams(vmem_limit_bytes=4 * MIB),
        name="half_of",
    )(x)


def run_tiles(pair, sharp_ref, bias_ref, jobs):
    sharp_scalar = jnp.max(sharp_ref[...])
    bias = jnp.max(bias_ref[...])
    steps = [(job, k) for job in jobs for k in range(len(job[1]))]

    def products(step):
        job, k = step
        return lax.dot_general(
            job[0][...], job[1][k][0][...], (((1,), (1,)), ((), ())), preferred_element_type=jnp.float32
        )

    loss = jnp.zeros((8, 128), jnp.float32)
    following = products(steps[0])
    for i, (job, k) in enumerate(steps):
        current = following
        if i + 1 < len(steps):
            following = products(steps[i + 1])
        _, blocks, before, out, corner = job
        texts, weights_out = blocks[k]
        rows, cols = current.shape
        sharp = jnp.exp(jnp.full((1, cols), sharp_scalar, jnp.float32))
        logits = current * sharp + bias
        grown = jnp.exp(logits)
        one_more = 1.0 + grown
        weights = sharp * (grown / one_more)
        weights_out[...] = weights.astype(jnp.bfloat16)
        logs = jnp.log(one_more[: rows // 2] * one_more[rows // 2 :])
        logs = jnp.sum(logs.reshape(rows // 16, 8, cols), axis=0)
        if corner is not None:
            row_ids = lax.broadcasted_iota(jnp.int32, (pair, pair), 0)
            col_ids = lax.broadcasted_iota(jnp.int32, (pair, pair), 1)
            wanted = jnp.where(row_ids < pair // 2, row_ids + pair // 2, row_ids - pair // 2)
            same = (wanted == col_ids) & (corner == 0)
            own = weights[:pair, :pair] - jnp.where(same, sharp[:, :pair], 0.0)
            weights_out[:pair, :pair] = own.astype(jnp.bfloat16)
            matched = jnp.where(same, logits[:pair, :pair], 0.0)
            matched = jnp.sum(matched.reshape(pair // 8, 8, pair), axis=0)
            for start in range(0, pair, 128):
                loss = loss - matched[:, start : start + 128]
        for start in range(0, cols, 128):
            loss = loss + logs[:, start : start + 128]
        part = jnp.dot(weights_out[...], texts[...], preferred_element_type=jnp.float32)
        if k == 0:
            total = part if before is None else part + before[...]
        else:
            total = total + part
        if k == len(blocks) - 1:
            out[...] = total
    return loss


def row_blocks(ref, size, rows=None):
    return [ref.at[pl.ds(start, size)] for start in range(0, rows or ref.shape[0], size)]


def near_tile_kernel(core_ref, sharp_ref, bias_ref, near_ref, received_ref, far_ref, img_ref, txt_ref, weights_ref, part_ref, loss_ref):
    pair = far_ref.shape[0] // 3

    def work(is_first):
        if is_first:
            txt_ref[...] = near_ref[...]
            img_ref[...] = received_ref[: 3 * pair]
        else:
            txt_ref[...] = received_ref[...]
            img_ref[:pair] = near_ref[3 * pair :]
            img_ref[pair:] = far_ref[pair:]

    by_core(core_ref, work)
    jobs = []
    for k, rows in enumerate(row_blocks(img_ref, pair)):
        span = pl.ds(k * pair, pair)
        corner = core_ref[0] if k == 0 else None
        jobs.append((rows, [(txt_ref, weights_ref.at[span])], None, part_ref.at[span], corner))
    loss_ref[...] = run_tiles(pair, sharp_ref, bias_ref, jobs)


def far_tile_kernel(
    core_ref, sharp_ref, bias_ref, far_ref, received_ref, near_txt_ref, img_ref, before_ref,
    txt_ref, second_ref, weights_ref, part_ref, near_half_ref, far_half_ref, part_half_ref, loss_ref,
):
    pair = far_ref.shape[0] // 3
    half = pair // 2

    def work(is_first):
        txt_ref[...] = far_ref[...] if is_first else received_ref[...]
        second_ref[...] = received_ref[:half] if is_first else far_ref[half:pair]

    by_core(core_ref, work)
    jobs = []
    for k, rows in enumerate(row_blocks(img_ref, pair)):
        span = pl.ds(k * pair, pair)
        jobs.append((rows, [(txt_ref, weights_ref.at[span])], before_ref.at[span], part_ref.at[span], None))
    blocks = [(near_txt_ref, near_half_ref), (txt_ref, far_half_ref)]
    jobs.append((second_ref, blocks, None, part_half_ref, None))
    loss_ref[...] = run_tiles(pair, sharp_ref, bias_ref, jobs)


def last_tile_kernel(
    core_ref, sharp_ref, bias_ref, last_ref, received_ref, near_txt_ref, far_txt_ref,
    img_ref, second_ref, before_ref, before_half_ref, near_half_ref, far_half_ref,
    weights_ref, part_ref, img_tail_ref, near_tail_ref, far_tail_ref, last_tail_ref, part_tail_ref, loss_ref, txt_ref,
):
    pair = last_ref.shape[0]
    half = pair // 2
    low, high = pl.ds(0, half), pl.ds(half, half)

    def work(is_first):
        txt_ref[...] = last_ref[...] if is_first else received_ref[...]
        img_tail_ref[high] = received_ref[low] if is_first else last_ref[high]

    by_core(core_ref, work)
    img_tail_ref[low] = second_ref[...]
    near_tail_ref[low] = near_half_ref[...]
    far_tail_ref[low] = far_half_ref[...]
    jobs = []
    for k, rows in enumerate(row_blocks(img_ref, pair)):
        span = pl.ds(k * pair, pair)
        jobs.append((rows, [(txt_ref, weights_ref.at[span])], before_ref.at[span], part_ref.at[span], None))
    jobs.append((second_ref, [(txt_ref, last_tail_ref.at[low])], before_half_ref, part_tail_ref.at[low], None))
    blocks = [
        (near_txt_ref, near_tail_ref.at[high]),
        (far_txt_ref, far_tail_ref.at[high]),
        (txt_ref, last_tail_ref.at[high]),
    ]
    jobs.append((img_tail_ref.at[high], blocks, None, part_tail_ref.at[high], None))
    loss_ref[...] = run_tiles(pair, sharp_ref, bias_ref, jobs)


def tile_call(kernel, name, pairs, scalars, arrays, outs, scratch=()):
    features = arrays[0].shape[1]
    return pl.pallas_call(
        kernel,
        out_shape=outs,
        in_specs=[SMEM] + [VMEM] * (len(scalars) - 1 + len(arrays)),
        out_specs=(VMEM,) * len(outs),
        scratch_shapes=[pltpu.VMEM(x.shape, x.dtype) for x in scratch],
        compiler_params=pltpu.CompilerParams(vmem_limit_bytes=16 * MIB),
        cost_estimate=pl.CostEstimate(
            flops=4 * pairs * features,
            bytes_accessed=sum(2 * x.size for x in arrays),
            transcendentals=3 * pairs,
        ),
        name=name,
    )(*scalars, *arrays)


def small_call(kernel, name, core, arrays, outs):
    size = sum(x.size * x.dtype.itemsize for x in (*arrays, *outs))
    return pl.pallas_call(
        kernel,
        out_shape=outs,
        in_specs=[SMEM] + [VMEM] * len(arrays),
        out_specs=(VMEM,) * len(outs),
        compiler_params=pltpu.CompilerParams(vmem_limit_bytes=size + 4 * MIB),
        name=name,
    )(core, *arrays)


CHUNK = 32


def each_chunk(rows, work):
    def step(i, carry):
        first = pl.multiple_of(i * CHUNK, CHUNK)
        work(lambda start=0: pl.ds(start + first, CHUNK))
        return carry

    lax.fori_loop(0, rows // CHUNK, step, 0)


def opposite_kernel(core_ref, txt_ref, img_ref, received_ref, a_ref, b_ref):
    half = a_ref.shape[0]

    def work(is_first):
        def texts(at):
            a_ref[at()] = encode(txt_ref[at()] + decode(received_ref[at()], ONE_CHIP), ONE_CHIP)
            b_ref[at()] = encode(txt_ref[at(half)] + decode(received_ref[at(half)], ONE_CHIP), ONE_CHIP)

        def images(at):
            a_ref[at()] = received_ref[at(half)]
            b_ref[at()] = encode(img_ref[at(half)], ONE_CHIP)

        each_chunk(half, texts if is_first else images)

    by_core(core_ref, work)


def second_kernel(core_ref, txt_ref, txt_received_ref, img_ref, img_received_ref, out_ref):
    pair = out_ref.shape[0]
    half = pair // 2

    def work(is_first):
        def texts(at):
            out_ref[at()] = encode(txt_ref[at()] + decode(txt_received_ref[at()], ONE_CHIP), TWO_CHIPS)

        def images(at):
            out_ref[at()] = encode(decode(img_received_ref[at()], ONE_CHIP), TWO_CHIPS)
            out_ref[at(half)] = encode(img_ref[at()], TWO_CHIPS)

        if is_first:
            each_chunk(pair, texts)
        else:
            each_chunk(half, images)

    by_core(core_ref, work)


def far_kernel(core_ref, txt_ref, img_ref, received_ref, from_a_ref, from_b_ref, x_ref, b_ref):
    half = x_ref.shape[0] // 2

    def work(is_first):
        def rows(at):
            def base(i):
                if is_first:
                    return txt_ref[at(i * half)] + decode(received_ref[at(i * half)], ONE_CHIP)
                return img_ref[at(i * half)]

            x_ref[at()] = encode(base(2), TWO_CHIPS)
            x_ref[at(half)] = encode(base(3) + decode(from_b_ref[at()], ONE_CHIP), TWO_CHIPS)
            b_ref[at()] = encode(base(4) + decode(from_a_ref[at()], ONE_CHIP), TWO_CHIPS)
            b_ref[at(half)] = encode(base(5), TWO_CHIPS)

        each_chunk(half, rows)

    by_core(core_ref, work)


def base_kernel(core_ref, txt_ref, received_ref, img_ref, img_received_ref, out_ref):
    count = out_ref.shape[0]
    three = 3 * count // 4

    def work(is_first):
        def texts(at):
            out_ref[at()] = txt_ref[at()] + decode(received_ref[at()], ONE_CHIP)

        def images(at):
            out_ref[at()] = decode(img_received_ref[at()], ONE_CHIP)

        if is_first:
            each_chunk(count, texts)
        else:
            each_chunk(three, images)
            out_ref[three:] = img_ref[: count - three]

    by_core(core_ref, work)


def near_kernel(k, core_ref, base_ref, received_ref, out_ref):
    pair = out_ref.shape[0]

    def rows(at):
        value = base_ref[at(k * pair)] + decode(received_ref[at()], TWO_CHIPS)
        out_ref[at()] = encode(value, FOUR_CHIPS)

    each_chunk(pair, rows)


def gather_sums_kernel(core_ref, base_ref, a_ref, b_ref, x_ref, keep_ref, give_ref):
    own = keep_ref.shape[0]

    def rows(at):
        for start, ref in ((0, keep_ref), (own, give_ref)):
            total = base_ref[at(start)] + decode(x_ref[at(start)], FOUR_CHIPS)
            total = total + decode(a_ref[at(start)], FOUR_CHIPS)
            ref[at()] = total + decode(b_ref[at(start)], FOUR_CHIPS)

    each_chunk(own, rows)


def finish_kernel(batch, core_ref, img_ref, txt_ref, kept_ref, received_ref, loss_parts_ref, loss_ref, grad_img_ref, grad_txt_ref):
    loss_ref[...] = jnp.full((1, 1), jnp.sum(loss_parts_ref[...]) * (1.0 / batch), jnp.float32)

    def side(at, raw_ref, sum_ref, grad_ref):
        raw = raw_ref[at()]
        scale = row_scale(raw)
        unit = raw * scale
        summed = sum_ref[at()]
        grad_ref[at()] = (summed - unit * jnp.sum(unit * summed, axis=1, keepdims=True)) * scale

    def work(is_first):
        def rows(at):
            side(at, img_ref, received_ref if is_first else kept_ref, grad_img_ref)
            side(at, txt_ref, kept_ref if is_first else received_ref, grad_txt_ref)

        each_chunk(kept_ref.shape[0], rows)

    by_core(core_ref, work)


def transposed_product(weights, img):
    return lax.dot_general(
        weights, img, (((0,), (0,)), ((), ())), preferred_element_type=jnp.float32
    )


def body(image_embed, text_embed, exponent_of_sharpness, bias):
    own, features = image_embed.shape
    pair = 2 * own
    batch = own * ROWS * COLS
    core = lax.axis_index("row") & 1
    core, on_first = lax.optimization_barrier((core.reshape(1), core == 0))

    def array(rows, dtype, columns=features):
        return jax.ShapeDtypeStruct((rows, columns), dtype)

    low_half, low_piece = array(own, jnp.bfloat16), array(pair, jnp.bfloat16)

    keep, give = normalize(core, image_embed, text_embed)
    low = pack(keep, swap(give))
    slot_x, slot_1, slot_3 = move(low, "x"), move(low, "a"), move(low, "b")
    slot_2, slot_x3, slot_x1 = move(slot_3, "a"), move(slot_x, "b"), move(slot_1, "x")
    near = pack(low, slot_x, slot_1, slot_3)
    near_received = swap(near)
    sharpness = jnp.broadcast_to(exponent_of_sharpness.reshape(1, 1), (8, 128))
    shift = jnp.broadcast_to(bias.reshape(1, 1), (8, 128))
    slot_x3, sharpness, shift = lax.optimization_barrier((slot_x3, sharpness, shift))
    last_a = move(half_of(slot_x3, 0), "a")
    last_b = move(half_of(slot_x1, 1), "b")
    far = pack(slot_2, slot_x1, slot_x3)
    far_received = swap(far)

    scalars = (core, sharpness, shift)
    losses = array(8, jnp.float32, 128)
    wide, three = 4 * pair, 3 * pair
    img, near_txt, near_weights, part, near_loss = tile_call(
        near_tile_kernel,
        "tile_near",
        three * wide,
        scalars,
        (near, near_received, far),
        (
            array(three, jnp.bfloat16),
            array(wide, jnp.bfloat16),
            array(three, jnp.bfloat16, wide),
            array(three, jnp.float32),
            losses,
        ),
    )
    last_a, last_b, part = lax.optimization_barrier((last_a, last_b, part))
    last = pack(last_a, last_b)
    last_received = swap(last)
    far_txt, second, far_weights, part, near_half, far_half, part_half, far_loss = tile_call(
        far_tile_kernel,
        "tile_far",
        three * three + own * (wide + three),
        scalars,
        (far, far_received, near_txt, img, part),
        (
            array(three, jnp.bfloat16),
            low_half,
            array(three, jnp.bfloat16, three),
            array(three, jnp.float32),
            array(own, jnp.bfloat16, wide),
            array(own, jnp.bfloat16, three),
            array(own, jnp.float32),
            losses,
        ),
    )
    last_weights, img_part, img_tail, near_tail, far_tail, last_tail, img_part_tail, last_loss = tile_call(
        last_tile_kernel,
        "tile_last",
        (three + own) * pair + own * 2 * wide,
        scalars,
        (last, last_received, near_txt, far_txt, img, second, part, part_half, near_half, far_half),
        (
            array(three, jnp.bfloat16, pair),
            array(three, jnp.float32),
            low_piece,
            array(pair, jnp.bfloat16, wide),
            array(pair, jnp.bfloat16, three),
            array(pair, jnp.bfloat16, pair),
            array(pair, jnp.float32),
            losses,
        ),
        (low_piece,),
    )
    loss = near_loss + far_loss + last_loss

    def text_sums(weights, tail):
        return transposed_product(weights, img) + transposed_product(tail, img_tail)

    loss = loss + swap(loss)
    opposite_part = text_sums(last_weights, last_tail)
    sent = encode(jnp.where(on_first, img_part_tail, opposite_part), ONE_CHIP)
    sent, far_weights, far_tail = lax.optimization_barrier((sent, far_weights, far_tail))
    tail_received = swap(sent)
    far_part = text_sums(far_weights, far_tail)
    sent = encode(jnp.where(on_first, img_part, far_part), ONE_CHIP)
    loss = loss + swap(loss, 0, 1)
    tail_received, sent, loss = lax.optimization_barrier((tail_received, sent, loss))

    a, b = small_call(
        opposite_kernel, "opposite", core, (opposite_part, img_part_tail, tail_received), (low_half, low_half)
    )
    a, b, sent, near_weights, near_tail = lax.optimization_barrier((a, b, sent, near_weights, near_tail))
    from_a, from_b = move(a, "a"), move(b, "b")
    rest_received = swap(sent)
    near_part = text_sums(near_weights, near_tail)
    sent = encode(near_part, ONE_CHIP)
    loss = loss + swap(loss, 8, 1)
    (second,) = small_call(
        second_kernel, "second", core, (far_part, rest_received, img_part_tail, tail_received), (low_piece,)
    )
    from_a, from_b, second, sent, loss = lax.optimization_barrier((from_a, from_b, second, sent, loss))

    second_received = move(second, "a")
    x, b = small_call(
        far_kernel, "far", core, (far_part, img_part, rest_received, from_a, from_b), (low_piece,) * 2
    )
    x, b, sent = lax.optimization_barrier((x, b, sent))
    from_x, from_b = move(x, "x"), move(b, "b")
    near_received = swap(sent)
    (base,) = small_call(
        base_kernel, "base", core, (near_part, near_received, img_part, rest_received), (array(wide, jnp.float32),)
    )
    base, loss = lax.optimization_barrier((base, loss))
    loss = loss + swap(loss, 0, 2)
    second_received, base, loss = lax.optimization_barrier((second_received, base, loss))

    def near_slot(k, received):
        (out,) = small_call(
            lambda *refs: near_kernel(k, *refs), "near", core, (base, received), (low_piece,)
        )
        return out

    from_b, from_x, from_a = (
        move(near_slot(3, second_received), "b"),
        move(near_slot(1, from_b), "x"),
        move(near_slot(2, from_x), "a"),
    )
    loss = loss + swap(loss, 0, 6)
    loss = loss + swap(loss, 2, 0)
    from_x, from_a, from_b, loss = lax.optimization_barrier((from_x, from_a, from_b, loss))
    loss = loss + swap(loss, 6, 0)
    keep, give = small_call(
        gather_sums_kernel, "gather_sums", core, (base, from_a, from_b, from_x), (array(own, jnp.float32),) * 2
    )
    grad = array(own, jnp.float32)
    loss_value, grad_image, grad_text = small_call(
        lambda *refs: finish_kernel(batch, *refs),
        "finish",
        core,
        (image_embed, text_embed, keep, swap(give), loss),
        (array(1, jnp.float32, 1), grad, grad),
    )
    return (loss_value.reshape(()), grad_image, grad_text)


def solution(mesh):
    in_specs = (P(("row", "col"), None), P(("row", "col"), None), P(), P())
    out_specs = (P(), P(("row", "col"), None), P(("row", "col"), None))
    return jax.shard_map(body, mesh=mesh, in_specs=in_specs, out_specs=out_specs, check_vma=False)
```

```python
import jax
import jax.numpy as jnp
from jax import lax
from jax.experimental import pallas as pl
from jax.experimental.pallas import tpu as pltpu
from jax.sharding import PartitionSpec as P

VMEM = pl.BlockSpec(memory_space=pltpu.VMEM)
SMEM = pl.BlockSpec(memory_space=pltpu.SMEM)
HBM = pl.BlockSpec(memory_space=pltpu.HBM)
MIB = 1024 * 1024
TINY = 1.1754944e-38
AXES = ("row", "col")
ROWS, COLS = 16, 8
ONE_CHIP, TWO_CHIPS, FOUR_CHIPS = 0.5, 0.25, 0.125
PARTNERS = {"x": ((0, 1), (8, 1)), "a": ((0, 2), (2, 0)), "b": ((0, 6), (6, 0))}


def exchange(x, bits_of_core):
    pairs = []
    for row in range(ROWS):
        for col in range(COLS):
            row_bits, col_bits = bits_of_core[row & 1]
            pairs.append((row * COLS + col, (row ^ row_bits) * COLS + (col ^ col_bits)))
    return lax.ppermute(x, AXES, pairs)


def move(x, step):
    return exchange(x, PARTNERS[step])


def swap(x, row_bits=1, col_bits=0):
    return exchange(x, ((row_bits, col_bits),) * 2)


def encode(x, shift):
    y = x * shift
    y2 = y * y
    y4 = y2 * y2
    return (y4 * y2 * (y * jnp.abs(y))).astype(jnp.bfloat16)


def decode(e, shift):
    f = e.astype(jnp.float32)
    size = jnp.exp2(jnp.log2(jnp.maximum(jnp.abs(f), TINY)) * 0.125)
    return jnp.where(f < 0.0, -size, size) * (1.0 / shift)


def row_scale(raw):
    return lax.rsqrt(jnp.sum(raw * raw, axis=1, keepdims=True) + 1e-06)


def by_core(core_ref, work):
    pl.when(core_ref[0] == 0)(lambda: work(True))
    pl.when(core_ref[0] != 0)(lambda: work(False))


def normalize_kernel(core_ref, img_ref, txt_ref, keep_ref, give_ref, raw_ref, sems):
    copies = [
        pltpu.make_async_copy(source, raw_ref.at[k], sems.at[k])
        for k, source in enumerate((txt_ref, img_ref))
    ]
    for copy in copies:
        copy.start()

    def low(k):
        raw = raw_ref[k]
        return (raw * row_scale(raw)).astype(jnp.bfloat16)

    for k, copy in enumerate(copies):
        copy.wait()

        def work(is_first, k=k):
            ref = keep_ref if (k == 0) == is_first else give_ref
            ref[...] = low(k)

        by_core(core_ref, work)


def normalize(core, img, txt):
    low = jax.ShapeDtypeStruct(img.shape, jnp.bfloat16)
    return pl.pallas_call(
        normalize_kernel,
        out_shape=(low, low),
        in_specs=[SMEM, HBM, HBM],
        out_specs=(VMEM, VMEM),
        scratch_shapes=[pltpu.VMEM((2, *img.shape), jnp.float32), pltpu.SemaphoreType.DMA((2,))],
        compiler_params=pltpu.CompilerParams(vmem_limit_bytes=6 * MIB),
        name="normalize",
    )(core, img, txt)


def pack_kernel(*refs):
    out_ref = refs[-1]
    start = 0
    for ref in refs[:-1]:
        out_ref[start : start + ref.shape[0]] = ref[...]
        start += ref.shape[0]


def pack(*pieces):
    shape = (sum(p.shape[0] for p in pieces), pieces[0].shape[1])
    return pl.pallas_call(
        pack_kernel,
        out_shape=jax.ShapeDtypeStruct(shape, pieces[0].dtype),
        in_specs=[VMEM] * len(pieces),
        out_specs=VMEM,
        compiler_params=pltpu.CompilerParams(vmem_limit_bytes=8 * MIB),
        name="pack",
    )(*pieces)


def half_kernel(k, in_ref, out_ref):
    rows = out_ref.shape[0]
    out_ref[...] = in_ref[k * rows : (k + 1) * rows]


def half_of(x, k):
    return pl.pallas_call(
        lambda *refs: half_kernel(k, *refs),
        out_shape=jax.ShapeDtypeStruct((x.shape[0] // 2, x.shape[1]), x.dtype),
        in_specs=[VMEM],
        out_specs=VMEM,
        compiler_params=pltpu.CompilerParams(vmem_limit_bytes=4 * MIB),
        name="half_of",
    )(x)


def run_tiles(pair, sharp_ref, bias_ref, jobs):
    sharp_scalar = jnp.max(sharp_ref[...])
    bias = jnp.max(bias_ref[...])
    steps = [(job, k) for job in jobs for k in range(len(job[1]))]

    def products(step):
        job, k = step
        return lax.dot_general(
            job[0][...], job[1][k][0][...], (((1,), (1,)), ((), ())), preferred_element_type=jnp.float32
        )

    loss = jnp.zeros((8, 128), jnp.float32)
    following = products(steps[0])
    for i, (job, k) in enumerate(steps):
        current = following
        if i + 1 < len(steps):
            following = products(steps[i + 1])
        _, blocks, before, out, corner = job
        texts, weights_out = blocks[k]
        rows, cols = current.shape
        sharp = jnp.exp(jnp.full((1, cols), sharp_scalar, jnp.float32))
        logits = current * sharp + bias
        grown = jnp.exp(logits)
        one_more = 1.0 + grown
        weights = sharp * (grown / one_more)
        weights_out[...] = weights.astype(jnp.bfloat16)
        logs = jnp.log(one_more[: rows // 2] * one_more[rows // 2 :])
        logs = jnp.sum(logs.reshape(rows // 16, 8, cols), axis=0)
        if corner is not None:
            row_ids = lax.broadcasted_iota(jnp.int32, (pair, pair), 0)
            col_ids = lax.broadcasted_iota(jnp.int32, (pair, pair), 1)
            wanted = jnp.where(row_ids < pair // 2, row_ids + pair // 2, row_ids - pair // 2)
            same = (wanted == col_ids) & (corner == 0)
            own = weights[:pair, :pair] - jnp.where(same, sharp[:, :pair], 0.0)
            weights_out[:pair, :pair] = own.astype(jnp.bfloat16)
            matched = jnp.where(same, logits[:pair, :pair], 0.0)
            matched = jnp.sum(matched.reshape(pair // 8, 8, pair), axis=0)
            for start in range(0, pair, 128):
                loss = loss - matched[:, start : start + 128]
        for start in range(0, cols, 128):
            loss = loss + logs[:, start : start + 128]
        part = jnp.dot(weights_out[...], texts[...], preferred_element_type=jnp.float32)
        if k == 0:
            total = part if before is None else part + before[...]
        else:
            total = total + part
        if k == len(blocks) - 1:
            out[...] = total
    return loss


def row_blocks(ref, size, rows=None):
    return [ref.at[pl.ds(start, size)] for start in range(0, rows or ref.shape[0], size)]


def near_tile_kernel(core_ref, sharp_ref, bias_ref, near_ref, received_ref, far_ref, img_ref, txt_ref, weights_ref, part_ref, loss_ref):
    pair = far_ref.shape[0] // 3

    def work(is_first):
        if is_first:
            txt_ref[...] = near_ref[...]
            img_ref[...] = received_ref[: 3 * pair]
        else:
            txt_ref[...] = received_ref[...]
            img_ref[:pair] = near_ref[3 * pair :]
            img_ref[pair:] = far_ref[pair:]

    by_core(core_ref, work)
    jobs = []
    for k, rows in enumerate(row_blocks(img_ref, pair)):
        span = pl.ds(k * pair, pair)
        corner = core_ref[0] if k == 0 else None
        jobs.append((rows, [(txt_ref, weights_ref.at[span])], None, part_ref.at[span], corner))
    loss_ref[...] = run_tiles(pair, sharp_ref, bias_ref, jobs)


def far_tile_kernel(core_ref, sharp_ref, bias_ref, far_ref, received_ref, img_ref, before_ref, txt_ref, weights_ref, part_ref, loss_ref):
    pair = far_ref.shape[0] // 3

    def work(is_first):
        txt_ref[...] = far_ref[...] if is_first else received_ref[...]

    by_core(core_ref, work)
    jobs = []
    for k, rows in enumerate(row_blocks(img_ref, pair)):
        span = pl.ds(k * pair, pair)
        jobs.append((rows, [(txt_ref, weights_ref.at[span])], before_ref.at[span], part_ref.at[span], None))
    loss_ref[...] = run_tiles(pair, sharp_ref, bias_ref, jobs)


def last_tile_kernel(
    core_ref, sharp_ref, bias_ref, last_ref, received_ref, far_ref, far_received_ref, near_txt_ref, far_txt_ref,
    img_ref, before_ref,
    weights_ref, part_ref, img_tail_ref, near_tail_ref, far_tail_ref, last_tail_ref, part_tail_ref, loss_ref, txt_ref,
):
    pair = last_ref.shape[0]
    half = pair // 2

    def work(is_first):
        txt_ref[...] = last_ref[...] if is_first else received_ref[...]
        img_tail_ref[:half] = far_received_ref[:half] if is_first else far_ref[half:pair]
        img_tail_ref[half:] = received_ref[:half] if is_first else last_ref[half:]

    by_core(core_ref, work)
    jobs = []
    for k, rows in enumerate(row_blocks(img_ref, pair)):
        span = pl.ds(k * pair, pair)
        jobs.append((rows, [(txt_ref, weights_ref.at[span])], before_ref.at[span], part_ref.at[span], None))
    blocks = [(near_txt_ref, near_tail_ref), (far_txt_ref, far_tail_ref), (txt_ref, last_tail_ref)]
    jobs.append((img_tail_ref, blocks, None, part_tail_ref, None))
    loss_ref[...] = run_tiles(pair, sharp_ref, bias_ref, jobs)


def tile_call(kernel, name, pairs, scalars, arrays, outs, scratch=()):
    features = arrays[0].shape[1]
    return pl.pallas_call(
        kernel,
        out_shape=outs,
        in_specs=[SMEM] + [VMEM] * (len(scalars) - 1 + len(arrays)),
        out_specs=(VMEM,) * len(outs),
        scratch_shapes=[pltpu.VMEM(x.shape, x.dtype) for x in scratch],
        compiler_params=pltpu.CompilerParams(vmem_limit_bytes=16 * MIB),
        cost_estimate=pl.CostEstimate(
            flops=4 * pairs * features,
            bytes_accessed=sum(2 * x.size for x in arrays),
            transcendentals=3 * pairs,
        ),
        name=name,
    )(*scalars, *arrays)


def small_call(kernel, name, core, arrays, outs):
    size = sum(x.size * x.dtype.itemsize for x in (*arrays, *outs))
    return pl.pallas_call(
        kernel,
        out_shape=outs,
        in_specs=[SMEM] + [VMEM] * len(arrays),
        out_specs=(VMEM,) * len(outs),
        compiler_params=pltpu.CompilerParams(vmem_limit_bytes=size + 4 * MIB),
        name=name,
    )(core, *arrays)


CHUNK = 32


def each_chunk(rows, work):
    def step(i, carry):
        first = pl.multiple_of(i * CHUNK, CHUNK)
        work(lambda start=0: pl.ds(start + first, CHUNK))
        return carry

    lax.fori_loop(0, rows // CHUNK, step, 0)


def opposite_kernel(core_ref, txt_ref, img_ref, received_ref, a_ref, b_ref):
    half = a_ref.shape[0]

    def work(is_first):
        def texts(at):
            a_ref[at()] = encode(txt_ref[at()] + decode(received_ref[at()], ONE_CHIP), ONE_CHIP)
            b_ref[at()] = encode(txt_ref[at(half)] + decode(received_ref[at(half)], ONE_CHIP), ONE_CHIP)

        def images(at):
            a_ref[at()] = received_ref[at(half)]
            b_ref[at()] = encode(img_ref[at(half)], ONE_CHIP)

        each_chunk(half, texts if is_first else images)

    by_core(core_ref, work)


def second_kernel(core_ref, txt_ref, txt_received_ref, img_ref, img_received_ref, out_ref):
    pair = out_ref.shape[0]
    half = pair // 2

    def work(is_first):
        def texts(at):
            out_ref[at()] = encode(txt_ref[at()] + decode(txt_received_ref[at()], ONE_CHIP), TWO_CHIPS)

        def images(at):
            out_ref[at()] = encode(decode(img_received_ref[at()], ONE_CHIP), TWO_CHIPS)
            out_ref[at(half)] = encode(img_ref[at()], TWO_CHIPS)

        if is_first:
            each_chunk(pair, texts)
        else:
            each_chunk(half, images)

    by_core(core_ref, work)


def far_kernel(core_ref, txt_ref, img_ref, received_ref, from_a_ref, from_b_ref, x_ref, b_ref):
    half = x_ref.shape[0] // 2

    def work(is_first):
        def rows(at):
            def base(i):
                if is_first:
                    return txt_ref[at(i * half)] + decode(received_ref[at(i * half)], ONE_CHIP)
                return img_ref[at(i * half)]

            x_ref[at()] = encode(base(2), TWO_CHIPS)
            x_ref[at(half)] = encode(base(3) + decode(from_b_ref[at()], ONE_CHIP), TWO_CHIPS)
            b_ref[at()] = encode(base(4) + decode(from_a_ref[at()], ONE_CHIP), TWO_CHIPS)
            b_ref[at(half)] = encode(base(5), TWO_CHIPS)

        each_chunk(half, rows)

    by_core(core_ref, work)


def base_kernel(core_ref, txt_ref, received_ref, img_ref, img_received_ref, out_ref):
    count = out_ref.shape[0]
    three = 3 * count // 4

    def work(is_first):
        def texts(at):
            out_ref[at()] = txt_ref[at()] + decode(received_ref[at()], ONE_CHIP)

        def images(at):
            out_ref[at()] = decode(img_received_ref[at()], ONE_CHIP)

        if is_first:
            each_chunk(count, texts)
        else:
            each_chunk(three, images)
            out_ref[three:] = img_ref[: count - three]

    by_core(core_ref, work)


def near_kernel(k, core_ref, base_ref, received_ref, out_ref):
    pair = out_ref.shape[0]

    def rows(at):
        value = base_ref[at(k * pair)] + decode(received_ref[at()], TWO_CHIPS)
        out_ref[at()] = encode(value, FOUR_CHIPS)

    each_chunk(pair, rows)


def gather_sums_kernel(core_ref, base_ref, a_ref, b_ref, x_ref, loss_ref, keep_ref, give_ref):
    own = keep_ref.shape[0]
    give_ref[own:] = jnp.zeros((8, give_ref.shape[1]), jnp.float32)
    give_ref[own:, :128] = loss_ref[...]

    def rows(at):
        for start, ref in ((0, keep_ref), (own, give_ref)):
            total = base_ref[at(start)] + decode(x_ref[at(start)], FOUR_CHIPS)
            total = total + decode(a_ref[at(start)], FOUR_CHIPS)
            ref[at()] = total + decode(b_ref[at(start)], FOUR_CHIPS)

    each_chunk(own, rows)


def finish_kernel(batch, core_ref, img_ref, txt_ref, kept_ref, received_ref, loss_parts_ref, loss_ref, grad_img_ref, grad_txt_ref):
    own = kept_ref.shape[0]
    both = loss_parts_ref[...] + received_ref[own:, :128]
    loss_ref[...] = jnp.full((1, 1), jnp.sum(both) * (1.0 / batch), jnp.float32)

    def side(at, raw_ref, sum_ref, grad_ref):
        raw = raw_ref[at()]
        scale = row_scale(raw)
        unit = raw * scale
        summed = sum_ref[at()]
        grad_ref[at()] = (summed - unit * jnp.sum(unit * summed, axis=1, keepdims=True)) * scale

    def work(is_first):
        def rows(at):
            side(at, img_ref, received_ref if is_first else kept_ref, grad_img_ref)
            side(at, txt_ref, kept_ref if is_first else received_ref, grad_txt_ref)

        each_chunk(own, rows)

    by_core(core_ref, work)


def transposed_product(weights, img):
    return lax.dot_general(
        weights, img, (((0,), (0,)), ((), ())), preferred_element_type=jnp.float32
    )


def body(image_embed, text_embed, exponent_of_sharpness, bias):
    own, features = image_embed.shape
    pair = 2 * own
    batch = own * ROWS * COLS
    core = lax.axis_index("row") & 1
    core, on_first = lax.optimization_barrier((core.reshape(1), core == 0))

    def array(rows, dtype, columns=features):
        return jax.ShapeDtypeStruct((rows, columns), dtype)

    low_half, low_piece = array(own, jnp.bfloat16), array(pair, jnp.bfloat16)

    keep, give = normalize(core, image_embed, text_embed)
    low = pack(keep, swap(give))
    slot_x, slot_1, slot_3 = move(low, "x"), move(low, "a"), move(low, "b")
    slot_2, slot_x3, slot_x1 = move(slot_3, "a"), move(slot_x, "b"), move(slot_1, "x")
    near = pack(low, slot_x, slot_1, slot_3)
    near_received = swap(near)
    sharpness = jnp.broadcast_to(exponent_of_sharpness.reshape(1, 1), (8, 128))
    shift = jnp.broadcast_to(bias.reshape(1, 1), (8, 128))
    slot_x3, sharpness, shift = lax.optimization_barrier((slot_x3, sharpness, shift))
    last_a = move(half_of(slot_x3, 0), "a")
    last_b = move(half_of(slot_x1, 1), "b")
    far = pack(slot_2, slot_x1, slot_x3)
    far_received = swap(far)

    scalars = (core, sharpness, shift)
    losses = array(8, jnp.float32, 128)
    wide, three = 4 * pair, 3 * pair
    img, near_txt, near_weights, part, near_loss = tile_call(
        near_tile_kernel,
        "tile_near",
        three * wide,
        scalars,
        (near, near_received, far),
        (
            array(three, jnp.bfloat16),
            array(wide, jnp.bfloat16),
            array(three, jnp.bfloat16, wide),
            array(three, jnp.float32),
            losses,
        ),
    )
    last_a, last_b, part = lax.optimization_barrier((last_a, last_b, part))
    last = pack(last_a, last_b)
    last_received = swap(last)
    far_txt, far_weights, part, far_loss = tile_call(
        far_tile_kernel,
        "tile_far",
        three * three,
        scalars,
        (far, far_received, img, part),
        (array(three, jnp.bfloat16), array(three, jnp.bfloat16, three), array(three, jnp.float32), losses),
    )
    last_weights, img_part, img_tail, near_tail, far_tail, last_tail, img_part_tail, last_loss = tile_call(
        last_tile_kernel,
        "tile_last",
        three * pair + pair * 2 * wide,
        scalars,
        (last, last_received, far, far_received, near_txt, far_txt, img, part),
        (
            array(three, jnp.bfloat16, pair),
            array(three, jnp.float32),
            low_piece,
            array(pair, jnp.bfloat16, wide),
            array(pair, jnp.bfloat16, three),
            array(pair, jnp.bfloat16, pair),
            array(pair, jnp.float32),
            losses,
        ),
        (low_piece,),
    )
    loss = near_loss + far_loss + last_loss

    def text_sums(weights, tail):
        return transposed_product(weights, img) + transposed_product(tail, img_tail)

    loss = loss + swap(loss, 0, 1)
    opposite_part = text_sums(last_weights, last_tail)
    sent = encode(jnp.where(on_first, img_part_tail, opposite_part), ONE_CHIP)
    sent, far_weights, far_tail, loss = lax.optimization_barrier((sent, far_weights, far_tail, loss))
    tail_received = swap(sent)
    far_part = text_sums(far_weights, far_tail)
    sent = encode(jnp.where(on_first, img_part, far_part), ONE_CHIP)
    loss = loss + swap(loss, 8, 1)
    tail_received, sent, loss = lax.optimization_barrier((tail_received, sent, loss))

    a, b = small_call(
        opposite_kernel, "opposite", core, (opposite_part, img_part_tail, tail_received), (low_half, low_half)
    )
    a, b, sent, near_weights, near_tail = lax.optimization_barrier((a, b, sent, near_weights, near_tail))
    from_a, from_b = move(a, "a"), move(b, "b")
    rest_received = swap(sent)
    near_part = text_sums(near_weights, near_tail)
    sent = encode(near_part, ONE_CHIP)
    loss = loss + swap(loss, 0, 2)
    (second,) = small_call(
        second_kernel, "second", core, (far_part, rest_received, img_part_tail, tail_received), (low_piece,)
    )
    from_a, from_b, second, sent, loss = lax.optimization_barrier((from_a, from_b, second, sent, loss))

    second_received = move(second, "a")
    x, b = small_call(
        far_kernel, "far", core, (far_part, img_part, rest_received, from_a, from_b), (low_piece,) * 2
    )
    x, b, sent = lax.optimization_barrier((x, b, sent))
    from_x, from_b = move(x, "x"), move(b, "b")
    near_received = swap(sent)
    (base,) = small_call(
        base_kernel, "base", core, (near_part, near_received, img_part, rest_received), (array(wide, jnp.float32),)
    )
    base, loss = lax.optimization_barrier((base, loss))
    loss = loss + swap(loss, 0, 6)
    second_received, base, loss = lax.optimization_barrier((second_received, base, loss))

    def near_slot(k, received):
        (out,) = small_call(
            lambda *refs: near_kernel(k, *refs), "near", core, (base, received), (low_piece,)
        )
        return out

    from_b, from_x, from_a = (
        move(near_slot(3, second_received), "b"),
        move(near_slot(1, from_b), "x"),
        move(near_slot(2, from_x), "a"),
    )
    loss = loss + swap(loss, 2, 0)
    loss = loss + swap(loss, 6, 0)
    keep, give = small_call(
        gather_sums_kernel,
        "gather_sums",
        core,
        (base, from_a, from_b, from_x, loss),
        (array(own, jnp.float32), array(own + 8, jnp.float32)),
    )
    grad = array(own, jnp.float32)
    loss_value, grad_image, grad_text = small_call(
        lambda *refs: finish_kernel(batch, *refs),
        "finish",
        core,
        (image_embed, text_embed, keep, swap(give), loss),
        (array(1, jnp.float32, 1), grad, grad),
    )
    return (loss_value.reshape(()), grad_image, grad_text)


def solution(mesh):
    in_specs = (P(("row", "col"), None), P(("row", "col"), None), P(), P())
    out_specs = (P(), P(("row", "col"), None), P(("row", "col"), None))
    return jax.shard_map(body, mesh=mesh, in_specs=in_specs, out_specs=out_specs, check_vma=False)
```

```python
import jax
import jax.numpy as jnp
from jax import lax
from jax.experimental import pallas as pl
from jax.experimental.pallas import tpu as pltpu
from jax.sharding import PartitionSpec as P

VMEM = pl.BlockSpec(memory_space=pltpu.VMEM)
SMEM = pl.BlockSpec(memory_space=pltpu.SMEM)
HBM = pl.BlockSpec(memory_space=pltpu.HBM)
MIB = 1024 * 1024
TINY = 1.1754944e-38
AXES = ("row", "col")
ROWS, COLS = 16, 8
ONE_CHIP, TWO_CHIPS, FOUR_CHIPS = 0.5, 0.25, 0.125
PARTNERS = {"x": ((0, 1), (8, 1)), "a": ((0, 2), (2, 0)), "b": ((0, 6), (6, 0))}


def exchange(x, bits_of_core):
    pairs = []
    for row in range(ROWS):
        for col in range(COLS):
            row_bits, col_bits = bits_of_core[row & 1]
            pairs.append((row * COLS + col, (row ^ row_bits) * COLS + (col ^ col_bits)))
    return lax.ppermute(x, AXES, pairs)


def move(x, step):
    return exchange(x, PARTNERS[step])


def swap(x, row_bits=1, col_bits=0):
    return exchange(x, ((row_bits, col_bits),) * 2)


def encode(x, shift):
    y = x * shift
    y2 = y * y
    y4 = y2 * y2
    return (y4 * y2 * (y * jnp.abs(y))).astype(jnp.bfloat16)


def decode(e, shift):
    f = e.astype(jnp.float32)
    size = jnp.exp(jnp.log(jnp.maximum(jnp.abs(f), TINY)) * 0.125)
    return jnp.where(f < 0.0, -size, size) * (1.0 / shift)


def row_scale(raw):
    return lax.rsqrt(jnp.sum(raw * raw, axis=1, keepdims=True) + 1e-06)


def by_core(core_ref, work):
    pl.when(core_ref[0] == 0)(lambda: work(True))
    pl.when(core_ref[0] != 0)(lambda: work(False))


def normalize_kernel(core_ref, img_ref, txt_ref, keep_ref, give_ref, raw_ref, sems):
    copies = [
        pltpu.make_async_copy(source, raw_ref.at[k], sems.at[k])
        for k, source in enumerate((txt_ref, img_ref))
    ]
    for copy in copies:
        copy.start()

    def low(k):
        raw = raw_ref[k]
        return (raw * row_scale(raw)).astype(jnp.bfloat16)

    for k, copy in enumerate(copies):
        copy.wait()

        def work(is_first, k=k):
            ref = keep_ref if (k == 0) == is_first else give_ref
            ref[...] = low(k)

        by_core(core_ref, work)


def normalize(core, img, txt):
    low = jax.ShapeDtypeStruct(img.shape, jnp.bfloat16)
    return pl.pallas_call(
        normalize_kernel,
        out_shape=(low, low),
        in_specs=[SMEM, HBM, HBM],
        out_specs=(VMEM, VMEM),
        scratch_shapes=[pltpu.VMEM((2, *img.shape), jnp.float32), pltpu.SemaphoreType.DMA((2,))],
        compiler_params=pltpu.CompilerParams(vmem_limit_bytes=6 * MIB),
        name="normalize",
    )(core, img, txt)


def pack_kernel(*refs):
    out_ref = refs[-1]
    start = 0
    for ref in refs[:-1]:
        out_ref[start : start + ref.shape[0]] = ref[...]
        start += ref.shape[0]


def pack(*pieces):
    shape = (sum(p.shape[0] for p in pieces), pieces[0].shape[1])
    return pl.pallas_call(
        pack_kernel,
        out_shape=jax.ShapeDtypeStruct(shape, pieces[0].dtype),
        in_specs=[VMEM] * len(pieces),
        out_specs=VMEM,
        compiler_params=pltpu.CompilerParams(vmem_limit_bytes=8 * MIB),
        name="pack",
    )(*pieces)


def half_kernel(k, in_ref, out_ref):
    rows = out_ref.shape[0]
    out_ref[...] = in_ref[k * rows : (k + 1) * rows]


def half_of(x, k):
    return pl.pallas_call(
        lambda *refs: half_kernel(k, *refs),
        out_shape=jax.ShapeDtypeStruct((x.shape[0] // 2, x.shape[1]), x.dtype),
        in_specs=[VMEM],
        out_specs=VMEM,
        compiler_params=pltpu.CompilerParams(vmem_limit_bytes=4 * MIB),
        name="half_of",
    )(x)


def run_tiles(pair, sharp_ref, bias_ref, jobs):
    sharp_scalar = jnp.max(sharp_ref[...])
    bias = jnp.max(bias_ref[...])
    steps = [(job, k) for job in jobs for k in range(len(job[1]))]

    def products(step):
        job, k = step
        return lax.dot_general(
            job[0][...], job[1][k][0][...], (((1,), (1,)), ((), ())), preferred_element_type=jnp.float32
        )

    loss = jnp.zeros((8, 128), jnp.float32)
    following = products(steps[0])
    for i, (job, k) in enumerate(steps):
        current = following
        if i + 1 < len(steps):
            following = products(steps[i + 1])
        _, blocks, before, out, corner = job
        texts, weights_out = blocks[k]
        rows, cols = current.shape
        sharp = jnp.exp(jnp.full((1, cols), sharp_scalar, jnp.float32))
        logits = current * sharp + bias
        grown = jnp.exp(logits)
        one_more = 1.0 + grown
        weights = sharp * (grown / one_more)
        weights_out[...] = weights.astype(jnp.bfloat16)
        logs = jnp.log(one_more[: rows // 2] * one_more[rows // 2 :])
        logs = jnp.sum(logs.reshape(rows // 16, 8, cols), axis=0)
        if corner is not None:
            row_ids = lax.broadcasted_iota(jnp.int32, (pair, pair), 0)
            col_ids = lax.broadcasted_iota(jnp.int32, (pair, pair), 1)
            wanted = jnp.where(row_ids < pair // 2, row_ids + pair // 2, row_ids - pair // 2)
            same = (wanted == col_ids) & (corner == 0)
            own = weights[:pair, :pair] - jnp.where(same, sharp[:, :pair], 0.0)
            weights_out[:pair, :pair] = own.astype(jnp.bfloat16)
            matched = jnp.where(same, logits[:pair, :pair], 0.0)
            matched = jnp.sum(matched.reshape(pair // 8, 8, pair), axis=0)
            for start in range(0, pair, 128):
                loss = loss - matched[:, start : start + 128]
        for start in range(0, cols, 128):
            loss = loss + logs[:, start : start + 128]
        part = jnp.dot(weights_out[...], texts[...], preferred_element_type=jnp.float32)
        if k == 0:
            total = part if before is None else part + before[...]
        else:
            total = total + part
        if k == len(blocks) - 1:
            out[...] = total
    return loss


def row_blocks(ref, size, rows=None):
    return [ref.at[pl.ds(start, size)] for start in range(0, rows or ref.shape[0], size)]


def near_tile_kernel(core_ref, sharp_ref, bias_ref, near_ref, received_ref, img_ref, txt_ref, weights_ref, part_ref, loss_ref):
    count = img_ref.shape[0]
    pair = count // 2

    def work(is_first):
        txt_ref[...] = near_ref[...] if is_first else received_ref[...]
        img_ref[...] = received_ref[:count] if is_first else near_ref[count:]

    by_core(core_ref, work)
    jobs = []
    for k, rows in enumerate(row_blocks(img_ref, pair)):
        span = pl.ds(k * pair, pair)
        corner = core_ref[0] if k == 0 else None
        jobs.append((rows, [(txt_ref, weights_ref.at[span])], None, part_ref.at[span], corner))
    loss_ref[...] = run_tiles(pair, sharp_ref, bias_ref, jobs)


def middle_tile_kernel(core_ref, sharp_ref, bias_ref, far_ref, received_ref, txt_ref, img_ref, weights_ref, part_ref, loss_ref):
    pair = img_ref.shape[0]

    def work(is_first):
        img_ref[...] = received_ref[:pair] if is_first else far_ref[2 * pair :]

    by_core(core_ref, work)
    loss_ref[...] = run_tiles(pair, sharp_ref, bias_ref, [(img_ref, [(txt_ref, weights_ref)], None, part_ref, None)])


def far_tile_kernel(
    core_ref, sharp_ref, bias_ref, far_ref, received_ref, near_img_ref, far_img_ref, near_before_ref, far_before_ref,
    near_weights_ref, middle_weights_ref,
    txt_ref, img_ref, all_weights_ref, weights_ref, part_ref, loss_ref,
):
    pair = far_img_ref.shape[0]

    def work(is_first):
        txt_ref[...] = far_ref[...] if is_first else received_ref[...]

    by_core(core_ref, work)
    img_ref[: 2 * pair] = near_img_ref[...]
    img_ref[2 * pair :] = far_img_ref[...]
    all_weights_ref[: 2 * pair] = near_weights_ref[...]
    all_weights_ref[2 * pair :] = middle_weights_ref[...]
    jobs = []
    images = row_blocks(near_img_ref, pair) + [far_img_ref]
    before = row_blocks(near_before_ref, pair) + [far_before_ref]
    for k in range(3):
        span = pl.ds(k * pair, pair)
        jobs.append((images[k], [(txt_ref, weights_ref.at[span])], before[k], part_ref.at[span], None))
    loss_ref[...] = run_tiles(pair, sharp_ref, bias_ref, jobs)


def last_tile_kernel(
    core_ref, sharp_ref, bias_ref, last_ref, received_ref, far_ref, far_received_ref, near_txt_ref, far_txt_ref,
    img_ref, before_ref,
    weights_ref, part_ref, img_tail_ref, near_tail_ref, far_tail_ref, last_tail_ref, part_tail_ref, loss_ref, txt_ref,
):
    pair = last_ref.shape[0]
    half = pair // 2

    def work(is_first):
        txt_ref[...] = last_ref[...] if is_first else received_ref[...]
        img_tail_ref[:half] = far_received_ref[pair : pair + half] if is_first else far_ref[pair + half : 2 * pair]
        img_tail_ref[half:] = received_ref[:half] if is_first else last_ref[half:]

    by_core(core_ref, work)
    jobs = []
    for k, rows in enumerate(row_blocks(img_ref, pair)):
        span = pl.ds(k * pair, pair)
        jobs.append((rows, [(txt_ref, weights_ref.at[span])], before_ref.at[span], part_ref.at[span], None))
    blocks = [(near_txt_ref, near_tail_ref), (far_txt_ref, far_tail_ref), (txt_ref, last_tail_ref)]
    jobs.append((img_tail_ref, blocks, None, part_tail_ref, None))
    loss_ref[...] = run_tiles(pair, sharp_ref, bias_ref, jobs)


def tile_call(kernel, name, pairs, scalars, arrays, outs, scratch=()):
    features = arrays[0].shape[1]
    return pl.pallas_call(
        kernel,
        out_shape=outs,
        in_specs=[SMEM] + [VMEM] * (len(scalars) - 1 + len(arrays)),
        out_specs=(VMEM,) * len(outs),
        scratch_shapes=[pltpu.VMEM(x.shape, x.dtype) for x in scratch],
        compiler_params=pltpu.CompilerParams(vmem_limit_bytes=16 * MIB),
        cost_estimate=pl.CostEstimate(
            flops=4 * pairs * features,
            bytes_accessed=sum(2 * x.size for x in arrays),
            transcendentals=3 * pairs,
        ),
        name=name,
    )(*scalars, *arrays)


def small_call(kernel, name, core, arrays, outs):
    size = sum(x.size * x.dtype.itemsize for x in (*arrays, *outs))
    return pl.pallas_call(
        kernel,
        out_shape=outs,
        in_specs=[SMEM] + [VMEM] * len(arrays),
        out_specs=(VMEM,) * len(outs),
        compiler_params=pltpu.CompilerParams(vmem_limit_bytes=size + 4 * MIB),
        name=name,
    )(core, *arrays)


CHUNK = 32


def each_chunk(rows, work):
    def step(i, carry):
        first = pl.multiple_of(i * CHUNK, CHUNK)
        work(lambda start=0: pl.ds(start + first, CHUNK))
        return carry

    lax.fori_loop(0, rows // CHUNK, step, 0)


def opposite_kernel(core_ref, txt_ref, img_ref, received_ref, a_ref, b_ref):
    half = a_ref.shape[0]

    def work(is_first):
        def texts(at):
            a_ref[at()] = encode(txt_ref[at()] + decode(received_ref[at()], ONE_CHIP), ONE_CHIP)
            b_ref[at()] = encode(txt_ref[at(half)] + decode(received_ref[at(half)], ONE_CHIP), ONE_CHIP)

        def images(at):
            a_ref[at()] = received_ref[at(half)]
            b_ref[at()] = encode(img_ref[at(half)], ONE_CHIP)

        each_chunk(half, texts if is_first else images)

    by_core(core_ref, work)


def second_kernel(core_ref, txt_ref, received_ref, out_ref):
    pair = out_ref.shape[0]

    def work(is_first):
        def rows(at):
            if is_first:
                value = txt_ref[at()] + decode(received_ref[at()], ONE_CHIP)
            else:
                value = decode(received_ref[at(2 * pair)], ONE_CHIP)
            out_ref[at()] = encode(value, TWO_CHIPS)

        each_chunk(pair, rows)

    by_core(core_ref, work)


def far_kernel(
    core_ref, txt_ref, txt_received_ref, img_ref, img_tail_ref, tail_received_ref, from_a_ref, from_b_ref, x_ref, b_ref
):
    pair = x_ref.shape[0]
    half = pair // 2

    def work(is_first):
        def rows(at):
            def base(i):
                if is_first:
                    return txt_ref[at(i * half)] + decode(txt_received_ref[at(i * half)], ONE_CHIP)
                if i == 2:
                    return decode(tail_received_ref[at()], ONE_CHIP)
                return img_tail_ref[at()] if i == 3 else img_ref[at(i * half)]

            x_ref[at()] = encode(base(2), TWO_CHIPS)
            x_ref[at(half)] = encode(base(3) + decode(from_b_ref[at()], ONE_CHIP), TWO_CHIPS)
            b_ref[at()] = encode(base(4) + decode(from_a_ref[at()], ONE_CHIP), TWO_CHIPS)
            b_ref[at(half)] = encode(base(5), TWO_CHIPS)

        each_chunk(half, rows)

    by_core(core_ref, work)


def base_kernel(core_ref, txt_ref, received_ref, img_ref, img_received_ref, out_ref):
    count = out_ref.shape[0]
    two = count // 2

    def work(is_first):
        def texts(at):
            out_ref[at()] = txt_ref[at()] + decode(received_ref[at()], ONE_CHIP)

        def images(at):
            out_ref[at()] = decode(img_received_ref[at()], ONE_CHIP)

        if is_first:
            each_chunk(count, texts)
        else:
            each_chunk(two, images)
            out_ref[two:] = img_ref[:two]

    by_core(core_ref, work)


def near_kernel(k, core_ref, base_ref, received_ref, out_ref):
    pair = out_ref.shape[0]

    def rows(at):
        value = base_ref[at(k * pair)] + decode(received_ref[at()], TWO_CHIPS)
        out_ref[at()] = encode(value, FOUR_CHIPS)

    each_chunk(pair, rows)


def gather_sums_kernel(core_ref, base_ref, a_ref, b_ref, x_ref, loss_ref, keep_ref, give_ref):
    own = keep_ref.shape[0]
    give_ref[own:] = jnp.zeros((8, give_ref.shape[1]), jnp.float32)
    give_ref[own:, :128] = loss_ref[...]

    def rows(at):
        for start, ref in ((0, keep_ref), (own, give_ref)):
            total = base_ref[at(start)] + decode(x_ref[at(start)], FOUR_CHIPS)
            total = total + decode(a_ref[at(start)], FOUR_CHIPS)
            ref[at()] = total + decode(b_ref[at(start)], FOUR_CHIPS)

    each_chunk(own, rows)


def finish_kernel(batch, core_ref, img_ref, txt_ref, kept_ref, received_ref, loss_parts_ref, loss_ref, grad_img_ref, grad_txt_ref):
    own = kept_ref.shape[0]
    both = loss_parts_ref[...] + received_ref[own:, :128]
    loss_ref[...] = jnp.full((1, 1), jnp.sum(both) * (1.0 / batch), jnp.float32)

    def side(at, raw_ref, sum_ref, grad_ref):
        raw = raw_ref[at()]
        scale = row_scale(raw)
        unit = raw * scale
        summed = sum_ref[at()]
        grad_ref[at()] = (summed - unit * jnp.sum(unit * summed, axis=1, keepdims=True)) * scale

    def work(is_first):
        def rows(at):
            side(at, img_ref, received_ref if is_first else kept_ref, grad_img_ref)
            side(at, txt_ref, kept_ref if is_first else received_ref, grad_txt_ref)

        each_chunk(own, rows)

    by_core(core_ref, work)


def transposed_product(weights, img):
    return lax.dot_general(
        weights, img, (((0,), (0,)), ((), ())), preferred_element_type=jnp.float32
    )


def body(image_embed, text_embed, exponent_of_sharpness, bias):
    own, features = image_embed.shape
    pair = 2 * own
    batch = own * ROWS * COLS
    core = lax.axis_index("row") & 1
    core, on_first = lax.optimization_barrier((core.reshape(1), core == 0))

    def array(rows, dtype, columns=features):
        return jax.ShapeDtypeStruct((rows, columns), dtype)

    low_half, low_piece = array(own, jnp.bfloat16), array(pair, jnp.bfloat16)

    keep, give = normalize(core, image_embed, text_embed)
    low = pack(keep, swap(give))
    slot_x, slot_1, slot_3 = move(low, "x"), move(low, "a"), move(low, "b")
    slot_2, slot_x3, slot_x1 = move(slot_3, "a"), move(slot_x, "b"), move(slot_1, "x")
    near = pack(low, slot_x, slot_1, slot_3)
    near_received = swap(near)
    sharpness = jnp.broadcast_to(exponent_of_sharpness.reshape(1, 1), (8, 128))
    shift = jnp.broadcast_to(bias.reshape(1, 1), (8, 128))

    scalars = (core, sharpness, shift)
    losses = array(8, jnp.float32, 128)
    wide, three, two = 4 * pair, 3 * pair, 2 * pair
    near_img, near_txt, near_weights, near_part, near_loss = tile_call(
        near_tile_kernel,
        "tile_near",
        two * wide,
        scalars,
        (near, near_received),
        (
            array(two, jnp.bfloat16),
            array(wide, jnp.bfloat16),
            array(two, jnp.bfloat16, wide),
            array(two, jnp.float32),
            losses,
        ),
    )
    slot_2, slot_x3, slot_x1, near_part = lax.optimization_barrier((slot_2, slot_x3, slot_x1, near_part))
    last_a = move(half_of(slot_x3, 0), "a")
    last_b = move(half_of(slot_x1, 1), "b")
    far = pack(slot_2, slot_x1, slot_x3)
    far_received = swap(far)
    far_img, middle_weights, middle_part, middle_loss = tile_call(
        middle_tile_kernel,
        "tile_middle",
        pair * wide,
        scalars,
        (far, far_received, near_txt),
        (low_piece, array(pair, jnp.bfloat16, wide), array(pair, jnp.float32), losses),
    )
    last_a, last_b, middle_part = lax.optimization_barrier((last_a, last_b, middle_part))
    last = pack(last_a, last_b)
    last_received = swap(last)
    far_txt, img, near_weights, far_weights, part, far_loss = tile_call(
        far_tile_kernel,
        "tile_far",
        three * three,
        scalars,
        (far, far_received, near_img, far_img, near_part, middle_part, near_weights, middle_weights),
        (
            array(three, jnp.bfloat16),
            array(three, jnp.bfloat16),
            array(three, jnp.bfloat16, wide),
            array(three, jnp.bfloat16, three),
            array(three, jnp.float32),
            losses,
        ),
    )
    last_weights, img_part, img_tail, near_tail, far_tail, last_tail, img_part_tail, last_loss = tile_call(
        last_tile_kernel,
        "tile_last",
        three * pair + pair * 2 * wide,
        scalars,
        (last, last_received, far, far_received, near_txt, far_txt, img, part),
        (
            array(three, jnp.bfloat16, pair),
            array(three, jnp.float32),
            low_piece,
            array(pair, jnp.bfloat16, wide),
            array(pair, jnp.bfloat16, three),
            array(pair, jnp.bfloat16, pair),
            array(pair, jnp.float32),
            losses,
        ),
        (low_piece,),
    )
    loss = near_loss + middle_loss + far_loss + last_loss

    def text_sums(weights, tail):
        return transposed_product(weights, img) + transposed_product(tail, img_tail)

    loss = loss + swap(loss, 0, 1)
    opposite_part = text_sums(last_weights, last_tail)
    sent = encode(jnp.where(on_first, img_part_tail, opposite_part), ONE_CHIP)
    sent, far_weights, far_tail, loss = lax.optimization_barrier((sent, far_weights, far_tail, loss))
    tail_received = swap(sent)
    far_part = text_sums(far_weights, far_tail)
    sent = encode(jnp.where(on_first, img_part, far_part), ONE_CHIP)
    loss = loss + swap(loss, 8, 1)
    tail_received, sent, loss = lax.optimization_barrier((tail_received, sent, loss))

    a, b = small_call(
        opposite_kernel, "opposite", core, (opposite_part, img_part_tail, tail_received), (low_half, low_half)
    )
    a, b, sent, near_weights, near_tail = lax.optimization_barrier((a, b, sent, near_weights, near_tail))
    from_a, from_b = move(a, "a"), move(b, "b")
    rest_received = swap(sent)
    near_part = text_sums(near_weights, near_tail)
    sent = encode(near_part, ONE_CHIP)
    loss = loss + swap(loss, 0, 2)
    (second,) = small_call(
        second_kernel, "second", core, (far_part, rest_received), (low_piece,)
    )
    from_a, from_b, second, sent, loss = lax.optimization_barrier((from_a, from_b, second, sent, loss))

    second_received = move(second, "a")
    x, b = small_call(
        far_kernel,
        "far",
        core,
        (far_part, rest_received, img_part, img_part_tail, tail_received, from_a, from_b),
        (low_piece,) * 2,
    )
    x, b, sent = lax.optimization_barrier((x, b, sent))
    from_x, from_b = move(x, "x"), move(b, "b")
    near_received = swap(sent)
    (base,) = small_call(
        base_kernel, "base", core, (near_part, near_received, img_part, rest_received), (array(wide, jnp.float32),)
    )
    base, loss = lax.optimization_barrier((base, loss))
    loss = loss + swap(loss, 0, 6)
    second_received, base, loss = lax.optimization_barrier((second_received, base, loss))

    def near_slot(k, received):
        (out,) = small_call(
            lambda *refs: near_kernel(k, *refs), "near", core, (base, received), (low_piece,)
        )
        return out

    from_b, from_x, from_a = (
        move(near_slot(3, second_received), "b"),
        move(near_slot(1, from_b), "x"),
        move(near_slot(2, from_x), "a"),
    )
    loss = loss + swap(loss, 2, 0)
    loss = loss + swap(loss, 6, 0)
    keep, give = small_call(
        gather_sums_kernel,
        "gather_sums",
        core,
        (base, from_a, from_b, from_x, loss),
        (array(own, jnp.float32), array(own + 8, jnp.float32)),
    )
    grad = array(own, jnp.float32)
    loss_value, grad_image, grad_text = small_call(
        lambda *refs: finish_kernel(batch, *refs),
        "finish",
        core,
        (image_embed, text_embed, keep, swap(give), loss),
        (array(1, jnp.float32, 1), grad, grad),
    )
    return (loss_value.reshape(()), grad_image, grad_text)


def solution(mesh):
    in_specs = (P(("row", "col"), None), P(("row", "col"), None), P(), P())
    out_specs = (P(), P(("row", "col"), None), P(("row", "col"), None))
    return jax.shard_map(body, mesh=mesh, in_specs=in_specs, out_specs=out_specs, check_vma=False)
```

```python
import jax
import jax.numpy as jnp
from jax import lax
from jax.experimental import pallas as pl
from jax.experimental.pallas import tpu as pltpu
from jax.sharding import PartitionSpec as P

VMEM = pl.BlockSpec(memory_space=pltpu.VMEM)
SMEM = pl.BlockSpec(memory_space=pltpu.SMEM)
HBM = pl.BlockSpec(memory_space=pltpu.HBM)
MIB = 1024 * 1024
TINY = 1.1754944e-38
AXES = ("row", "col")
ROWS, COLS = 16, 8
ONE_CHIP, TWO_CHIPS, FOUR_CHIPS = 0.5, 0.25, 0.125
PARTNERS = {"x": ((0, 1), (8, 1)), "a": ((0, 2), (2, 0)), "b": ((0, 6), (6, 0))}


def exchange(x, bits_of_core):
    pairs = []
    for row in range(ROWS):
        for col in range(COLS):
            row_bits, col_bits = bits_of_core[row & 1]
            pairs.append((row * COLS + col, (row ^ row_bits) * COLS + (col ^ col_bits)))
    return lax.ppermute(x, AXES, pairs)


def move(x, step):
    return exchange(x, PARTNERS[step])


def swap(x, row_bits=1, col_bits=0):
    return exchange(x, ((row_bits, col_bits),) * 2)


def encode(x, shift):
    y = x * shift
    y2 = y * y
    y4 = y2 * y2
    return (y4 * y2 * (y * jnp.abs(y))).astype(jnp.bfloat16)


def decode(e, shift):
    f = e.astype(jnp.float32)
    size = jnp.exp2(jnp.log2(jnp.maximum(jnp.abs(f), TINY)) * 0.125)
    return jnp.where(f < 0.0, -size, size) * (1.0 / shift)


def row_scale(raw):
    return lax.rsqrt(jnp.sum(raw * raw, axis=1, keepdims=True) + 1e-06)


def by_core(core_ref, work):
    pl.when(core_ref[0] == 0)(lambda: work(True))
    pl.when(core_ref[0] != 0)(lambda: work(False))


def normalize_kernel(core_ref, img_ref, txt_ref, keep_ref, give_ref, raw_ref, sems):
    copies = [
        pltpu.make_async_copy(source, raw_ref.at[k], sems.at[k])
        for k, source in enumerate((txt_ref, img_ref))
    ]
    for copy in copies:
        copy.start()

    def low(k):
        raw = raw_ref[k]
        return (raw * row_scale(raw)).astype(jnp.bfloat16)

    for k, copy in enumerate(copies):
        copy.wait()

        def work(is_first, k=k):
            ref = keep_ref if (k == 0) == is_first else give_ref
            ref[...] = low(k)

        by_core(core_ref, work)


def normalize(core, img, txt):
    low = jax.ShapeDtypeStruct(img.shape, jnp.bfloat16)
    return pl.pallas_call(
        normalize_kernel,
        out_shape=(low, low),
        in_specs=[SMEM, HBM, HBM],
        out_specs=(VMEM, VMEM),
        scratch_shapes=[pltpu.VMEM((2, *img.shape), jnp.float32), pltpu.SemaphoreType.DMA((2,))],
        compiler_params=pltpu.CompilerParams(vmem_limit_bytes=59 * MIB),
        name="normalize",
    )(core, img, txt)


def pack_kernel(*refs):
    out_ref = refs[-1]
    start = 0
    for ref in refs[:-1]:
        out_ref[start : start + ref.shape[0]] = ref[...]
        start += ref.shape[0]


def pack(*pieces):
    shape = (sum(p.shape[0] for p in pieces), pieces[0].shape[1])
    return pl.pallas_call(
        pack_kernel,
        out_shape=jax.ShapeDtypeStruct(shape, pieces[0].dtype),
        in_specs=[VMEM] * len(pieces),
        out_specs=VMEM,
        compiler_params=pltpu.CompilerParams(vmem_limit_bytes=8 * MIB),
        name="pack",
    )(*pieces)


def half_kernel(k, in_ref, out_ref):
    rows = out_ref.shape[0]
    out_ref[...] = in_ref[k * rows : (k + 1) * rows]


def half_of(x, k):
    return pl.pallas_call(
        lambda *refs: half_kernel(k, *refs),
        out_shape=jax.ShapeDtypeStruct((x.shape[0] // 2, x.shape[1]), x.dtype),
        in_specs=[VMEM],
        out_specs=VMEM,
        compiler_params=pltpu.CompilerParams(vmem_limit_bytes=4 * MIB),
        name="half_of",
    )(x)


def run_tiles(pair, sharp_ref, bias_ref, jobs):
    sharp_scalar = jnp.max(sharp_ref[...])
    bias = jnp.max(bias_ref[...])
    steps = [(job, k) for job in jobs for k in range(len(job[1]))]

    def products(step):
        job, k = step
        return lax.dot_general(
            job[0][...], job[1][k][0][...], (((1,), (1,)), ((), ())), preferred_element_type=jnp.float32
        )

    loss = jnp.zeros((8, 128), jnp.float32)
    following = products(steps[0])
    for i, (job, k) in enumerate(steps):
        current = following
        if i + 1 < len(steps):
            following = products(steps[i + 1])
        _, blocks, before, out, corner = job
        texts, weights_out = blocks[k]
        rows, cols = current.shape
        sharp = jnp.exp(jnp.full((1, cols), sharp_scalar, jnp.float32))
        logits = current * sharp + bias
        grown = jnp.exp(logits)
        one_more = 1.0 + grown
        weights = sharp * (grown / one_more)
        weights_out[...] = weights.astype(jnp.bfloat16)
        logs = jnp.log(one_more[: rows // 2] * one_more[rows // 2 :])
        logs = jnp.sum(logs.reshape(rows // 16, 8, cols), axis=0)
        if corner is not None:
            row_ids = lax.broadcasted_iota(jnp.int32, (pair, pair), 0)
            col_ids = lax.broadcasted_iota(jnp.int32, (pair, pair), 1)
            wanted = jnp.where(row_ids < pair // 2, row_ids + pair // 2, row_ids - pair // 2)
            same = (wanted == col_ids) & (corner == 0)
            own = weights[:pair, :pair] - jnp.where(same, sharp[:, :pair], 0.0)
            weights_out[:pair, :pair] = own.astype(jnp.bfloat16)
            matched = jnp.where(same, logits[:pair, :pair], 0.0)
            matched = jnp.sum(matched.reshape(pair // 8, 8, pair), axis=0)
            for start in range(0, pair, 128):
                loss = loss - matched[:, start : start + 128]
        for start in range(0, cols, 128):
            loss = loss + logs[:, start : start + 128]
        part = jnp.dot(weights_out[...], texts[...], preferred_element_type=jnp.float32)
        if k == 0:
            total = part if before is None else part + before[...]
        else:
            total = total + part
        if k == len(blocks) - 1:
            out[...] = total
    return loss


def row_blocks(ref, size, rows=None):
    return [ref.at[pl.ds(start, size)] for start in range(0, rows or ref.shape[0], size)]


def near_tile_kernel(core_ref, sharp_ref, bias_ref, near_ref, received_ref, img_ref, txt_ref, weights_ref, part_ref, loss_ref):
    count = img_ref.shape[0]
    pair = count // 2

    def work(is_first):
        txt_ref[...] = near_ref[...] if is_first else received_ref[...]
        img_ref[...] = received_ref[:count] if is_first else near_ref[count:]

    by_core(core_ref, work)
    jobs = []
    for k, rows in enumerate(row_blocks(img_ref, pair)):
        span = pl.ds(k * pair, pair)
        corner = core_ref[0] if k == 0 else None
        jobs.append((rows, [(txt_ref, weights_ref.at[span])], None, part_ref.at[span], corner))
    loss_ref[...] = run_tiles(pair, sharp_ref, bias_ref, jobs)


def middle_tile_kernel(core_ref, sharp_ref, bias_ref, far_ref, received_ref, txt_ref, img_ref, weights_ref, part_ref, loss_ref):
    pair = img_ref.shape[0]

    def work(is_first):
        img_ref[...] = received_ref[:pair] if is_first else far_ref[2 * pair :]

    by_core(core_ref, work)
    loss_ref[...] = run_tiles(pair, sharp_ref, bias_ref, [(img_ref, [(txt_ref, weights_ref)], None, part_ref, None)])


def far_tile_kernel(
    core_ref, sharp_ref, bias_ref, far_ref, received_ref, near_img_ref, far_img_ref, near_before_ref, far_before_ref,
    near_weights_ref, middle_weights_ref,
    txt_ref, img_ref, all_weights_ref, weights_ref, part_ref, loss_ref,
):
    pair = far_img_ref.shape[0]

    def work(is_first):
        txt_ref[...] = far_ref[...] if is_first else received_ref[...]

    by_core(core_ref, work)
    img_ref[: 2 * pair] = near_img_ref[...]
    img_ref[2 * pair :] = far_img_ref[...]
    all_weights_ref[: 2 * pair] = near_weights_ref[...]
    all_weights_ref[2 * pair :] = middle_weights_ref[...]
    jobs = []
    images = row_blocks(near_img_ref, pair) + [far_img_ref]
    before = row_blocks(near_before_ref, pair) + [far_before_ref]
    for k in range(3):
        span = pl.ds(k * pair, pair)
        jobs.append((images[k], [(txt_ref, weights_ref.at[span])], before[k], part_ref.at[span], None))
    loss_ref[...] = run_tiles(pair, sharp_ref, bias_ref, jobs)


def last_tile_kernel(
    core_ref, sharp_ref, bias_ref, last_ref, received_ref, far_ref, far_received_ref, near_txt_ref, far_txt_ref,
    img_ref, before_ref,
    weights_ref, part_ref, img_tail_ref, near_tail_ref, far_tail_ref, last_tail_ref, part_tail_ref, loss_ref, txt_ref,
):
    pair = last_ref.shape[0]
    half = pair // 2

    def work(is_first):
        txt_ref[...] = last_ref[...] if is_first else received_ref[...]
        img_tail_ref[:half] = far_received_ref[pair : pair + half] if is_first else far_ref[pair + half : 2 * pair]
        img_tail_ref[half:] = received_ref[:half] if is_first else last_ref[half:]

    by_core(core_ref, work)
    jobs = []
    for k, rows in enumerate(row_blocks(img_ref, pair)):
        span = pl.ds(k * pair, pair)
        jobs.append((rows, [(txt_ref, weights_ref.at[span])], before_ref.at[span], part_ref.at[span], None))
    blocks = [(near_txt_ref, near_tail_ref), (far_txt_ref, far_tail_ref), (txt_ref, last_tail_ref)]
    jobs.append((img_tail_ref, blocks, None, part_tail_ref, None))
    loss_ref[...] = run_tiles(pair, sharp_ref, bias_ref, jobs)


def tile_call(kernel, name, pairs, scalars, arrays, outs, scratch=()):
    features = arrays[0].shape[1]
    return pl.pallas_call(
        kernel,
        out_shape=outs,
        in_specs=[SMEM] + [VMEM] * (len(scalars) - 1 + len(arrays)),
        out_specs=(VMEM,) * len(outs),
        scratch_shapes=[pltpu.VMEM(x.shape, x.dtype) for x in scratch],
        compiler_params=pltpu.CompilerParams(vmem_limit_bytes=16 * MIB),
        cost_estimate=pl.CostEstimate(
            flops=4 * pairs * features,
            bytes_accessed=sum(2 * x.size for x in arrays),
            transcendentals=3 * pairs,
        ),
        name=name,
    )(*scalars, *arrays)


def small_call(kernel, name, core, arrays, outs):
    size = sum(x.size * x.dtype.itemsize for x in (*arrays, *outs))
    return pl.pallas_call(
        kernel,
        out_shape=outs,
        in_specs=[SMEM] + [VMEM] * len(arrays),
        out_specs=(VMEM,) * len(outs),
        compiler_params=pltpu.CompilerParams(vmem_limit_bytes=size + 4 * MIB),
        name=name,
    )(core, *arrays)


CHUNK = 64


def each_chunk(rows, work):
    def step(i, carry):
        first = pl.multiple_of(i * CHUNK, CHUNK)
        work(lambda start=0: pl.ds(start + first, CHUNK))
        return carry

    lax.fori_loop(0, rows // CHUNK, step, 0)


def opposite_kernel(core_ref, txt_ref, img_ref, received_ref, a_ref, b_ref):
    half = a_ref.shape[0]

    def work(is_first):
        def texts(at):
            a_ref[at()] = encode(txt_ref[at()] + decode(received_ref[at()], ONE_CHIP), ONE_CHIP)
            b_ref[at()] = encode(txt_ref[at(half)] + decode(received_ref[at(half)], ONE_CHIP), ONE_CHIP)

        def images(at):
            a_ref[at()] = received_ref[at(half)]
            b_ref[at()] = encode(img_ref[at(half)], ONE_CHIP)

        each_chunk(half, texts if is_first else images)

    by_core(core_ref, work)


def second_kernel(core_ref, txt_ref, received_ref, out_ref):
    pair = out_ref.shape[0]

    def work(is_first):
        def rows(at):
            if is_first:
                value = txt_ref[at()] + decode(received_ref[at()], ONE_CHIP)
            else:
                value = decode(received_ref[at(2 * pair)], ONE_CHIP)
            out_ref[at()] = encode(value, TWO_CHIPS)

        each_chunk(pair, rows)

    by_core(core_ref, work)


def far_kernel(
    core_ref, txt_ref, txt_received_ref, img_ref, img_tail_ref, tail_received_ref, from_a_ref, from_b_ref, x_ref, b_ref
):
    pair = x_ref.shape[0]
    half = pair // 2

    def work(is_first):
        def rows(at):
            def base(i):
                if is_first:
                    return txt_ref[at(i * half)] + decode(txt_received_ref[at(i * half)], ONE_CHIP)
                if i == 2:
                    return decode(tail_received_ref[at()], ONE_CHIP)
                return img_tail_ref[at()] if i == 3 else img_ref[at(i * half)]

            x_ref[at()] = encode(base(2), TWO_CHIPS)
            x_ref[at(half)] = encode(base(3) + decode(from_b_ref[at()], ONE_CHIP), TWO_CHIPS)
            b_ref[at()] = encode(base(4) + decode(from_a_ref[at()], ONE_CHIP), TWO_CHIPS)
            b_ref[at(half)] = encode(base(5), TWO_CHIPS)

        each_chunk(half, rows)

    by_core(core_ref, work)


def base_kernel(core_ref, txt_ref, received_ref, img_ref, img_received_ref, out_ref):
    count = out_ref.shape[0]
    two = count // 2

    def work(is_first):
        def texts(at):
            out_ref[at()] = txt_ref[at()] + decode(received_ref[at()], ONE_CHIP)

        def images(at):
            out_ref[at()] = decode(img_received_ref[at()], ONE_CHIP)

        if is_first:
            each_chunk(count, texts)
        else:
            each_chunk(two, images)
            out_ref[two:] = img_ref[:two]

    by_core(core_ref, work)


def near_kernel(k, core_ref, base_ref, received_ref, out_ref):
    pair = out_ref.shape[0]

    def rows(at):
        value = base_ref[at(k * pair)] + decode(received_ref[at()], TWO_CHIPS)
        out_ref[at()] = encode(value, FOUR_CHIPS)

    each_chunk(pair, rows)


def gather_sums_kernel(core_ref, base_ref, a_ref, b_ref, x_ref, loss_ref, keep_ref, give_ref):
    own = keep_ref.shape[0]
    give_ref[own:] = jnp.zeros((8, give_ref.shape[1]), jnp.float32)
    give_ref[own:, :128] = loss_ref[...]

    def rows(at):
        for start, ref in ((0, keep_ref), (own, give_ref)):
            total = base_ref[at(start)] + decode(x_ref[at(start)], FOUR_CHIPS)
            total = total + decode(a_ref[at(start)], FOUR_CHIPS)
            ref[at()] = total + decode(b_ref[at(start)], FOUR_CHIPS)

    each_chunk(own, rows)


def finish_kernel(batch, core_ref, img_ref, txt_ref, kept_ref, received_ref, loss_parts_ref, loss_ref, grad_img_ref, grad_txt_ref):
    own = kept_ref.shape[0]
    both = loss_parts_ref[...] + received_ref[own:, :128]
    loss_ref[...] = jnp.full((1, 1), jnp.sum(both) * (1.0 / batch), jnp.float32)

    def side(at, raw_ref, sum_ref, grad_ref):
        raw = raw_ref[at()]
        scale = row_scale(raw)
        unit = raw * scale
        summed = sum_ref[at()]
        grad_ref[at()] = (summed - unit * jnp.sum(unit * summed, axis=1, keepdims=True)) * scale

    def work(is_first):
        def rows(at):
            side(at, img_ref, received_ref if is_first else kept_ref, grad_img_ref)
            side(at, txt_ref, kept_ref if is_first else received_ref, grad_txt_ref)

        each_chunk(own, rows)

    by_core(core_ref, work)


def transposed_product(weights, img):
    return lax.dot_general(
        weights, img, (((0,), (0,)), ((), ())), preferred_element_type=jnp.float32
    )


def body(image_embed, text_embed, exponent_of_sharpness, bias):
    own, features = image_embed.shape
    pair = 2 * own
    batch = own * ROWS * COLS
    core = lax.axis_index("row") & 1
    core, on_first = lax.optimization_barrier((core.reshape(1), core == 0))

    def array(rows, dtype, columns=features):
        return jax.ShapeDtypeStruct((rows, columns), dtype)

    low_half, low_piece = array(own, jnp.bfloat16), array(pair, jnp.bfloat16)

    keep, give = normalize(core, image_embed, text_embed)
    low = pack(keep, swap(give))
    slot_x, slot_1, slot_3 = move(low, "x"), move(low, "a"), move(low, "b")
    slot_2, slot_x3, slot_x1 = move(slot_3, "a"), move(slot_x, "b"), move(slot_1, "x")
    near = pack(low, slot_x, slot_1, slot_3)
    near_received = swap(near)
    sharpness = jnp.broadcast_to(exponent_of_sharpness.reshape(1, 1), (8, 128))
    shift = jnp.broadcast_to(bias.reshape(1, 1), (8, 128))

    scalars = (core, sharpness, shift)
    losses = array(8, jnp.float32, 128)
    wide, three, two = 4 * pair, 3 * pair, 2 * pair
    near_img, near_txt, near_weights, near_part, near_loss = tile_call(
        near_tile_kernel,
        "tile_near",
        two * wide,
        scalars,
        (near, near_received),
        (
            array(two, jnp.bfloat16),
            array(wide, jnp.bfloat16),
            array(two, jnp.bfloat16, wide),
            array(two, jnp.float32),
            losses,
        ),
    )
    slot_2, slot_x3, slot_x1, near_part = lax.optimization_barrier((slot_2, slot_x3, slot_x1, near_part))
    last_a = move(half_of(slot_x3, 0), "a")
    last_b = move(half_of(slot_x1, 1), "b")
    far = pack(slot_2, slot_x1, slot_x3)
    far_received = swap(far)
    far_img, middle_weights, middle_part, middle_loss = tile_call(
        middle_tile_kernel,
        "tile_middle",
        pair * wide,
        scalars,
        (far, far_received, near_txt),
        (low_piece, array(pair, jnp.bfloat16, wide), array(pair, jnp.float32), losses),
    )
    far_txt, img, near_weights, far_weights, part, far_loss = tile_call(
        far_tile_kernel,
        "tile_far",
        three * three,
        scalars,
        (far, far_received, near_img, far_img, near_part, middle_part, near_weights, middle_weights),
        (
            array(three, jnp.bfloat16),
            array(three, jnp.bfloat16),
            array(three, jnp.bfloat16, wide),
            array(three, jnp.bfloat16, three),
            array(three, jnp.float32),
            losses,
        ),
    )
    last_a, last_b, part = lax.optimization_barrier((last_a, last_b, part))
    last = pack(last_a, last_b)
    last_received = swap(last)
    last_weights, img_part, img_tail, near_tail, far_tail, last_tail, img_part_tail, last_loss = tile_call(
        last_tile_kernel,
        "tile_last",
        three * pair + pair * 2 * wide,
        scalars,
        (last, last_received, far, far_received, near_txt, far_txt, img, part),
        (
            array(three, jnp.bfloat16, pair),
            array(three, jnp.float32),
            low_piece,
            array(pair, jnp.bfloat16, wide),
            array(pair, jnp.bfloat16, three),
            array(pair, jnp.bfloat16, pair),
            array(pair, jnp.float32),
            losses,
        ),
        (low_piece,),
    )
    loss = near_loss + middle_loss + far_loss + last_loss

    def text_sums(weights, tail):
        return transposed_product(weights, img) + transposed_product(tail, img_tail)

    loss = loss + swap(loss, 0, 1)
    opposite_part = text_sums(last_weights, last_tail)
    sent = encode(jnp.where(on_first, img_part_tail, opposite_part), ONE_CHIP)
    sent, far_weights, far_tail, loss = lax.optimization_barrier((sent, far_weights, far_tail, loss))
    tail_received = swap(sent)
    far_part = text_sums(far_weights, far_tail)
    sent = encode(jnp.where(on_first, img_part, far_part), ONE_CHIP)
    loss = loss + swap(loss, 8, 1)
    tail_received, sent, loss = lax.optimization_barrier((tail_received, sent, loss))

    a, b = small_call(
        opposite_kernel, "opposite", core, (opposite_part, img_part_tail, tail_received), (low_half, low_half)
    )
    a, b, sent, near_weights, near_tail = lax.optimization_barrier((a, b, sent, near_weights, near_tail))
    from_a, from_b = move(a, "a"), move(b, "b")
    rest_received = swap(sent)
    near_part = text_sums(near_weights, near_tail)
    sent = encode(near_part, ONE_CHIP)
    loss = loss + swap(loss, 0, 2)
    (second,) = small_call(
        second_kernel, "second", core, (far_part, rest_received), (low_piece,)
    )
    from_a, from_b, second, sent, loss = lax.optimization_barrier((from_a, from_b, second, sent, loss))

    second_received = move(second, "a")
    x, b = small_call(
        far_kernel,
        "far",
        core,
        (far_part, rest_received, img_part, img_part_tail, tail_received, from_a, from_b),
        (low_piece,) * 2,
    )
    x, b, sent = lax.optimization_barrier((x, b, sent))
    from_x, from_b = move(x, "x"), move(b, "b")
    near_received = swap(sent)
    (base,) = small_call(
        base_kernel, "base", core, (near_part, near_received, img_part, rest_received), (array(wide, jnp.float32),)
    )
    base, loss = lax.optimization_barrier((base, loss))
    loss = loss + swap(loss, 0, 6)
    second_received, base, loss = lax.optimization_barrier((second_received, base, loss))

    def near_slot(k, received):
        (out,) = small_call(
            lambda *refs: near_kernel(k, *refs), "near", core, (base, received), (low_piece,)
        )
        return out

    from_b, from_x, from_a = (
        move(near_slot(3, second_received), "b"),
        move(near_slot(1, from_b), "x"),
        move(near_slot(2, from_x), "a"),
    )
    loss = loss + swap(loss, 2, 0)
    loss = loss + swap(loss, 6, 0)
    keep, give = small_call(
        gather_sums_kernel,
        "gather_sums",
        core,
        (base, from_a, from_b, from_x, loss),
        (array(own, jnp.float32), array(own + 8, jnp.float32)),
    )
    grad = array(own, jnp.float32)
    loss_value, grad_image, grad_text = small_call(
        lambda *refs: finish_kernel(batch, *refs),
        "finish",
        core,
        (image_embed, text_embed, keep, swap(give), loss),
        (array(1, jnp.float32, 1), grad, grad),
    )
    return (loss_value.reshape(()), grad_image, grad_text)


def solution(mesh):
    in_specs = (P(("row", "col"), None), P(("row", "col"), None), P(), P())
    out_specs = (P(), P(("row", "col"), None), P(("row", "col"), None))
    return jax.shard_map(body, mesh=mesh, in_specs=in_specs, out_specs=out_specs, check_vma=False)
```

```python
import jax
import jax.numpy as jnp
from jax import lax
from jax.experimental import pallas as pl
from jax.experimental.pallas import tpu as pltpu
from jax.sharding import PartitionSpec as P

VMEM = pl.BlockSpec(memory_space=pltpu.VMEM)
SMEM = pl.BlockSpec(memory_space=pltpu.SMEM)
HBM = pl.BlockSpec(memory_space=pltpu.HBM)
MIB = 1024 * 1024
TINY = 1.1754944e-38
AXES = ("row", "col")
ROWS, COLS = 16, 8
ONE_CHIP, TWO_CHIPS, FOUR_CHIPS = 0.5, 0.25, 0.125
PARTNERS = {"x": ((0, 1), (8, 1)), "a": ((0, 2), (2, 0)), "b": ((0, 6), (6, 0))}


def exchange(x, bits_of_core):
    pairs = []
    for row in range(ROWS):
        for col in range(COLS):
            row_bits, col_bits = bits_of_core[row & 1]
            pairs.append((row * COLS + col, (row ^ row_bits) * COLS + (col ^ col_bits)))
    return lax.ppermute(x, AXES, pairs)


def move(x, step):
    return exchange(x, PARTNERS[step])


def swap(x, row_bits=1, col_bits=0):
    return exchange(x, ((row_bits, col_bits),) * 2)


def encode(x, shift):
    y = x * shift
    y2 = y * y
    y4 = y2 * y2
    return (y4 * y2 * (y * jnp.abs(y))).astype(jnp.bfloat16)


def decode(e, shift):
    f = e.astype(jnp.float32)
    size = jnp.exp2(jnp.log2(jnp.maximum(jnp.abs(f), TINY)) * 0.125)
    return jnp.where(f < 0.0, -size, size) * (1.0 / shift)


def row_scale(raw):
    return lax.rsqrt(jnp.sum(raw * raw, axis=1, keepdims=True) + 1e-06)


def by_core(core_ref, work):
    pl.when(core_ref[0] == 0)(lambda: work(True))
    pl.when(core_ref[0] != 0)(lambda: work(False))


def normalize_kernel(core_ref, img_ref, txt_ref, keep_ref, give_ref, raw_ref, sems):
    copies = [
        pltpu.make_async_copy(source, raw_ref.at[k], sems.at[k])
        for k, source in enumerate((txt_ref, img_ref))
    ]
    for copy in copies:
        copy.start()

    def low(k):
        raw = raw_ref[k]
        return (raw * row_scale(raw)).astype(jnp.bfloat16)

    for k, copy in enumerate(copies):
        copy.wait()

        def work(is_first, k=k):
            ref = keep_ref if (k == 0) == is_first else give_ref
            ref[...] = low(k)

        by_core(core_ref, work)


def normalize(core, img, txt):
    low = jax.ShapeDtypeStruct(img.shape, jnp.bfloat16)
    return pl.pallas_call(
        normalize_kernel,
        out_shape=(low, low),
        in_specs=[SMEM, HBM, HBM],
        out_specs=(VMEM, VMEM),
        scratch_shapes=[pltpu.VMEM((2, *img.shape), jnp.float32), pltpu.SemaphoreType.DMA((2,))],
        compiler_params=pltpu.CompilerParams(vmem_limit_bytes=6 * MIB),
        name="normalize",
    )(core, img, txt)


def pack_kernel(*refs):
    out_ref = refs[-1]
    start = 0
    for ref in refs[:-1]:
        out_ref[start : start + ref.shape[0]] = ref[...]
        start += ref.shape[0]


def pack(*pieces):
    shape = (sum(p.shape[0] for p in pieces), pieces[0].shape[1])
    return pl.pallas_call(
        pack_kernel,
        out_shape=jax.ShapeDtypeStruct(shape, pieces[0].dtype),
        in_specs=[VMEM] * len(pieces),
        out_specs=VMEM,
        compiler_params=pltpu.CompilerParams(vmem_limit_bytes=8 * MIB),
        name="pack",
    )(*pieces)


def half_kernel(k, in_ref, out_ref):
    rows = out_ref.shape[0]
    out_ref[...] = in_ref[k * rows : (k + 1) * rows]


def half_of(x, k):
    return pl.pallas_call(
        lambda *refs: half_kernel(k, *refs),
        out_shape=jax.ShapeDtypeStruct((x.shape[0] // 2, x.shape[1]), x.dtype),
        in_specs=[VMEM],
        out_specs=VMEM,
        compiler_params=pltpu.CompilerParams(vmem_limit_bytes=4 * MIB),
        name="half_of",
    )(x)


def run_tiles(pair, sharp_ref, bias_ref, jobs):
    sharp_scalar = jnp.max(sharp_ref[...])
    bias = jnp.max(bias_ref[...])
    steps = [(job, k) for job in jobs for k in range(len(job[1]))]

    def products(step):
        job, k = step
        return lax.dot_general(
            job[0][...], job[1][k][0][...], (((1,), (1,)), ((), ())), preferred_element_type=jnp.float32
        )

    loss = jnp.zeros((8, 128), jnp.float32)
    following = products(steps[0])
    for i, (job, k) in enumerate(steps):
        current = following
        if i + 1 < len(steps):
            following = products(steps[i + 1])
        _, blocks, before, out, corner = job
        texts, weights_out = blocks[k]
        rows, cols = current.shape
        sharp = jnp.exp(jnp.full((1, cols), sharp_scalar, jnp.float32))
        logits = current * sharp + bias
        grown = jnp.exp(logits)
        one_more = 1.0 + grown
        weights = sharp * (grown / one_more)
        weights_out[...] = weights.astype(jnp.bfloat16)
        logs = jnp.log(one_more[: rows // 2] * one_more[rows // 2 :])
        logs = jnp.sum(logs.reshape(rows // 16, 8, cols), axis=0)
        if corner is not None:
            row_ids = lax.broadcasted_iota(jnp.int32, (pair, pair), 0)
            col_ids = lax.broadcasted_iota(jnp.int32, (pair, pair), 1)
            wanted = jnp.where(row_ids < pair // 2, row_ids + pair // 2, row_ids - pair // 2)
            same = (wanted == col_ids) & (corner == 0)
            own = weights[:pair, :pair] - jnp.where(same, sharp[:, :pair], 0.0)
            weights_out[:pair, :pair] = own.astype(jnp.bfloat16)
            matched = jnp.where(same, logits[:pair, :pair], 0.0)
            matched = jnp.sum(matched.reshape(pair // 8, 8, pair), axis=0)
            for start in range(0, pair, 128):
                loss = loss - matched[:, start : start + 128]
        for start in range(0, cols, 128):
            loss = loss + logs[:, start : start + 128]
        part = jnp.dot(weights_out[...], texts[...], preferred_element_type=jnp.float32)
        if k == 0:
            total = part if before is None else part + before[...]
        else:
            total = total + part
        if k == len(blocks) - 1:
            out[...] = total
    return loss


def row_blocks(ref, size, rows=None):
    return [ref.at[pl.ds(start, size)] for start in range(0, rows or ref.shape[0], size)]


def near_tile_kernel(core_ref, sharp_ref, bias_ref, near_ref, received_ref, img_ref, txt_ref, weights_ref, part_ref, loss_ref):
    count = img_ref.shape[0]
    pair = count // 2

    def work(is_first):
        txt_ref[...] = near_ref[...] if is_first else received_ref[...]
        img_ref[...] = received_ref[:count] if is_first else near_ref[count:]

    by_core(core_ref, work)
    jobs = []
    for k, rows in enumerate(row_blocks(img_ref, pair)):
        span = pl.ds(k * pair, pair)
        corner = core_ref[0] if k == 0 else None
        jobs.append((rows, [(txt_ref, weights_ref.at[span])], None, part_ref.at[span], corner))
    loss_ref[...] = run_tiles(pair, sharp_ref, bias_ref, jobs)


def far_tile_kernel(
    core_ref, sharp_ref, bias_ref, far_ref, received_ref, near_img_ref, near_before_ref,
    txt_ref, img_ref, weights_ref, part_ref, loss_ref,
):
    count = near_img_ref.shape[0]
    pair = count // 2

    def work(is_first):
        txt_ref[...] = far_ref[...] if is_first else received_ref[...]
        img_ref[count:] = received_ref[:pair] if is_first else far_ref[count:]

    by_core(core_ref, work)
    img_ref[:count] = near_img_ref[...]
    jobs = []
    before = row_blocks(near_before_ref, pair) + [None]
    for k, rows in enumerate(row_blocks(img_ref, pair)):
        span = pl.ds(k * pair, pair)
        jobs.append((rows, [(txt_ref, weights_ref.at[span])], before[k], part_ref.at[span], None))
    loss_ref[...] = run_tiles(pair, sharp_ref, bias_ref, jobs)


def middle_tile_kernel(
    core_ref, sharp_ref, bias_ref, img_ref, txt_ref, before_ref, near_weights_ref, weights_ref, part_ref, loss_ref
):
    pair = part_ref.shape[0]
    span = pl.ds(2 * pair, pair)
    weights_ref[: 2 * pair] = near_weights_ref[...]
    job = (img_ref.at[span], [(txt_ref, weights_ref.at[span])], before_ref.at[span], part_ref, None)
    loss_ref[...] = run_tiles(pair, sharp_ref, bias_ref, [job])


def last_tile_kernel(
    core_ref, sharp_ref, bias_ref, last_ref, received_ref, far_ref, far_received_ref, near_txt_ref, far_txt_ref,
    img_ref, before_ref, middle_before_ref,
    weights_ref, part_ref, img_tail_ref, near_tail_ref, far_tail_ref, last_tail_ref, part_tail_ref, loss_ref, txt_ref,
):
    pair = last_ref.shape[0]
    half = pair // 2

    def work(is_first):
        txt_ref[...] = last_ref[...] if is_first else received_ref[...]
        img_tail_ref[:half] = far_received_ref[pair : pair + half] if is_first else far_ref[pair + half : 2 * pair]
        img_tail_ref[half:] = received_ref[:half] if is_first else last_ref[half:]

    by_core(core_ref, work)
    jobs = []
    before = row_blocks(before_ref, pair, 2 * pair) + [middle_before_ref]
    for k, rows in enumerate(row_blocks(img_ref, pair)):
        span = pl.ds(k * pair, pair)
        jobs.append((rows, [(txt_ref, weights_ref.at[span])], before[k], part_ref.at[span], None))
    blocks = [(near_txt_ref, near_tail_ref), (far_txt_ref, far_tail_ref), (txt_ref, last_tail_ref)]
    jobs.append((img_tail_ref, blocks, None, part_tail_ref, None))
    loss_ref[...] = run_tiles(pair, sharp_ref, bias_ref, jobs)


def tile_call(kernel, name, pairs, scalars, arrays, outs, scratch=()):
    features = arrays[0].shape[1]
    return pl.pallas_call(
        kernel,
        out_shape=outs,
        in_specs=[SMEM] + [VMEM] * (len(scalars) - 1 + len(arrays)),
        out_specs=(VMEM,) * len(outs),
        scratch_shapes=[pltpu.VMEM(x.shape, x.dtype) for x in scratch],
        compiler_params=pltpu.CompilerParams(vmem_limit_bytes=16 * MIB),
        cost_estimate=pl.CostEstimate(
            flops=4 * pairs * features,
            bytes_accessed=sum(2 * x.size for x in arrays),
            transcendentals=3 * pairs,
        ),
        name=name,
    )(*scalars, *arrays)


def small_call(kernel, name, core, arrays, outs):
    size = sum(x.size * x.dtype.itemsize for x in (*arrays, *outs))
    return pl.pallas_call(
        kernel,
        out_shape=outs,
        in_specs=[SMEM] + [VMEM] * len(arrays),
        out_specs=(VMEM,) * len(outs),
        compiler_params=pltpu.CompilerParams(vmem_limit_bytes=size + 4 * MIB),
        name=name,
    )(core, *arrays)


CHUNK = 64


def each_chunk(rows, work):
    def step(i, carry):
        first = pl.multiple_of(i * CHUNK, CHUNK)
        work(lambda start=0: pl.ds(start + first, CHUNK))
        return carry

    lax.fori_loop(0, rows // CHUNK, step, 0)


def opposite_kernel(core_ref, txt_ref, img_ref, received_ref, a_ref, b_ref):
    half = a_ref.shape[0]

    def work(is_first):
        def texts(at):
            a_ref[at()] = encode(txt_ref[at()] + decode(received_ref[at()], ONE_CHIP), ONE_CHIP)
            b_ref[at()] = encode(txt_ref[at(half)] + decode(received_ref[at(half)], ONE_CHIP), ONE_CHIP)

        def images(at):
            a_ref[at()] = received_ref[at(half)]
            b_ref[at()] = encode(img_ref[at(half)], ONE_CHIP)

        each_chunk(half, texts if is_first else images)

    by_core(core_ref, work)


def second_kernel(core_ref, txt_ref, received_ref, out_ref):
    pair = out_ref.shape[0]

    def work(is_first):
        def rows(at):
            if is_first:
                value = txt_ref[at()] + decode(received_ref[at()], ONE_CHIP)
            else:
                value = decode(received_ref[at(2 * pair)], ONE_CHIP)
            out_ref[at()] = encode(value, TWO_CHIPS)

        each_chunk(pair, rows)

    by_core(core_ref, work)


def far_kernel(
    core_ref, txt_ref, txt_received_ref, img_ref, img_tail_ref, tail_received_ref, from_a_ref, from_b_ref, x_ref, b_ref
):
    pair = x_ref.shape[0]
    half = pair // 2

    def work(is_first):
        def rows(at):
            def base(i):
                if is_first:
                    return txt_ref[at(i * half)] + decode(txt_received_ref[at(i * half)], ONE_CHIP)
                if i == 2:
                    return decode(tail_received_ref[at()], ONE_CHIP)
                return img_tail_ref[at()] if i == 3 else img_ref[at(i * half)]

            x_ref[at()] = encode(base(2), TWO_CHIPS)
            x_ref[at(half)] = encode(base(3) + decode(from_b_ref[at()], ONE_CHIP), TWO_CHIPS)
            b_ref[at()] = encode(base(4) + decode(from_a_ref[at()], ONE_CHIP), TWO_CHIPS)
            b_ref[at(half)] = encode(base(5), TWO_CHIPS)

        each_chunk(half, rows)

    by_core(core_ref, work)


def base_kernel(core_ref, txt_ref, received_ref, img_ref, img_received_ref, out_ref):
    count = out_ref.shape[0]
    two = count // 2

    def work(is_first):
        def texts(at):
            out_ref[at()] = txt_ref[at()] + decode(received_ref[at()], ONE_CHIP)

        def images(at):
            out_ref[at()] = decode(img_received_ref[at()], ONE_CHIP)

        if is_first:
            each_chunk(count, texts)
        else:
            each_chunk(two, images)
            out_ref[two:] = img_ref[:two]

    by_core(core_ref, work)


def near_kernel(k, core_ref, base_ref, received_ref, out_ref):
    pair = out_ref.shape[0]

    def rows(at):
        value = base_ref[at(k * pair)] + decode(received_ref[at()], TWO_CHIPS)
        out_ref[at()] = encode(value, FOUR_CHIPS)

    each_chunk(pair, rows)


def gather_sums_kernel(core_ref, base_ref, a_ref, b_ref, x_ref, loss_ref, keep_ref, give_ref):
    own = keep_ref.shape[0]
    give_ref[own:] = jnp.zeros((8, give_ref.shape[1]), jnp.float32)
    give_ref[own:, :128] = loss_ref[...]

    def rows(at):
        for start, ref in ((0, keep_ref), (own, give_ref)):
            total = base_ref[at(start)] + decode(x_ref[at(start)], FOUR_CHIPS)
            total = total + decode(a_ref[at(start)], FOUR_CHIPS)
            ref[at()] = total + decode(b_ref[at(start)], FOUR_CHIPS)

    each_chunk(own, rows)


def finish_kernel(batch, core_ref, img_ref, txt_ref, kept_ref, received_ref, loss_parts_ref, loss_ref, grad_img_ref, grad_txt_ref):
    own = kept_ref.shape[0]
    both = loss_parts_ref[...] + received_ref[own:, :128]
    loss_ref[...] = jnp.full((1, 1), jnp.sum(both) * (1.0 / batch), jnp.float32)

    def side(at, raw_ref, sum_ref, grad_ref):
        raw = raw_ref[at()]
        scale = row_scale(raw)
        unit = raw * scale
        summed = sum_ref[at()]
        grad_ref[at()] = (summed - unit * jnp.sum(unit * summed, axis=1, keepdims=True)) * scale

    def work(is_first):
        def rows(at):
            side(at, img_ref, received_ref if is_first else kept_ref, grad_img_ref)
            side(at, txt_ref, kept_ref if is_first else received_ref, grad_txt_ref)

        each_chunk(own, rows)

    by_core(core_ref, work)


def transposed_product(weights, img):
    return lax.dot_general(
        weights, img, (((0,), (0,)), ((), ())), preferred_element_type=jnp.float32
    )


def body(image_embed, text_embed, exponent_of_sharpness, bias):
    own, features = image_embed.shape
    pair = 2 * own
    batch = own * ROWS * COLS
    core = lax.axis_index("row") & 1
    core, on_first = lax.optimization_barrier((core.reshape(1), core == 0))

    def array(rows, dtype, columns=features):
        return jax.ShapeDtypeStruct((rows, columns), dtype)

    low_half, low_piece = array(own, jnp.bfloat16), array(pair, jnp.bfloat16)

    keep, give = normalize(core, image_embed, text_embed)
    low = pack(keep, swap(give))
    slot_x, slot_1, slot_3 = move(low, "x"), move(low, "a"), move(low, "b")
    slot_2, slot_x3, slot_x1 = move(slot_3, "a"), move(slot_x, "b"), move(slot_1, "x")
    near = pack(low, slot_x, slot_1, slot_3)
    near_received = swap(near)
    sharpness = jnp.broadcast_to(exponent_of_sharpness.reshape(1, 1), (8, 128))
    shift = jnp.broadcast_to(bias.reshape(1, 1), (8, 128))

    scalars = (core, sharpness, shift)
    losses = array(8, jnp.float32, 128)
    wide, three, two = 4 * pair, 3 * pair, 2 * pair
    near_img, near_txt, near_weights, near_part, near_loss = tile_call(
        near_tile_kernel,
        "tile_near",
        two * wide,
        scalars,
        (near, near_received),
        (
            array(two, jnp.bfloat16),
            array(wide, jnp.bfloat16),
            array(two, jnp.bfloat16, wide),
            array(two, jnp.float32),
            losses,
        ),
    )
    slot_2, slot_x3, slot_x1, near_part = lax.optimization_barrier((slot_2, slot_x3, slot_x1, near_part))
    last_a = move(half_of(slot_x3, 0), "a")
    last_b = move(half_of(slot_x1, 1), "b")
    far = pack(slot_2, slot_x1, slot_x3)
    far_received = swap(far)
    far_txt, img, far_weights, part, far_loss = tile_call(
        far_tile_kernel,
        "tile_far",
        three * three,
        scalars,
        (far, far_received, near_img, near_part),
        (
            array(three, jnp.bfloat16),
            array(three, jnp.bfloat16),
            array(three, jnp.bfloat16, three),
            array(three, jnp.float32),
            losses,
        ),
    )
    last_a, last_b, part = lax.optimization_barrier((last_a, last_b, part))
    last = pack(last_a, last_b)
    last_received = swap(last)
    near_weights, middle_part, middle_loss = tile_call(
        middle_tile_kernel,
        "tile_middle",
        pair * wide,
        scalars,
        (img, near_txt, part, near_weights),
        (array(three, jnp.bfloat16, wide), array(pair, jnp.float32), losses),
    )
    last_weights, img_part, img_tail, near_tail, far_tail, last_tail, img_part_tail, last_loss = tile_call(
        last_tile_kernel,
        "tile_last",
        three * pair + pair * 2 * wide,
        scalars,
        (last, last_received, far, far_received, near_txt, far_txt, img, part, middle_part),
        (
            array(three, jnp.bfloat16, pair),
            array(three, jnp.float32),
            low_piece,
            array(pair, jnp.bfloat16, wide),
            array(pair, jnp.bfloat16, three),
            array(pair, jnp.bfloat16, pair),
            array(pair, jnp.float32),
            losses,
        ),
        (low_piece,),
    )
    loss = near_loss + middle_loss + far_loss + last_loss

    def text_sums(weights, tail):
        return transposed_product(weights, img) + transposed_product(tail, img_tail)

    loss = loss + swap(loss, 0, 1)
    opposite_part = text_sums(last_weights, last_tail)
    sent = encode(jnp.where(on_first, img_part_tail, opposite_part), ONE_CHIP)
    sent, far_weights, far_tail, loss = lax.optimization_barrier((sent, far_weights, far_tail, loss))
    tail_received = swap(sent)
    far_part = text_sums(far_weights, far_tail)
    sent = encode(jnp.where(on_first, img_part, far_part), ONE_CHIP)
    loss = loss + swap(loss, 8, 1)
    tail_received, sent, loss = lax.optimization_barrier((tail_received, sent, loss))

    a, b = small_call(
        opposite_kernel, "opposite", core, (opposite_part, img_part_tail, tail_received), (low_half, low_half)
    )
    a, b, sent, near_weights, near_tail = lax.optimization_barrier((a, b, sent, near_weights, near_tail))
    from_a, from_b = move(a, "a"), move(b, "b")
    rest_received = swap(sent)
    near_part = text_sums(near_weights, near_tail)
    sent = encode(near_part, ONE_CHIP)
    loss = loss + swap(loss, 0, 2)
    (second,) = small_call(
        second_kernel, "second", core, (far_part, rest_received), (low_piece,)
    )
    from_a, from_b, second, sent, loss = lax.optimization_barrier((from_a, from_b, second, sent, loss))

    second_received = move(second, "a")
    x, b = small_call(
        far_kernel,
        "far",
        core,
        (far_part, rest_received, img_part, img_part_tail, tail_received, from_a, from_b),
        (low_piece,) * 2,
    )
    x, b, sent = lax.optimization_barrier((x, b, sent))
    from_x, from_b = move(x, "x"), move(b, "b")
    near_received = swap(sent)
    (base,) = small_call(
        base_kernel, "base", core, (near_part, near_received, img_part, rest_received), (array(wide, jnp.float32),)
    )
    base, loss = lax.optimization_barrier((base, loss))
    loss = loss + swap(loss, 0, 6)

    def near_slot(k, received):
        (out,) = small_call(
            lambda *refs: near_kernel(k, *refs), "near", core, (base, received), (low_piece,)
        )
        return out

    from_b, from_x, from_a = (
        move(near_slot(3, second_received), "b"),
        move(near_slot(1, from_b), "x"),
        move(near_slot(2, from_x), "a"),
    )
    loss = loss + swap(loss, 2, 0)
    loss = loss + swap(loss, 6, 0)
    keep, give = small_call(
        gather_sums_kernel,
        "gather_sums",
        core,
        (base, from_a, from_b, from_x, loss),
        (array(own, jnp.float32), array(own + 8, jnp.float32)),
    )
    grad = array(own, jnp.float32)
    loss_value, grad_image, grad_text = small_call(
        lambda *refs: finish_kernel(batch, *refs),
        "finish",
        core,
        (image_embed, text_embed, keep, swap(give), loss),
        (array(1, jnp.float32, 1), grad, grad),
    )
    return (loss_value.reshape(()), grad_image, grad_text)


def solution(mesh):
    in_specs = (P(("row", "col"), None), P(("row", "col"), None), P(), P())
    out_specs = (P(), P(("row", "col"), None), P(("row", "col"), None))
    return jax.shard_map(body, mesh=mesh, in_specs=in_specs, out_specs=out_specs, check_vma=False)
```

```python
import jax
import jax.numpy as jnp
from jax import lax
from jax.experimental import pallas as pl
from jax.experimental.pallas import tpu as pltpu
from jax.sharding import PartitionSpec as P

VMEM = pl.BlockSpec(memory_space=pltpu.VMEM)
SMEM = pl.BlockSpec(memory_space=pltpu.SMEM)
HBM = pl.BlockSpec(memory_space=pltpu.HBM)
MIB = 1024 * 1024
TINY = 1.1754944e-38
AXES = ("row", "col")
ROWS, COLS = 16, 8
ONE_CHIP, TWO_CHIPS, FOUR_CHIPS = 0.5, 0.25, 0.125
PARTNERS = {"x": ((0, 1), (8, 1)), "a": ((0, 2), (2, 0)), "b": ((0, 6), (6, 0))}


def exchange(x, bits_of_core):
    pairs = []
    for row in range(ROWS):
        for col in range(COLS):
            row_bits, col_bits = bits_of_core[row & 1]
            pairs.append((row * COLS + col, (row ^ row_bits) * COLS + (col ^ col_bits)))
    return lax.ppermute(x, AXES, pairs)


def move(x, step):
    return exchange(x, PARTNERS[step])


def swap(x, row_bits=1, col_bits=0):
    return exchange(x, ((row_bits, col_bits),) * 2)


def encode(x, shift):
    y = x * shift
    y2 = y * y
    y4 = y2 * y2
    return (y4 * y2 * (y * jnp.abs(y))).astype(jnp.bfloat16)


def decode(e, shift):
    f = e.astype(jnp.float32)
    size = jnp.exp2(jnp.log2(jnp.maximum(jnp.abs(f), TINY)) * 0.125)
    return jnp.where(f < 0.0, -size, size) * (1.0 / shift)


def row_scale(raw):
    return lax.rsqrt(jnp.sum(raw * raw, axis=1, keepdims=True) + 1e-06)


def by_core(core_ref, work):
    pl.when(core_ref[0] == 0)(lambda: work(True))
    pl.when(core_ref[0] != 0)(lambda: work(False))


def normalize_kernel(core_ref, img_ref, txt_ref, keep_ref, give_ref, raw_ref, sems):
    copies = [
        pltpu.make_async_copy(source, raw_ref.at[k], sems.at[k])
        for k, source in enumerate((txt_ref, img_ref))
    ]
    for copy in copies:
        copy.start()

    def low(k):
        raw = raw_ref[k]
        return (raw * row_scale(raw)).astype(jnp.bfloat16)

    for k, copy in enumerate(copies):
        copy.wait()

        def work(is_first, k=k):
            ref = keep_ref if (k == 0) == is_first else give_ref
            ref[...] = low(k)

        by_core(core_ref, work)


def normalize(core, img, txt):
    low = jax.ShapeDtypeStruct(img.shape, jnp.bfloat16)
    return pl.pallas_call(
        normalize_kernel,
        out_shape=(low, low),
        in_specs=[SMEM, HBM, HBM],
        out_specs=(VMEM, VMEM),
        scratch_shapes=[pltpu.VMEM((2, *img.shape), jnp.float32), pltpu.SemaphoreType.DMA((2,))],
        compiler_params=pltpu.CompilerParams(vmem_limit_bytes=6 * MIB),
        name="normalize",
    )(core, img, txt)


def pack_kernel(*refs):
    out_ref = refs[-1]
    start = 0
    for ref in refs[:-1]:
        out_ref[start : start + ref.shape[0]] = ref[...]
        start += ref.shape[0]


def pack(*pieces):
    shape = (sum(p.shape[0] for p in pieces), pieces[0].shape[1])
    return pl.pallas_call(
        pack_kernel,
        out_shape=jax.ShapeDtypeStruct(shape, pieces[0].dtype),
        in_specs=[VMEM] * len(pieces),
        out_specs=VMEM,
        compiler_params=pltpu.CompilerParams(vmem_limit_bytes=8 * MIB),
        name="pack",
    )(*pieces)


def half_kernel(k, in_ref, out_ref):
    rows = out_ref.shape[0]
    out_ref[...] = in_ref[k * rows : (k + 1) * rows]


def half_of(x, k):
    return pl.pallas_call(
        lambda *refs: half_kernel(k, *refs),
        out_shape=jax.ShapeDtypeStruct((x.shape[0] // 2, x.shape[1]), x.dtype),
        in_specs=[VMEM],
        out_specs=VMEM,
        compiler_params=pltpu.CompilerParams(vmem_limit_bytes=4 * MIB),
        name="half_of",
    )(x)


def run_tiles(pair, sharp_ref, bias_ref, jobs):
    sharp_scalar = jnp.max(sharp_ref[...])
    bias = jnp.max(bias_ref[...])
    steps = [(job, k) for job in jobs for k in range(len(job[1]))]

    def products(step):
        job, k = step
        return lax.dot_general(
            job[0][...], job[1][k][0][...], (((1,), (1,)), ((), ())), preferred_element_type=jnp.float32
        )

    loss = jnp.zeros((8, 128), jnp.float32)
    following = products(steps[0])
    for i, (job, k) in enumerate(steps):
        current = following
        if i + 1 < len(steps):
            following = products(steps[i + 1])
        _, blocks, before, out, corner = job
        texts, weights_out = blocks[k]
        rows, cols = current.shape
        sharp = jnp.exp(jnp.full((1, cols), sharp_scalar, jnp.float32))
        logits = current * sharp + bias
        grown = jnp.exp(logits)
        one_more = 1.0 + grown
        weights = sharp * (grown / one_more)
        weights_out[...] = weights.astype(jnp.bfloat16)
        logs = jnp.log(one_more[: rows // 2] * one_more[rows // 2 :])
        logs = jnp.sum(logs.reshape(rows // 16, 8, cols), axis=0)
        if corner is not None:
            row_ids = lax.broadcasted_iota(jnp.int32, (pair, pair), 0)
            col_ids = lax.broadcasted_iota(jnp.int32, (pair, pair), 1)
            wanted = jnp.where(row_ids < pair // 2, row_ids + pair // 2, row_ids - pair // 2)
            same = (wanted == col_ids) & (corner == 0)
            own = weights[:pair, :pair] - jnp.where(same, sharp[:, :pair], 0.0)
            weights_out[:pair, :pair] = own.astype(jnp.bfloat16)
            matched = jnp.where(same, logits[:pair, :pair], 0.0)
            matched = jnp.sum(matched.reshape(pair // 8, 8, pair), axis=0)
            for start in range(0, pair, 128):
                loss = loss - matched[:, start : start + 128]
        for start in range(0, cols, 128):
            loss = loss + logs[:, start : start + 128]
        part = jnp.dot(weights_out[...], texts[...], preferred_element_type=jnp.float32)
        if k == 0:
            total = part if before is None else part + before[...]
        else:
            total = total + part
        if k == len(blocks) - 1:
            out[...] = total
    return loss


def row_blocks(ref, size, rows=None):
    return [ref.at[pl.ds(start, size)] for start in range(0, rows or ref.shape[0], size)]


def near_tile_kernel(core_ref, sharp_ref, bias_ref, near_ref, received_ref, img_ref, txt_ref, weights_ref, part_ref, loss_ref):
    count = img_ref.shape[0]
    pair = count // 2

    def work(is_first):
        txt_ref[...] = near_ref[...] if is_first else received_ref[...]
        img_ref[...] = received_ref[:count] if is_first else near_ref[count:]

    by_core(core_ref, work)
    jobs = []
    for k, rows in enumerate(row_blocks(img_ref, pair)):
        span = pl.ds(k * pair, pair)
        corner = core_ref[0] if k == 0 else None
        jobs.append((rows, [(txt_ref, weights_ref.at[span])], None, part_ref.at[span], corner))
    loss_ref[...] = run_tiles(pair, sharp_ref, bias_ref, jobs)


def far_tile_kernel(
    core_ref, sharp_ref, bias_ref, far_ref, received_ref, near_img_ref, near_before_ref,
    txt_ref, img_ref, weights_ref, part_ref, loss_ref,
):
    count = near_img_ref.shape[0]
    pair = count // 2

    def work(is_first):
        txt_ref[...] = far_ref[...] if is_first else received_ref[...]
        img_ref[count:] = received_ref[:pair] if is_first else far_ref[count:]

    by_core(core_ref, work)
    img_ref[:count] = near_img_ref[...]
    jobs = []
    before = row_blocks(near_before_ref, pair) + [None]
    for k, rows in enumerate(row_blocks(img_ref, pair)):
        span = pl.ds(k * pair, pair)
        jobs.append((rows, [(txt_ref, weights_ref.at[span])], before[k], part_ref.at[span], None))
    loss_ref[...] = run_tiles(pair, sharp_ref, bias_ref, jobs)


def middle_tile_kernel(
    core_ref, sharp_ref, bias_ref, img_ref, txt_ref, before_ref, near_weights_ref, weights_ref, part_ref, loss_ref
):
    pair = part_ref.shape[0]
    span = pl.ds(2 * pair, pair)
    weights_ref[: 2 * pair] = near_weights_ref[...]
    job = (img_ref.at[span], [(txt_ref, weights_ref.at[span])], before_ref.at[span], part_ref, None)
    loss_ref[...] = run_tiles(pair, sharp_ref, bias_ref, [job])


def last_tile_kernel(
    core_ref, sharp_ref, bias_ref, last_ref, received_ref, far_ref, far_received_ref, near_txt_ref, far_txt_ref,
    img_ref, before_ref, middle_before_ref,
    weights_ref, part_ref, img_tail_ref, near_tail_ref, far_tail_ref, last_tail_ref, part_tail_ref, loss_ref, txt_ref,
):
    pair = last_ref.shape[0]
    half = pair // 2

    def work(is_first):
        txt_ref[...] = last_ref[...] if is_first else received_ref[...]
        img_tail_ref[:half] = far_received_ref[pair : pair + half] if is_first else far_ref[pair + half : 2 * pair]
        img_tail_ref[half:] = received_ref[:half] if is_first else last_ref[half:]

    by_core(core_ref, work)
    jobs = []
    before = row_blocks(before_ref, pair, 2 * pair) + [middle_before_ref]
    for k, rows in enumerate(row_blocks(img_ref, pair)):
        span = pl.ds(k * pair, pair)
        jobs.append((rows, [(txt_ref, weights_ref.at[span])], before[k], part_ref.at[span], None))
    blocks = [(near_txt_ref, near_tail_ref), (far_txt_ref, far_tail_ref), (txt_ref, last_tail_ref)]
    jobs.append((img_tail_ref, blocks, None, part_tail_ref, None))
    loss_ref[...] = run_tiles(pair, sharp_ref, bias_ref, jobs)


def tile_call(kernel, name, pairs, scalars, arrays, outs, scratch=()):
    features = arrays[0].shape[1]
    return pl.pallas_call(
        kernel,
        out_shape=outs,
        in_specs=[SMEM] + [VMEM] * (len(scalars) - 1 + len(arrays)),
        out_specs=(VMEM,) * len(outs),
        scratch_shapes=[pltpu.VMEM(x.shape, x.dtype) for x in scratch],
        compiler_params=pltpu.CompilerParams(vmem_limit_bytes=16 * MIB),
        cost_estimate=pl.CostEstimate(
            flops=4 * pairs * features,
            bytes_accessed=sum(2 * x.size for x in arrays),
            transcendentals=3 * pairs,
        ),
        name=name,
    )(*scalars, *arrays)


def small_call(kernel, name, core, arrays, outs):
    size = sum(x.size * x.dtype.itemsize for x in (*arrays, *outs))
    return pl.pallas_call(
        kernel,
        out_shape=outs,
        in_specs=[SMEM] + [VMEM] * len(arrays),
        out_specs=(VMEM,) * len(outs),
        compiler_params=pltpu.CompilerParams(vmem_limit_bytes=size + 4 * MIB),
        name=name,
    )(core, *arrays)


CHUNK = 64


def each_chunk(rows, work):
    def step(i, carry):
        first = pl.multiple_of(i * CHUNK, CHUNK)
        work(lambda start=0: pl.ds(start + first, CHUNK))
        return carry

    lax.fori_loop(0, rows // CHUNK, step, 0)


def opposite_kernel(core_ref, txt_ref, img_ref, received_ref, a_ref, b_ref):
    half = a_ref.shape[0]

    def work(is_first):
        def texts(at):
            a_ref[at()] = encode(txt_ref[at()] + decode(received_ref[at()], ONE_CHIP), ONE_CHIP)
            b_ref[at()] = encode(txt_ref[at(half)] + decode(received_ref[at(half)], ONE_CHIP), ONE_CHIP)

        def images(at):
            a_ref[at()] = received_ref[at(half)]
            b_ref[at()] = encode(img_ref[at(half)], ONE_CHIP)

        each_chunk(half, texts if is_first else images)

    by_core(core_ref, work)


def second_kernel(core_ref, txt_ref, received_ref, out_ref):
    pair = out_ref.shape[0]

    def work(is_first):
        def rows(at):
            if is_first:
                value = txt_ref[at()] + decode(received_ref[at()], ONE_CHIP)
            else:
                value = decode(received_ref[at(2 * pair)], ONE_CHIP)
            out_ref[at()] = encode(value, TWO_CHIPS)

        each_chunk(pair, rows)

    by_core(core_ref, work)


def far_kernel(
    core_ref, txt_ref, txt_received_ref, img_ref, img_tail_ref, tail_received_ref, from_a_ref, from_b_ref, x_ref, b_ref
):
    pair = x_ref.shape[0]
    half = pair // 2

    def work(is_first):
        def rows(at):
            def base(i):
                if is_first:
                    return txt_ref[at(i * half)] + decode(txt_received_ref[at(i * half)], ONE_CHIP)
                if i == 2:
                    return decode(tail_received_ref[at()], ONE_CHIP)
                return img_tail_ref[at()] if i == 3 else img_ref[at(i * half)]

            x_ref[at()] = encode(base(2), TWO_CHIPS)
            x_ref[at(half)] = encode(base(3) + decode(from_b_ref[at()], ONE_CHIP), TWO_CHIPS)
            b_ref[at()] = encode(base(4) + decode(from_a_ref[at()], ONE_CHIP), TWO_CHIPS)
            b_ref[at(half)] = encode(base(5), TWO_CHIPS)

        each_chunk(half, rows)

    by_core(core_ref, work)


def base_kernel(core_ref, txt_ref, received_ref, img_ref, img_received_ref, out_ref):
    count = out_ref.shape[0]
    two = count // 2

    def work(is_first):
        def texts(at):
            out_ref[at()] = txt_ref[at()] + decode(received_ref[at()], ONE_CHIP)

        def images(at):
            out_ref[at()] = decode(img_received_ref[at()], ONE_CHIP)

        if is_first:
            each_chunk(count, texts)
        else:
            each_chunk(two, images)
            out_ref[two:] = img_ref[:two]

    by_core(core_ref, work)


def near_kernel(k, core_ref, base_ref, received_ref, out_ref):
    pair = out_ref.shape[0]

    def rows(at):
        value = base_ref[at(k * pair)] + decode(received_ref[at()], TWO_CHIPS)
        out_ref[at()] = encode(value, FOUR_CHIPS)

    each_chunk(pair, rows)


def gather_sums_kernel(core_ref, base_ref, a_ref, b_ref, x_ref, loss_ref, keep_ref, give_ref):
    own = keep_ref.shape[0]
    give_ref[own:] = jnp.zeros((8, give_ref.shape[1]), jnp.float32)
    give_ref[own:, :128] = loss_ref[...]

    def rows(at):
        for start, ref in ((0, keep_ref), (own, give_ref)):
            total = base_ref[at(start)] + decode(x_ref[at(start)], FOUR_CHIPS)
            total = total + decode(a_ref[at(start)], FOUR_CHIPS)
            ref[at()] = total + decode(b_ref[at(start)], FOUR_CHIPS)

    each_chunk(own, rows)


def finish_kernel(batch, core_ref, img_ref, txt_ref, kept_ref, received_ref, loss_parts_ref, loss_ref, grad_img_ref, grad_txt_ref):
    own = kept_ref.shape[0]
    both = loss_parts_ref[...] + received_ref[own:, :128]
    loss_ref[...] = jnp.full((1, 1), jnp.sum(both) * (1.0 / batch), jnp.float32)

    def side(at, raw_ref, sum_ref, grad_ref):
        raw = raw_ref[at()]
        scale = row_scale(raw)
        unit = raw * scale
        summed = sum_ref[at()]
        grad_ref[at()] = (summed - unit * jnp.sum(unit * summed, axis=1, keepdims=True)) * scale

    def work(is_first):
        def rows(at):
            side(at, img_ref, received_ref if is_first else kept_ref, grad_img_ref)
            side(at, txt_ref, kept_ref if is_first else received_ref, grad_txt_ref)

        each_chunk(own, rows)

    by_core(core_ref, work)


def transposed_product(weights, img):
    return lax.dot_general(
        weights, img, (((0,), (0,)), ((), ())), preferred_element_type=jnp.float32
    )


def body(image_embed, text_embed, exponent_of_sharpness, bias):
    own, features = image_embed.shape
    pair = 2 * own
    batch = own * ROWS * COLS
    core = lax.axis_index("row") & 1
    core, on_first = lax.optimization_barrier((core.reshape(1), core == 0))

    def array(rows, dtype, columns=features):
        return jax.ShapeDtypeStruct((rows, columns), dtype)

    low_half, low_piece = array(own, jnp.bfloat16), array(pair, jnp.bfloat16)

    keep, give = normalize(core, image_embed, text_embed)
    low = pack(keep, swap(give))
    slot_x, slot_1, slot_3 = move(low, "x"), move(low, "a"), move(low, "b")
    slot_2, slot_x3, slot_x1 = move(slot_3, "a"), move(slot_x, "b"), move(slot_1, "x")
    near = pack(low, slot_x, slot_1, slot_3)
    near_received = swap(near)
    sharpness = jnp.broadcast_to(exponent_of_sharpness.reshape(1, 1), (8, 128))
    shift = jnp.broadcast_to(bias.reshape(1, 1), (8, 128))

    scalars = (core, sharpness, shift)
    losses = array(8, jnp.float32, 128)
    wide, three, two = 4 * pair, 3 * pair, 2 * pair
    near_img, near_txt, near_weights, near_part, near_loss = tile_call(
        near_tile_kernel,
        "tile_near",
        two * wide,
        scalars,
        (near, near_received),
        (
            array(two, jnp.bfloat16),
            array(wide, jnp.bfloat16),
            array(two, jnp.bfloat16, wide),
            array(two, jnp.float32),
            losses,
        ),
    )
    slot_2, slot_x3, slot_x1, near_part = lax.optimization_barrier((slot_2, slot_x3, slot_x1, near_part))
    last_a = move(half_of(slot_x3, 0), "a")
    last_b = move(half_of(slot_x1, 1), "b")
    far = pack(slot_2, slot_x1, slot_x3)
    far_received = swap(far)
    far_txt, img, far_weights, part, far_loss = tile_call(
        far_tile_kernel,
        "tile_far",
        three * three,
        scalars,
        (far, far_received, near_img, near_part),
        (
            array(three, jnp.bfloat16),
            array(three, jnp.bfloat16),
            array(three, jnp.bfloat16, three),
            array(three, jnp.float32),
            losses,
        ),
    )
    last_a, last_b, part = lax.optimization_barrier((last_a, last_b, part))
    last = pack(last_a, last_b)
    last_received = swap(last)
    near_weights, middle_part, middle_loss = tile_call(
        middle_tile_kernel,
        "tile_middle",
        pair * wide,
        scalars,
        (img, near_txt, part, near_weights),
        (array(three, jnp.bfloat16, wide), array(pair, jnp.float32), losses),
    )
    last_weights, img_part, img_tail, near_tail, far_tail, last_tail, img_part_tail, last_loss = tile_call(
        last_tile_kernel,
        "tile_last",
        three * pair + pair * 2 * wide,
        scalars,
        (last, last_received, far, far_received, near_txt, far_txt, img, part, middle_part),
        (
            array(three, jnp.bfloat16, pair),
            array(three, jnp.float32),
            low_piece,
            array(pair, jnp.bfloat16, wide),
            array(pair, jnp.bfloat16, three),
            array(pair, jnp.bfloat16, pair),
            array(pair, jnp.float32),
            losses,
        ),
        (low_piece,),
    )
    loss = near_loss + middle_loss + far_loss + last_loss

    def text_sums(weights, tail):
        return transposed_product(weights, img) + transposed_product(tail, img_tail)

    loss = loss + swap(loss, 0, 1)
    opposite_part = text_sums(last_weights, last_tail)
    sent = encode(jnp.where(on_first, img_part_tail, opposite_part), ONE_CHIP)
    sent, far_weights, far_tail = lax.optimization_barrier((sent, far_weights, far_tail))
    tail_received = swap(sent)
    far_part = text_sums(far_weights, far_tail)
    sent = encode(jnp.where(on_first, img_part, far_part), ONE_CHIP)
    tail_received, sent, loss = lax.optimization_barrier((tail_received, sent, loss))

    a, b = small_call(
        opposite_kernel, "opposite", core, (opposite_part, img_part_tail, tail_received), (low_half, low_half)
    )
    a, b, sent, near_weights, near_tail = lax.optimization_barrier((a, b, sent, near_weights, near_tail))
    from_a, from_b = move(a, "a"), move(b, "b")
    rest_received = swap(sent)
    near_part = text_sums(near_weights, near_tail)
    sent = encode(near_part, ONE_CHIP)
    loss = loss + swap(loss, 8, 1)
    loss = loss + swap(loss, 0, 2)
    (second,) = small_call(
        second_kernel, "second", core, (far_part, rest_received), (low_piece,)
    )
    from_a, from_b, second, sent, loss = lax.optimization_barrier((from_a, from_b, second, sent, loss))

    second_received = move(second, "a")
    x, b = small_call(
        far_kernel,
        "far",
        core,
        (far_part, rest_received, img_part, img_part_tail, tail_received, from_a, from_b),
        (low_piece,) * 2,
    )
    x, b, sent = lax.optimization_barrier((x, b, sent))
    from_x, from_b = move(x, "x"), move(b, "b")
    near_received = swap(sent)
    (base,) = small_call(
        base_kernel, "base", core, (near_part, near_received, img_part, rest_received), (array(wide, jnp.float32),)
    )
    base, loss = lax.optimization_barrier((base, loss))
    loss = loss + swap(loss, 0, 6)
    base, loss = lax.optimization_barrier((base, loss))

    def near_slot(k, received):
        (out,) = small_call(
            lambda *refs: near_kernel(k, *refs), "near", core, (base, received), (low_piece,)
        )
        return out

    from_b, from_x, from_a = (
        move(near_slot(3, second_received), "b"),
        move(near_slot(1, from_b), "x"),
        move(near_slot(2, from_x), "a"),
    )
    loss = loss + swap(loss, 2, 0)
    loss = loss + swap(loss, 6, 0)
    keep, give = small_call(
        gather_sums_kernel,
        "gather_sums",
        core,
        (base, from_a, from_b, from_x, loss),
        (array(own, jnp.float32), array(own + 8, jnp.float32)),
    )
    grad = array(own, jnp.float32)
    loss_value, grad_image, grad_text = small_call(
        lambda *refs: finish_kernel(batch, *refs),
        "finish",
        core,
        (image_embed, text_embed, keep, swap(give), loss),
        (array(1, jnp.float32, 1), grad, grad),
    )
    return (loss_value.reshape(()), grad_image, grad_text)


def solution(mesh):
    in_specs = (P(("row", "col"), None), P(("row", "col"), None), P(), P())
    out_specs = (P(), P(("row", "col"), None), P(("row", "col"), None))
    return jax.shard_map(body, mesh=mesh, in_specs=in_specs, out_specs=out_specs, check_vma=False)
```

```python
import jax
import jax.numpy as jnp
from jax import lax
from jax.experimental import pallas as pl
from jax.experimental.pallas import tpu as pltpu
from jax.sharding import PartitionSpec as P

VMEM = pl.BlockSpec(memory_space=pltpu.VMEM)
SMEM = pl.BlockSpec(memory_space=pltpu.SMEM)
HBM = pl.BlockSpec(memory_space=pltpu.HBM)
MIB = 1024 * 1024
TINY = 1.1754944e-38
AXES = ("row", "col")
ROWS, COLS = 16, 8
ONE_CHIP, TWO_CHIPS, FOUR_CHIPS = 0.5, 0.25, 0.125
PARTNERS = {"x": ((0, 1), (8, 1)), "a": ((0, 2), (2, 0)), "b": ((0, 6), (6, 0))}


def exchange(x, bits_of_core):
    pairs = []
    for row in range(ROWS):
        for col in range(COLS):
            row_bits, col_bits = bits_of_core[row & 1]
            pairs.append((row * COLS + col, (row ^ row_bits) * COLS + (col ^ col_bits)))
    return lax.ppermute(x, AXES, pairs)


def move(x, step):
    return exchange(x, PARTNERS[step])


def swap(x, row_bits=1, col_bits=0):
    return exchange(x, ((row_bits, col_bits),) * 2)


def encode(x, shift):
    y = x * shift
    y2 = y * y
    y4 = y2 * y2
    return (y4 * y2 * (y * jnp.abs(y))).astype(jnp.bfloat16)


def decode(e, shift):
    f = e.astype(jnp.float32)
    size = jnp.exp2(jnp.log2(jnp.maximum(jnp.abs(f), TINY)) * 0.125)
    return jnp.where(f < 0.0, -size, size) * (1.0 / shift)


def row_scale(raw):
    return lax.rsqrt(jnp.sum(raw * raw, axis=1, keepdims=True) + 1e-06)


def by_core(core_ref, work):
    pl.when(core_ref[0] == 0)(lambda: work(True))
    pl.when(core_ref[0] != 0)(lambda: work(False))


def normalize_kernel(core_ref, img_ref, txt_ref, keep_ref, give_ref, raw_ref, sems):
    copies = [
        pltpu.make_async_copy(source, raw_ref.at[k], sems.at[k])
        for k, source in enumerate((txt_ref, img_ref))
    ]
    for copy in copies:
        copy.start()

    def low(k):
        raw = raw_ref[k]
        return (raw * row_scale(raw)).astype(jnp.bfloat16)

    for k, copy in enumerate(copies):
        copy.wait()

        def work(is_first, k=k):
            ref = keep_ref if (k == 0) == is_first else give_ref
            ref[...] = low(k)

        by_core(core_ref, work)


def normalize(core, img, txt):
    low = jax.ShapeDtypeStruct(img.shape, jnp.bfloat16)
    return pl.pallas_call(
        normalize_kernel,
        out_shape=(low, low),
        in_specs=[SMEM, HBM, HBM],
        out_specs=(VMEM, VMEM),
        scratch_shapes=[pltpu.VMEM((2, *img.shape), jnp.float32), pltpu.SemaphoreType.DMA((2,))],
        compiler_params=pltpu.CompilerParams(vmem_limit_bytes=6 * MIB),
        name="normalize",
    )(core, img, txt)


def pack_kernel(*refs):
    out_ref = refs[-1]
    start = 0
    for ref in refs[:-1]:
        out_ref[start : start + ref.shape[0]] = ref[...]
        start += ref.shape[0]


def pack(*pieces):
    shape = (sum(p.shape[0] for p in pieces), pieces[0].shape[1])
    return pl.pallas_call(
        pack_kernel,
        out_shape=jax.ShapeDtypeStruct(shape, pieces[0].dtype),
        in_specs=[VMEM] * len(pieces),
        out_specs=VMEM,
        compiler_params=pltpu.CompilerParams(vmem_limit_bytes=8 * MIB),
        name="pack",
    )(*pieces)


def half_kernel(k, in_ref, out_ref):
    rows = out_ref.shape[0]
    out_ref[...] = in_ref[k * rows : (k + 1) * rows]


def half_of(x, k):
    return pl.pallas_call(
        lambda *refs: half_kernel(k, *refs),
        out_shape=jax.ShapeDtypeStruct((x.shape[0] // 2, x.shape[1]), x.dtype),
        in_specs=[VMEM],
        out_specs=VMEM,
        compiler_params=pltpu.CompilerParams(vmem_limit_bytes=4 * MIB),
        name="half_of",
    )(x)


def run_tiles(pair, sharp_ref, bias_ref, jobs):
    sharp_scalar = jnp.max(sharp_ref[...])
    bias = jnp.max(bias_ref[...])
    steps = [(job, k) for job in jobs for k in range(len(job[1]))]

    def products(step):
        job, k = step
        return lax.dot_general(
            job[0][...], job[1][k][0][...], (((1,), (1,)), ((), ())), preferred_element_type=jnp.float32
        )

    loss = jnp.zeros((8, 128), jnp.float32)
    following = products(steps[0])
    for i, (job, k) in enumerate(steps):
        current = following
        if i + 1 < len(steps):
            following = products(steps[i + 1])
        _, blocks, before, out, corner = job
        texts, weights_out = blocks[k]
        rows, cols = current.shape
        sharp = jnp.exp(jnp.full((1, cols), sharp_scalar, jnp.float32))
        logits = current * sharp + bias
        grown = jnp.exp(logits)
        one_more = 1.0 + grown
        weights = sharp * (grown / one_more)
        weights_out[...] = weights.astype(jnp.bfloat16)
        logs = jnp.log(one_more[: rows // 2] * one_more[rows // 2 :])
        logs = jnp.sum(logs.reshape(rows // 16, 8, cols), axis=0)
        if corner is not None:
            row_ids = lax.broadcasted_iota(jnp.int32, (pair, pair), 0)
            col_ids = lax.broadcasted_iota(jnp.int32, (pair, pair), 1)
            wanted = jnp.where(row_ids < pair // 2, row_ids + pair // 2, row_ids - pair // 2)
            same = (wanted == col_ids) & (corner == 0)
            own = weights[:pair, :pair] - jnp.where(same, sharp[:, :pair], 0.0)
            weights_out[:pair, :pair] = own.astype(jnp.bfloat16)
            matched = jnp.where(same, logits[:pair, :pair], 0.0)
            matched = jnp.sum(matched.reshape(pair // 8, 8, pair), axis=0)
            for start in range(0, pair, 128):
                loss = loss - matched[:, start : start + 128]
        for start in range(0, cols, 128):
            loss = loss + logs[:, start : start + 128]
        part = jnp.dot(weights_out[...], texts[...], preferred_element_type=jnp.float32)
        if k == 0:
            total = part if before is None else part + before[...]
        else:
            total = total + part
        if k == len(blocks) - 1:
            out[...] = total
    return loss


def row_blocks(ref, size, rows=None):
    return [ref.at[pl.ds(start, size)] for start in range(0, rows or ref.shape[0], size)]


def near_tile_kernel(core_ref, sharp_ref, bias_ref, near_ref, received_ref, img_ref, txt_ref, weights_ref, part_ref, loss_ref):
    count = img_ref.shape[0]
    pair = count // 2

    def work(is_first):
        txt_ref[...] = near_ref[...] if is_first else received_ref[...]
        img_ref[...] = received_ref[:count] if is_first else near_ref[count:]

    by_core(core_ref, work)
    jobs = []
    for k, rows in enumerate(row_blocks(img_ref, pair)):
        span = pl.ds(k * pair, pair)
        corner = core_ref[0] if k == 0 else None
        jobs.append((rows, [(txt_ref, weights_ref.at[span])], None, part_ref.at[span], corner))
    loss_ref[...] = run_tiles(pair, sharp_ref, bias_ref, jobs)


def far_tile_kernel(
    core_ref, sharp_ref, bias_ref, far_ref, received_ref, near_img_ref, near_before_ref,
    txt_ref, img_ref, weights_ref, part_ref, loss_ref,
):
    count = near_img_ref.shape[0]
    pair = count // 2

    def work(is_first):
        txt_ref[...] = far_ref[...] if is_first else received_ref[...]
        img_ref[count:] = received_ref[:pair] if is_first else far_ref[count:]

    by_core(core_ref, work)
    img_ref[:count] = near_img_ref[...]
    jobs = []
    before = row_blocks(near_before_ref, pair) + [None]
    for k, rows in enumerate(row_blocks(img_ref, pair)):
        span = pl.ds(k * pair, pair)
        jobs.append((rows, [(txt_ref, weights_ref.at[span])], before[k], part_ref.at[span], None))
    loss_ref[...] = run_tiles(pair, sharp_ref, bias_ref, jobs)


def middle_tile_kernel(
    core_ref, sharp_ref, bias_ref, img_ref, txt_ref, before_ref, near_weights_ref, weights_ref, part_ref, loss_ref
):
    pair = part_ref.shape[0]
    span = pl.ds(2 * pair, pair)
    weights_ref[: 2 * pair] = near_weights_ref[...]
    job = (img_ref.at[span], [(txt_ref, weights_ref.at[span])], before_ref.at[span], part_ref, None)
    loss_ref[...] = run_tiles(pair, sharp_ref, bias_ref, [job])


def last_tile_kernel(
    core_ref, sharp_ref, bias_ref, last_ref, received_ref, far_ref, far_received_ref, near_txt_ref, far_txt_ref,
    img_ref, before_ref, middle_before_ref,
    weights_ref, part_ref, img_tail_ref, near_tail_ref, far_tail_ref, last_tail_ref, part_tail_ref, loss_ref, txt_ref,
):
    pair = last_ref.shape[0]
    half = pair // 2

    def work(is_first):
        txt_ref[...] = last_ref[...] if is_first else received_ref[...]
        img_tail_ref[:half] = far_received_ref[pair : pair + half] if is_first else far_ref[pair + half : 2 * pair]
        img_tail_ref[half:] = received_ref[:half] if is_first else last_ref[half:]

    by_core(core_ref, work)
    jobs = []
    before = row_blocks(before_ref, pair, 2 * pair) + [middle_before_ref]
    for k, rows in enumerate(row_blocks(img_ref, pair)):
        span = pl.ds(k * pair, pair)
        jobs.append((rows, [(txt_ref, weights_ref.at[span])], before[k], part_ref.at[span], None))
    blocks = [(near_txt_ref, near_tail_ref), (far_txt_ref, far_tail_ref), (txt_ref, last_tail_ref)]
    jobs.append((img_tail_ref, blocks, None, part_tail_ref, None))
    loss_ref[...] = run_tiles(pair, sharp_ref, bias_ref, jobs)


def tile_call(kernel, name, pairs, scalars, arrays, outs, scratch=()):
    features = arrays[0].shape[1]
    return pl.pallas_call(
        kernel,
        out_shape=outs,
        in_specs=[SMEM] + [VMEM] * (len(scalars) - 1 + len(arrays)),
        out_specs=(VMEM,) * len(outs),
        scratch_shapes=[pltpu.VMEM(x.shape, x.dtype) for x in scratch],
        compiler_params=pltpu.CompilerParams(vmem_limit_bytes=16 * MIB),
        cost_estimate=pl.CostEstimate(
            flops=4 * pairs * features,
            bytes_accessed=sum(2 * x.size for x in arrays),
            transcendentals=3 * pairs,
        ),
        name=name,
    )(*scalars, *arrays)


def small_call(kernel, name, core, arrays, outs):
    size = sum(x.size * x.dtype.itemsize for x in (*arrays, *outs))
    return pl.pallas_call(
        kernel,
        out_shape=outs,
        in_specs=[SMEM] + [VMEM] * len(arrays),
        out_specs=(VMEM,) * len(outs),
        compiler_params=pltpu.CompilerParams(vmem_limit_bytes=size + 4 * MIB),
        name=name,
    )(core, *arrays)


CHUNK = 64


def each_chunk(rows, work):
    def step(i, carry):
        first = pl.multiple_of(i * CHUNK, CHUNK)
        work(lambda start=0: pl.ds(start + first, CHUNK))
        return carry

    lax.fori_loop(0, rows // CHUNK, step, 0)


def opposite_kernel(core_ref, txt_ref, img_ref, received_ref, a_ref, b_ref):
    half = a_ref.shape[0]

    def work(is_first):
        def texts(at):
            a_ref[at()] = encode(txt_ref[at()] + decode(received_ref[at()], ONE_CHIP), ONE_CHIP)
            b_ref[at()] = encode(txt_ref[at(half)] + decode(received_ref[at(half)], ONE_CHIP), ONE_CHIP)

        def images(at):
            a_ref[at()] = received_ref[at(half)]
            b_ref[at()] = encode(img_ref[at(half)], ONE_CHIP)

        each_chunk(half, texts if is_first else images)

    by_core(core_ref, work)


def second_kernel(core_ref, txt_ref, received_ref, out_ref):
    pair = out_ref.shape[0]

    def work(is_first):
        def rows(at):
            if is_first:
                value = txt_ref[at()] + decode(received_ref[at()], ONE_CHIP)
            else:
                value = decode(received_ref[at(2 * pair)], ONE_CHIP)
            out_ref[at()] = encode(value, TWO_CHIPS)

        each_chunk(pair, rows)

    by_core(core_ref, work)


def far_kernel(
    core_ref, txt_ref, txt_received_ref, img_ref, img_tail_ref, tail_received_ref, from_a_ref, from_b_ref, x_ref, b_ref
):
    pair = x_ref.shape[0]
    half = pair // 2

    def work(is_first):
        def rows(at):
            def base(i):
                if is_first:
                    return txt_ref[at(i * half)] + decode(txt_received_ref[at(i * half)], ONE_CHIP)
                if i == 2:
                    return decode(tail_received_ref[at()], ONE_CHIP)
                return img_tail_ref[at()] if i == 3 else img_ref[at(i * half)]

            x_ref[at()] = encode(base(2), TWO_CHIPS)
            x_ref[at(half)] = encode(base(3) + decode(from_b_ref[at()], ONE_CHIP), TWO_CHIPS)
            b_ref[at()] = encode(base(4) + decode(from_a_ref[at()], ONE_CHIP), TWO_CHIPS)
            b_ref[at(half)] = encode(base(5), TWO_CHIPS)

        each_chunk(half, rows)

    by_core(core_ref, work)


def base_kernel(core_ref, txt_ref, received_ref, img_ref, img_received_ref, out_ref):
    count = out_ref.shape[0]
    two = count // 2

    def work(is_first):
        def texts(at):
            out_ref[at()] = txt_ref[at()] + decode(received_ref[at()], ONE_CHIP)

        def images(at):
            out_ref[at()] = decode(img_received_ref[at()], ONE_CHIP)

        if is_first:
            each_chunk(count, texts)
        else:
            each_chunk(two, images)
            out_ref[two:] = img_ref[:two]

    by_core(core_ref, work)


def near_kernel(k, core_ref, base_ref, received_ref, out_ref):
    pair = out_ref.shape[0]

    def rows(at):
        value = base_ref[at(k * pair)] + decode(received_ref[at()], TWO_CHIPS)
        out_ref[at()] = encode(value, FOUR_CHIPS)

    each_chunk(pair, rows)


def gather_sums_kernel(core_ref, base_ref, a_ref, b_ref, x_ref, loss_ref, keep_ref, give_ref):
    own = keep_ref.shape[0]
    give_ref[own:] = jnp.zeros((8, give_ref.shape[1]), jnp.float32)
    give_ref[own:, :128] = loss_ref[...]

    def rows(at):
        for start, ref in ((0, keep_ref), (own, give_ref)):
            total = base_ref[at(start)] + decode(x_ref[at(start)], FOUR_CHIPS)
            total = total + decode(a_ref[at(start)], FOUR_CHIPS)
            ref[at()] = total + decode(b_ref[at(start)], FOUR_CHIPS)

    each_chunk(own, rows)


def finish_kernel(batch, core_ref, img_ref, txt_ref, kept_ref, received_ref, loss_parts_ref, loss_ref, grad_img_ref, grad_txt_ref):
    own = kept_ref.shape[0]
    both = loss_parts_ref[...] + received_ref[own:, :128]
    loss_ref[...] = jnp.full((1, 1), jnp.sum(both) * (1.0 / batch), jnp.float32)

    def side(at, raw_ref, sum_ref, grad_ref):
        raw = raw_ref[at()]
        scale = row_scale(raw)
        unit = raw * scale
        summed = sum_ref[at()]
        grad_ref[at()] = (summed - unit * jnp.sum(unit * summed, axis=1, keepdims=True)) * scale

    def work(is_first):
        def rows(at):
            side(at, img_ref, received_ref if is_first else kept_ref, grad_img_ref)
            side(at, txt_ref, kept_ref if is_first else received_ref, grad_txt_ref)

        each_chunk(own, rows)

    by_core(core_ref, work)


def transposed_product(weights, img):
    return lax.dot_general(
        weights, img, (((0,), (0,)), ((), ())), preferred_element_type=jnp.float32
    )


def body(image_embed, text_embed, exponent_of_sharpness, bias):
    own, features = image_embed.shape
    pair = 2 * own
    batch = own * ROWS * COLS
    core = lax.axis_index("row") & 1
    core, on_first = lax.optimization_barrier((core.reshape(1), core == 0))

    def array(rows, dtype, columns=features):
        return jax.ShapeDtypeStruct((rows, columns), dtype)

    low_half, low_piece = array(own, jnp.bfloat16), array(pair, jnp.bfloat16)

    keep, give = normalize(core, image_embed, text_embed)
    low = pack(keep, swap(give))
    slot_x, slot_1, slot_3 = move(low, "x"), move(low, "a"), move(low, "b")
    slot_2, slot_x3, slot_x1 = move(slot_3, "a"), move(slot_x, "b"), move(slot_1, "x")
    near = pack(low, slot_x, slot_1, slot_3)
    near_received = swap(near)
    sharpness = jnp.broadcast_to(exponent_of_sharpness.reshape(1, 1), (8, 128))
    shift = jnp.broadcast_to(bias.reshape(1, 1), (8, 128))

    scalars = (core, sharpness, shift)
    losses = array(8, jnp.float32, 128)
    wide, three, two = 4 * pair, 3 * pair, 2 * pair
    near_img, near_txt, near_weights, near_part, near_loss = tile_call(
        near_tile_kernel,
        "tile_near",
        two * wide,
        scalars,
        (near, near_received),
        (
            array(two, jnp.bfloat16),
            array(wide, jnp.bfloat16),
            array(two, jnp.bfloat16, wide),
            array(two, jnp.float32),
            losses,
        ),
    )
    slot_2, slot_x3, slot_x1, near_part = lax.optimization_barrier((slot_2, slot_x3, slot_x1, near_part))
    last_a = move(half_of(slot_x3, 0), "a")
    last_b = move(half_of(slot_x1, 1), "b")
    far = pack(slot_2, slot_x1, slot_x3)
    far_received = swap(far)
    far_txt, img, far_weights, part, far_loss = tile_call(
        far_tile_kernel,
        "tile_far",
        three * three,
        scalars,
        (far, far_received, near_img, near_part),
        (
            array(three, jnp.bfloat16),
            array(three, jnp.bfloat16),
            array(three, jnp.bfloat16, three),
            array(three, jnp.float32),
            losses,
        ),
    )
    last_a, last_b, part = lax.optimization_barrier((last_a, last_b, part))
    last = pack(last_a, last_b)
    last_received = swap(last)
    near_weights, middle_part, middle_loss = tile_call(
        middle_tile_kernel,
        "tile_middle",
        pair * wide,
        scalars,
        (img, near_txt, part, near_weights),
        (array(three, jnp.bfloat16, wide), array(pair, jnp.float32), losses),
    )
    last_weights, img_part, img_tail, near_tail, far_tail, last_tail, img_part_tail, last_loss = tile_call(
        last_tile_kernel,
        "tile_last",
        three * pair + pair * 2 * wide,
        scalars,
        (last, last_received, far, far_received, near_txt, far_txt, img, part, middle_part),
        (
            array(three, jnp.bfloat16, pair),
            array(three, jnp.float32),
            low_piece,
            array(pair, jnp.bfloat16, wide),
            array(pair, jnp.bfloat16, three),
            array(pair, jnp.bfloat16, pair),
            array(pair, jnp.float32),
            losses,
        ),
        (low_piece,),
    )
    loss = near_loss + middle_loss + far_loss + last_loss

    def text_sums(weights, tail):
        return transposed_product(weights, img) + transposed_product(tail, img_tail)

    loss = loss + swap(loss, 0, 1)
    opposite_part = text_sums(last_weights, last_tail)
    sent = encode(jnp.where(on_first, img_part_tail, opposite_part), ONE_CHIP)
    sent, far_weights, far_tail = lax.optimization_barrier((sent, far_weights, far_tail))
    tail_received = swap(sent)
    far_part = text_sums(far_weights, far_tail)
    sent = encode(jnp.where(on_first, img_part, far_part), ONE_CHIP)
    tail_received, sent, loss = lax.optimization_barrier((tail_received, sent, loss))

    a, b = small_call(
        opposite_kernel, "opposite", core, (opposite_part, img_part_tail, tail_received), (low_half, low_half)
    )
    a, b, sent, near_weights, near_tail = lax.optimization_barrier((a, b, sent, near_weights, near_tail))
    from_a, from_b = move(a, "a"), move(b, "b")
    rest_received = swap(sent)
    near_part = text_sums(near_weights, near_tail)
    sent = encode(near_part, ONE_CHIP)
    loss = loss + swap(loss, 8, 1)
    loss = loss + swap(loss, 0, 2)
    (second,) = small_call(
        second_kernel, "second", core, (far_part, rest_received), (low_piece,)
    )
    from_a, from_b, second, sent, loss = lax.optimization_barrier((from_a, from_b, second, sent, loss))

    second_received = move(second, "a")
    x, b = small_call(
        far_kernel,
        "far",
        core,
        (far_part, rest_received, img_part, img_part_tail, tail_received, from_a, from_b),
        (low_piece,) * 2,
    )
    x, b, sent = lax.optimization_barrier((x, b, sent))
    from_x, from_b = move(x, "x"), move(b, "b")
    near_received = swap(sent)
    (base,) = small_call(
        base_kernel, "base", core, (near_part, near_received, img_part, rest_received), (array(wide, jnp.float32),)
    )
    more = swap(loss, 0, 6)
    base, more = lax.optimization_barrier((base, more))
    loss = loss + more

    def near_slot(k, received):
        (out,) = small_call(
            lambda *refs: near_kernel(k, *refs), "near", core, (base, received), (low_piece,)
        )
        return out

    from_b, from_x, from_a = (
        move(near_slot(3, second_received), "b"),
        move(near_slot(1, from_b), "x"),
        move(near_slot(2, from_x), "a"),
    )
    loss = loss + swap(loss, 2, 0)
    loss = loss + swap(loss, 6, 0)
    keep, give = small_call(
        gather_sums_kernel,
        "gather_sums",
        core,
        (base, from_a, from_b, from_x, loss),
        (array(own, jnp.float32), array(own + 8, jnp.float32)),
    )
    grad = array(own, jnp.float32)
    loss_value, grad_image, grad_text = small_call(
        lambda *refs: finish_kernel(batch, *refs),
        "finish",
        core,
        (image_embed, text_embed, keep, swap(give), loss),
        (array(1, jnp.float32, 1), grad, grad),
    )
    return (loss_value.reshape(()), grad_image, grad_text)


def solution(mesh):
    in_specs = (P(("row", "col"), None), P(("row", "col"), None), P(), P())
    out_specs = (P(), P(("row", "col"), None), P(("row", "col"), None))
    return jax.shard_map(body, mesh=mesh, in_specs=in_specs, out_specs=out_specs, check_vma=False)
```

```python
import jax
import jax.numpy as jnp
from jax import lax
from jax.experimental import pallas as pl
from jax.experimental.pallas import tpu as pltpu
from jax.sharding import PartitionSpec as P

VMEM = pl.BlockSpec(memory_space=pltpu.VMEM)
SMEM = pl.BlockSpec(memory_space=pltpu.SMEM)
HBM = pl.BlockSpec(memory_space=pltpu.HBM)
MIB = 1024 * 1024
TINY = 1.1754944e-38
AXES = ("row", "col")
ROWS, COLS = 16, 8
ONE_CHIP, TWO_CHIPS, FOUR_CHIPS = 0.5, 0.25, 0.125
PARTNERS = {"x": ((0, 1), (8, 1)), "a": ((0, 2), (2, 0)), "b": ((0, 6), (6, 0))}


def exchange(x, bits_of_core):
    pairs = []
    for row in range(ROWS):
        for col in range(COLS):
            row_bits, col_bits = bits_of_core[row & 1]
            pairs.append((row * COLS + col, (row ^ row_bits) * COLS + (col ^ col_bits)))
    return lax.ppermute(x, AXES, pairs)


def move(x, step):
    return exchange(x, PARTNERS[step])


def swap(x, row_bits=1, col_bits=0):
    return exchange(x, ((row_bits, col_bits),) * 2)


def encode(x, shift):
    y = x * shift
    y2 = y * y
    y4 = y2 * y2
    return (y4 * y2 * (y * jnp.abs(y))).astype(jnp.bfloat16)


def decode(e, shift):
    f = e.astype(jnp.float32)
    size = jnp.exp2(jnp.log2(jnp.maximum(jnp.abs(f), TINY)) * 0.125)
    return jnp.where(f < 0.0, -size, size) * (1.0 / shift)


def row_scale(raw):
    return lax.rsqrt(jnp.sum(raw * raw, axis=1, keepdims=True) + 1e-06)


def by_core(core_ref, work):
    pl.when(core_ref[0] == 0)(lambda: work(True))
    pl.when(core_ref[0] != 0)(lambda: work(False))


def normalize_kernel(core_ref, img_ref, txt_ref, keep_ref, give_ref, raw_ref, sems):
    copies = [
        pltpu.make_async_copy(source, raw_ref.at[k], sems.at[k])
        for k, source in enumerate((txt_ref, img_ref))
    ]
    for copy in copies:
        copy.start()

    def low(k):
        raw = raw_ref[k]
        return (raw * row_scale(raw)).astype(jnp.bfloat16)

    for k, copy in enumerate(copies):
        copy.wait()

        def work(is_first, k=k):
            ref = keep_ref if (k == 0) == is_first else give_ref
            ref[...] = low(k)

        by_core(core_ref, work)


def normalize(core, img, txt):
    low = jax.ShapeDtypeStruct(img.shape, jnp.bfloat16)
    return pl.pallas_call(
        normalize_kernel,
        out_shape=(low, low),
        in_specs=[SMEM, HBM, HBM],
        out_specs=(VMEM, VMEM),
        scratch_shapes=[pltpu.VMEM((2, *img.shape), jnp.float32), pltpu.SemaphoreType.DMA((2,))],
        compiler_params=pltpu.CompilerParams(vmem_limit_bytes=6 * MIB),
        name="normalize",
    )(core, img, txt)


def pack_kernel(*refs):
    out_ref = refs[-1]
    start = 0
    for ref in refs[:-1]:
        out_ref[start : start + ref.shape[0]] = ref[...]
        start += ref.shape[0]


def pack(*pieces):
    shape = (sum(p.shape[0] for p in pieces), pieces[0].shape[1])
    return pl.pallas_call(
        pack_kernel,
        out_shape=jax.ShapeDtypeStruct(shape, pieces[0].dtype),
        in_specs=[VMEM] * len(pieces),
        out_specs=VMEM,
        compiler_params=pltpu.CompilerParams(vmem_limit_bytes=8 * MIB),
        name="pack",
    )(*pieces)


def half_kernel(k, in_ref, out_ref):
    rows = out_ref.shape[0]
    out_ref[...] = in_ref[k * rows : (k + 1) * rows]


def half_of(x, k):
    return pl.pallas_call(
        lambda *refs: half_kernel(k, *refs),
        out_shape=jax.ShapeDtypeStruct((x.shape[0] // 2, x.shape[1]), x.dtype),
        in_specs=[VMEM],
        out_specs=VMEM,
        compiler_params=pltpu.CompilerParams(vmem_limit_bytes=4 * MIB),
        name="half_of",
    )(x)


def run_tiles(pair, sharp_ref, bias_ref, jobs):
    sharp_scalar = jnp.max(sharp_ref[...])
    bias = jnp.max(bias_ref[...])
    steps = [(job, k) for job in jobs for k in range(len(job[1]))]

    def products(step):
        job, k = step
        return lax.dot_general(
            job[0][...], job[1][k][0][...], (((1,), (1,)), ((), ())), preferred_element_type=jnp.float32
        )

    loss = jnp.zeros((8, 128), jnp.float32)
    following = products(steps[0])
    for i, (job, k) in enumerate(steps):
        current = following
        if i + 1 < len(steps):
            following = products(steps[i + 1])
        _, blocks, before, out, corner = job
        texts, weights_out = blocks[k]
        rows, cols = current.shape
        sharp = jnp.exp(jnp.full((1, cols), sharp_scalar, jnp.float32))
        logits = current * sharp + bias
        grown = jnp.exp(logits)
        one_more = 1.0 + grown
        weights = sharp * (grown / one_more)
        weights_out[...] = weights.astype(jnp.bfloat16)
        logs = jnp.log(one_more[: rows // 2] * one_more[rows // 2 :])
        logs = jnp.sum(logs.reshape(rows // 16, 8, cols), axis=0)
        if corner is not None:
            row_ids = lax.broadcasted_iota(jnp.int32, (pair, pair), 0)
            col_ids = lax.broadcasted_iota(jnp.int32, (pair, pair), 1)
            wanted = jnp.where(row_ids < pair // 2, row_ids + pair // 2, row_ids - pair // 2)
            same = (wanted == col_ids) & (corner == 0)
            own = weights[:pair, :pair] - jnp.where(same, sharp[:, :pair], 0.0)
            weights_out[:pair, :pair] = own.astype(jnp.bfloat16)
            matched = jnp.where(same, logits[:pair, :pair], 0.0)
            matched = jnp.sum(matched.reshape(pair // 8, 8, pair), axis=0)
            for start in range(0, pair, 128):
                loss = loss - matched[:, start : start + 128]
        for start in range(0, cols, 128):
            loss = loss + logs[:, start : start + 128]
        part = jnp.dot(weights_out[...], texts[...], preferred_element_type=jnp.float32)
        if k == 0:
            total = part if before is None else part + before[...]
        else:
            total = total + part
        if k == len(blocks) - 1:
            out[...] = total
    return loss


def row_blocks(ref, size, rows=None):
    return [ref.at[pl.ds(start, size)] for start in range(0, rows or ref.shape[0], size)]


def near_tile_kernel(core_ref, sharp_ref, bias_ref, near_ref, received_ref, img_ref, txt_ref, weights_ref, part_ref, loss_ref):
    count = img_ref.shape[0]
    pair = count // 2

    def work(is_first):
        txt_ref[...] = near_ref[...] if is_first else received_ref[...]
        img_ref[...] = received_ref[:count] if is_first else near_ref[count:]

    by_core(core_ref, work)
    jobs = []
    for k, rows in enumerate(row_blocks(img_ref, pair)):
        span = pl.ds(k * pair, pair)
        corner = core_ref[0] if k == 0 else None
        jobs.append((rows, [(txt_ref, weights_ref.at[span])], None, part_ref.at[span], corner))
    loss_ref[...] = run_tiles(pair, sharp_ref, bias_ref, jobs)


def far_tile_kernel(
    core_ref, sharp_ref, bias_ref, far_ref, received_ref, near_img_ref, near_before_ref,
    txt_ref, img_ref, weights_ref, part_ref, loss_ref,
):
    count = near_img_ref.shape[0]
    pair = count // 2

    def work(is_first):
        txt_ref[...] = far_ref[...] if is_first else received_ref[...]
        img_ref[count:] = received_ref[:pair] if is_first else far_ref[count:]

    by_core(core_ref, work)
    img_ref[:count] = near_img_ref[...]
    jobs = []
    before = row_blocks(near_before_ref, pair) + [None]
    for k, rows in enumerate(row_blocks(img_ref, pair)):
        span = pl.ds(k * pair, pair)
        jobs.append((rows, [(txt_ref, weights_ref.at[span])], before[k], part_ref.at[span], None))
    loss_ref[...] = run_tiles(pair, sharp_ref, bias_ref, jobs)


def middle_tile_kernel(
    core_ref, sharp_ref, bias_ref, img_ref, txt_ref, before_ref, near_weights_ref, weights_ref, part_ref, loss_ref
):
    pair = part_ref.shape[0]
    span = pl.ds(2 * pair, pair)
    weights_ref[: 2 * pair] = near_weights_ref[...]
    job = (img_ref.at[span], [(txt_ref, weights_ref.at[span])], before_ref.at[span], part_ref, None)
    loss_ref[...] = run_tiles(pair, sharp_ref, bias_ref, [job])


def last_tile_kernel(
    core_ref, sharp_ref, bias_ref, last_ref, received_ref, far_ref, far_received_ref, near_txt_ref, far_txt_ref,
    img_ref, before_ref, middle_before_ref,
    weights_ref, part_ref, img_tail_ref, near_tail_ref, far_tail_ref, last_tail_ref, part_tail_ref, loss_ref, txt_ref,
):
    pair = last_ref.shape[0]
    half = pair // 2

    def work(is_first):
        txt_ref[...] = last_ref[...] if is_first else received_ref[...]
        img_tail_ref[:half] = far_received_ref[pair : pair + half] if is_first else far_ref[pair + half : 2 * pair]
        img_tail_ref[half:] = received_ref[:half] if is_first else last_ref[half:]

    by_core(core_ref, work)
    jobs = []
    before = row_blocks(before_ref, pair, 2 * pair) + [middle_before_ref]
    for k, rows in enumerate(row_blocks(img_ref, pair)):
        span = pl.ds(k * pair, pair)
        jobs.append((rows, [(txt_ref, weights_ref.at[span])], before[k], part_ref.at[span], None))
    blocks = [(near_txt_ref, near_tail_ref), (far_txt_ref, far_tail_ref), (txt_ref, last_tail_ref)]
    jobs.append((img_tail_ref, blocks, None, part_tail_ref, None))
    loss_ref[...] = run_tiles(pair, sharp_ref, bias_ref, jobs)


def tile_call(kernel, name, pairs, scalars, arrays, outs, scratch=()):
    features = arrays[0].shape[1]
    return pl.pallas_call(
        kernel,
        out_shape=outs,
        in_specs=[SMEM] + [VMEM] * (len(scalars) - 1 + len(arrays)),
        out_specs=(VMEM,) * len(outs),
        scratch_shapes=[pltpu.VMEM(x.shape, x.dtype) for x in scratch],
        compiler_params=pltpu.CompilerParams(vmem_limit_bytes=16 * MIB),
        cost_estimate=pl.CostEstimate(
            flops=4 * pairs * features,
            bytes_accessed=sum(2 * x.size for x in arrays),
            transcendentals=3 * pairs,
        ),
        name=name,
    )(*scalars, *arrays)


def small_call(kernel, name, core, arrays, outs):
    size = sum(x.size * x.dtype.itemsize for x in (*arrays, *outs))
    return pl.pallas_call(
        kernel,
        out_shape=outs,
        in_specs=[SMEM] + [VMEM] * len(arrays),
        out_specs=(VMEM,) * len(outs),
        compiler_params=pltpu.CompilerParams(vmem_limit_bytes=size + 4 * MIB),
        name=name,
    )(core, *arrays)


CHUNK = 64


def each_chunk(rows, work):
    def step(i, carry):
        first = pl.multiple_of(i * CHUNK, CHUNK)
        work(lambda start=0: pl.ds(start + first, CHUNK))
        return carry

    lax.fori_loop(0, rows // CHUNK, step, 0)


def opposite_kernel(core_ref, txt_ref, img_ref, received_ref, a_ref, b_ref):
    half = a_ref.shape[0]

    def work(is_first):
        def texts(at):
            a_ref[at()] = encode(txt_ref[at()] + decode(received_ref[at()], ONE_CHIP), ONE_CHIP)
            b_ref[at()] = encode(txt_ref[at(half)] + decode(received_ref[at(half)], ONE_CHIP), ONE_CHIP)

        def images(at):
            a_ref[at()] = received_ref[at(half)]
            b_ref[at()] = encode(img_ref[at(half)], ONE_CHIP)

        each_chunk(half, texts if is_first else images)

    by_core(core_ref, work)


def second_kernel(core_ref, txt_ref, received_ref, out_ref):
    pair = out_ref.shape[0]

    def work(is_first):
        def rows(at):
            if is_first:
                value = txt_ref[at()] + decode(received_ref[at()], ONE_CHIP)
            else:
                value = decode(received_ref[at(2 * pair)], ONE_CHIP)
            out_ref[at()] = encode(value, TWO_CHIPS)

        each_chunk(pair, rows)

    by_core(core_ref, work)


def far_kernel(
    core_ref, txt_ref, txt_received_ref, img_ref, img_tail_ref, tail_received_ref, from_a_ref, from_b_ref, x_ref, b_ref
):
    pair = x_ref.shape[0]
    half = pair // 2

    def work(is_first):
        def rows(at):
            def base(i):
                if is_first:
                    return txt_ref[at(i * half)] + decode(txt_received_ref[at(i * half)], ONE_CHIP)
                if i == 2:
                    return decode(tail_received_ref[at()], ONE_CHIP)
                return img_tail_ref[at()] if i == 3 else img_ref[at(i * half)]

            x_ref[at()] = encode(base(2), TWO_CHIPS)
            x_ref[at(half)] = encode(base(3) + decode(from_b_ref[at()], ONE_CHIP), TWO_CHIPS)
            b_ref[at()] = encode(base(4) + decode(from_a_ref[at()], ONE_CHIP), TWO_CHIPS)
            b_ref[at(half)] = encode(base(5), TWO_CHIPS)

        each_chunk(half, rows)

    by_core(core_ref, work)


def base_kernel(core_ref, txt_ref, received_ref, img_ref, img_received_ref, out_ref):
    count = out_ref.shape[0]
    two = count // 2

    def work(is_first):
        def texts(at):
            out_ref[at()] = txt_ref[at()] + decode(received_ref[at()], ONE_CHIP)

        def images(at):
            out_ref[at()] = decode(img_received_ref[at()], ONE_CHIP)

        if is_first:
            each_chunk(count, texts)
        else:
            each_chunk(two, images)
            out_ref[two:] = img_ref[:two]

    by_core(core_ref, work)


def near_kernel(k, core_ref, base_ref, received_ref, out_ref):
    pair = out_ref.shape[0]

    def rows(at):
        value = base_ref[at(k * pair)] + decode(received_ref[at()], TWO_CHIPS)
        out_ref[at()] = encode(value, FOUR_CHIPS)

    each_chunk(pair, rows)


def gather_sums_kernel(core_ref, base_ref, a_ref, b_ref, x_ref, loss_ref, keep_ref, give_ref):
    own = keep_ref.shape[0]
    give_ref[own:] = jnp.zeros((8, give_ref.shape[1]), jnp.float32)
    give_ref[own:, :128] = loss_ref[...]

    def rows(at):
        for start, ref in ((0, keep_ref), (own, give_ref)):
            total = base_ref[at(start)] + decode(x_ref[at(start)], FOUR_CHIPS)
            total = total + decode(a_ref[at(start)], FOUR_CHIPS)
            ref[at()] = total + decode(b_ref[at(start)], FOUR_CHIPS)

    each_chunk(own, rows)


def finish_kernel(batch, core_ref, img_ref, txt_ref, kept_ref, received_ref, loss_parts_ref, loss_ref, grad_img_ref, grad_txt_ref):
    own = kept_ref.shape[0]
    both = loss_parts_ref[...] + received_ref[own:, :128]
    loss_ref[...] = jnp.full((1, 1), jnp.sum(both) * (1.0 / batch), jnp.float32)

    def side(at, raw_ref, sum_ref, grad_ref):
        raw = raw_ref[at()]
        scale = row_scale(raw)
        unit = raw * scale
        summed = sum_ref[at()]
        grad_ref[at()] = (summed - unit * jnp.sum(unit * summed, axis=1, keepdims=True)) * scale

    def work(is_first):
        def rows(at):
            side(at, img_ref, received_ref if is_first else kept_ref, grad_img_ref)
            side(at, txt_ref, kept_ref if is_first else received_ref, grad_txt_ref)

        each_chunk(own, rows)

    by_core(core_ref, work)


def transposed_product(weights, img):
    return lax.dot_general(
        weights, img, (((0,), (0,)), ((), ())), preferred_element_type=jnp.float32
    )


def body(image_embed, text_embed, exponent_of_sharpness, bias):
    own, features = image_embed.shape
    pair = 2 * own
    batch = own * ROWS * COLS
    core = lax.axis_index("row") & 1
    core, on_first = lax.optimization_barrier((core.reshape(1), core == 0))

    def array(rows, dtype, columns=features):
        return jax.ShapeDtypeStruct((rows, columns), dtype)

    low_half, low_piece = array(own, jnp.bfloat16), array(pair, jnp.bfloat16)

    keep, give = normalize(core, image_embed, text_embed)
    low = pack(keep, swap(give))
    slot_x, slot_1, slot_3 = move(low, "x"), move(low, "a"), move(low, "b")
    slot_2, slot_x3, slot_x1 = move(slot_3, "a"), move(slot_x, "b"), move(slot_1, "x")
    near = pack(low, slot_x, slot_1, slot_3)
    near_received = swap(near)
    sharpness = jnp.broadcast_to(exponent_of_sharpness.reshape(1, 1), (8, 128))
    shift = jnp.broadcast_to(bias.reshape(1, 1), (8, 128))

    scalars = (core, sharpness, shift)
    losses = array(8, jnp.float32, 128)
    wide, three, two = 4 * pair, 3 * pair, 2 * pair
    near_img, near_txt, near_weights, near_part, near_loss = tile_call(
        near_tile_kernel,
        "tile_near",
        two * wide,
        scalars,
        (near, near_received),
        (
            array(two, jnp.bfloat16),
            array(wide, jnp.bfloat16),
            array(two, jnp.bfloat16, wide),
            array(two, jnp.float32),
            losses,
        ),
    )
    slot_2, slot_x3, slot_x1, near_part = lax.optimization_barrier((slot_2, slot_x3, slot_x1, near_part))
    last_a = move(half_of(slot_x3, 0), "a")
    last_b = move(half_of(slot_x1, 1), "b")
    far = pack(slot_2, slot_x1, slot_x3)
    far_received = swap(far)
    far_txt, img, far_weights, part, far_loss = tile_call(
        far_tile_kernel,
        "tile_far",
        three * three,
        scalars,
        (far, far_received, near_img, near_part),
        (
            array(three, jnp.bfloat16),
            array(three, jnp.bfloat16),
            array(three, jnp.bfloat16, three),
            array(three, jnp.float32),
            losses,
        ),
    )
    last_a, last_b, part = lax.optimization_barrier((last_a, last_b, part))
    last = pack(last_a, last_b)
    last_received = swap(last)
    near_weights, middle_part, middle_loss = tile_call(
        middle_tile_kernel,
        "tile_middle",
        pair * wide,
        scalars,
        (img, near_txt, part, near_weights),
        (array(three, jnp.bfloat16, wide), array(pair, jnp.float32), losses),
    )
    last_weights, img_part, img_tail, near_tail, far_tail, last_tail, img_part_tail, last_loss = tile_call(
        last_tile_kernel,
        "tile_last",
        three * pair + pair * 2 * wide,
        scalars,
        (last, last_received, far, far_received, near_txt, far_txt, img, part, middle_part),
        (
            array(three, jnp.bfloat16, pair),
            array(three, jnp.float32),
            low_piece,
            array(pair, jnp.bfloat16, wide),
            array(pair, jnp.bfloat16, three),
            array(pair, jnp.bfloat16, pair),
            array(pair, jnp.float32),
            losses,
        ),
        (low_piece,),
    )
    loss = near_loss + middle_loss + far_loss + last_loss

    def text_sums(weights, tail):
        return transposed_product(weights, img) + transposed_product(tail, img_tail)

    loss = loss + swap(loss, 0, 1)
    opposite_part = text_sums(last_weights, last_tail)
    sent = encode(jnp.where(on_first, img_part_tail, opposite_part), ONE_CHIP)
    sent, far_weights, far_tail = lax.optimization_barrier((sent, far_weights, far_tail))
    tail_received = swap(sent)
    far_part = text_sums(far_weights, far_tail)
    sent = encode(jnp.where(on_first, img_part, far_part), ONE_CHIP)
    tail_received, sent, loss = lax.optimization_barrier((tail_received, sent, loss))

    a, b = small_call(
        opposite_kernel, "opposite", core, (opposite_part, img_part_tail, tail_received), (low_half, low_half)
    )
    a, b, sent, near_weights, near_tail = lax.optimization_barrier((a, b, sent, near_weights, near_tail))
    from_a, from_b = move(a, "a"), move(b, "b")
    rest_received = swap(sent)
    near_part = text_sums(near_weights, near_tail)
    sent = encode(near_part, ONE_CHIP)
    loss = loss + swap(loss, 8, 1)
    loss = loss + swap(loss, 0, 2)
    (second,) = small_call(
        second_kernel, "second", core, (far_part, rest_received), (low_piece,)
    )
    from_a, from_b, sent, loss = lax.optimization_barrier((from_a, from_b, sent, loss))

    second_received = move(second, "a")
    x, b = small_call(
        far_kernel,
        "far",
        core,
        (far_part, rest_received, img_part, img_part_tail, tail_received, from_a, from_b),
        (low_piece,) * 2,
    )
    x, b, sent = lax.optimization_barrier((x, b, sent))
    from_x, from_b = move(x, "x"), move(b, "b")
    near_received = swap(sent)
    (base,) = small_call(
        base_kernel, "base", core, (near_part, near_received, img_part, rest_received), (array(wide, jnp.float32),)
    )
    base, loss = lax.optimization_barrier((base, loss))
    loss = loss + swap(loss, 0, 6)
    base, loss = lax.optimization_barrier((base, loss))

    def near_slot(k, received):
        (out,) = small_call(
            lambda *refs: near_kernel(k, *refs), "near", core, (base, received), (low_piece,)
        )
        return out

    from_b, from_x, from_a = (
        move(near_slot(3, second_received), "b"),
        move(near_slot(1, from_b), "x"),
        move(near_slot(2, from_x), "a"),
    )
    loss = loss + swap(loss, 2, 0)
    loss = loss + swap(loss, 6, 0)
    keep, give = small_call(
        gather_sums_kernel,
        "gather_sums",
        core,
        (base, from_a, from_b, from_x, loss),
        (array(own, jnp.float32), array(own + 8, jnp.float32)),
    )
    grad = array(own, jnp.float32)
    loss_value, grad_image, grad_text = small_call(
        lambda *refs: finish_kernel(batch, *refs),
        "finish",
        core,
        (image_embed, text_embed, keep, swap(give), loss),
        (array(1, jnp.float32, 1), grad, grad),
    )
    return (loss_value.reshape(()), grad_image, grad_text)


def solution(mesh):
    in_specs = (P(("row", "col"), None), P(("row", "col"), None), P(), P())
    out_specs = (P(), P(("row", "col"), None), P(("row", "col"), None))
    return jax.shard_map(body, mesh=mesh, in_specs=in_specs, out_specs=out_specs, check_vma=False)
```

```python
import jax
import jax.numpy as jnp
from jax import lax
from jax.experimental import pallas as pl
from jax.experimental.pallas import tpu as pltpu
from jax.sharding import PartitionSpec as P

VMEM = pl.BlockSpec(memory_space=pltpu.VMEM)
SMEM = pl.BlockSpec(memory_space=pltpu.SMEM)
HBM = pl.BlockSpec(memory_space=pltpu.HBM)
MIB = 1024 * 1024
TINY = 1.1754944e-38
AXES = ("row", "col")
ROWS, COLS = 16, 8
ONE_CHIP, TWO_CHIPS, FOUR_CHIPS = 0.5, 0.25, 0.125
PARTNERS = {"x": ((0, 1), (8, 1)), "a": ((0, 2), (2, 0)), "b": ((0, 6), (6, 0))}


def exchange(x, bits_of_core):
    pairs = []
    for row in range(ROWS):
        for col in range(COLS):
            row_bits, col_bits = bits_of_core[row & 1]
            pairs.append((row * COLS + col, (row ^ row_bits) * COLS + (col ^ col_bits)))
    return lax.ppermute(x, AXES, pairs)


def move(x, step):
    return exchange(x, PARTNERS[step])


def swap(x, row_bits=1, col_bits=0):
    return exchange(x, ((row_bits, col_bits),) * 2)


def encode(x, shift):
    y = x * shift
    y2 = y * y
    y4 = y2 * y2
    return (y4 * y2 * (y * jnp.abs(y))).astype(jnp.bfloat16)


def decode(e, shift):
    f = e.astype(jnp.float32)
    size = jnp.exp2(jnp.log2(jnp.maximum(jnp.abs(f), TINY)) * 0.125)
    return jnp.where(f < 0.0, -size, size) * (1.0 / shift)


def row_scale(raw):
    return lax.rsqrt(jnp.sum(raw * raw, axis=1, keepdims=True) + 1e-06)


def by_core(core_ref, work):
    pl.when(core_ref[0] == 0)(lambda: work(True))
    pl.when(core_ref[0] != 0)(lambda: work(False))


def normalize_kernel(core_ref, img_ref, txt_ref, keep_ref, give_ref, raw_ref, sems):
    copies = [
        pltpu.make_async_copy(source, raw_ref.at[k], sems.at[k])
        for k, source in enumerate((txt_ref, img_ref))
    ]
    for copy in copies:
        copy.start()

    def low(k):
        raw = raw_ref[k]
        return (raw * row_scale(raw)).astype(jnp.bfloat16)

    for k, copy in enumerate(copies):
        copy.wait()

        def work(is_first, k=k):
            ref = keep_ref if (k == 0) == is_first else give_ref
            ref[...] = low(k)

        by_core(core_ref, work)


def normalize(core, img, txt):
    low = jax.ShapeDtypeStruct(img.shape, jnp.bfloat16)
    return pl.pallas_call(
        normalize_kernel,
        out_shape=(low, low),
        in_specs=[SMEM, HBM, HBM],
        out_specs=(VMEM, VMEM),
        scratch_shapes=[pltpu.VMEM((2, *img.shape), jnp.float32), pltpu.SemaphoreType.DMA((2,))],
        compiler_params=pltpu.CompilerParams(vmem_limit_bytes=6 * MIB),
        name="normalize",
    )(core, img, txt)


def pack_kernel(*refs):
    out_ref = refs[-1]
    start = 0
    for ref in refs[:-1]:
        out_ref[start : start + ref.shape[0]] = ref[...]
        start += ref.shape[0]


def pack(*pieces):
    shape = (sum(p.shape[0] for p in pieces), pieces[0].shape[1])
    return pl.pallas_call(
        pack_kernel,
        out_shape=jax.ShapeDtypeStruct(shape, pieces[0].dtype),
        in_specs=[VMEM] * len(pieces),
        out_specs=VMEM,
        compiler_params=pltpu.CompilerParams(vmem_limit_bytes=8 * MIB),
        name="pack",
    )(*pieces)


def half_kernel(k, in_ref, out_ref):
    rows = out_ref.shape[0]
    out_ref[...] = in_ref[k * rows : (k + 1) * rows]


def half_of(x, k):
    return pl.pallas_call(
        lambda *refs: half_kernel(k, *refs),
        out_shape=jax.ShapeDtypeStruct((x.shape[0] // 2, x.shape[1]), x.dtype),
        in_specs=[VMEM],
        out_specs=VMEM,
        compiler_params=pltpu.CompilerParams(vmem_limit_bytes=4 * MIB),
        name="half_of",
    )(x)


def run_tiles(pair, sharp_ref, bias_ref, jobs):
    sharp_scalar = jnp.max(sharp_ref[...])
    bias = jnp.max(bias_ref[...])
    steps = [(job, k) for job in jobs for k in range(len(job[1]))]

    def products(step):
        job, k = step
        return lax.dot_general(
            job[0][...], job[1][k][0][...], (((1,), (1,)), ((), ())), preferred_element_type=jnp.float32
        )

    loss = jnp.zeros((8, 128), jnp.float32)
    following = products(steps[0])
    for i, (job, k) in enumerate(steps):
        current = following
        if i + 1 < len(steps):
            following = products(steps[i + 1])
        _, blocks, before, out, corner = job
        texts, weights_out = blocks[k]
        rows, cols = current.shape
        sharp = jnp.exp(jnp.full((1, cols), sharp_scalar, jnp.float32))
        logits = current * sharp + bias
        grown = jnp.exp(logits)
        one_more = 1.0 + grown
        weights = sharp * (grown / one_more)
        weights_out[...] = weights.astype(jnp.bfloat16)
        logs = jnp.log(one_more[: rows // 2] * one_more[rows // 2 :])
        logs = jnp.sum(logs.reshape(rows // 16, 8, cols), axis=0)
        if corner is not None:
            row_ids = lax.broadcasted_iota(jnp.int32, (pair, pair), 0)
            col_ids = lax.broadcasted_iota(jnp.int32, (pair, pair), 1)
            wanted = jnp.where(row_ids < pair // 2, row_ids + pair // 2, row_ids - pair // 2)
            same = (wanted == col_ids) & (corner == 0)
            own = weights[:pair, :pair] - jnp.where(same, sharp[:, :pair], 0.0)
            weights_out[:pair, :pair] = own.astype(jnp.bfloat16)
            matched = jnp.where(same, logits[:pair, :pair], 0.0)
            matched = jnp.sum(matched.reshape(pair // 8, 8, pair), axis=0)
            for start in range(0, pair, 128):
                loss = loss - matched[:, start : start + 128]
        for start in range(0, cols, 128):
            loss = loss + logs[:, start : start + 128]
        part = jnp.dot(weights_out[...], texts[...], preferred_element_type=jnp.float32)
        if k == 0:
            total = part if before is None else part + before[...]
        else:
            total = total + part
        if k == len(blocks) - 1:
            out[...] = total
    return loss


def row_blocks(ref, size, rows=None):
    return [ref.at[pl.ds(start, size)] for start in range(0, rows or ref.shape[0], size)]


def near_tile_kernel(core_ref, sharp_ref, bias_ref, near_ref, received_ref, img_ref, txt_ref, weights_ref, part_ref, loss_ref):
    count = img_ref.shape[0]
    pair = count // 2

    def work(is_first):
        txt_ref[...] = near_ref[...] if is_first else received_ref[...]
        img_ref[...] = received_ref[:count] if is_first else near_ref[count:]

    by_core(core_ref, work)
    jobs = []
    for k, rows in enumerate(row_blocks(img_ref, pair)):
        span = pl.ds(k * pair, pair)
        corner = core_ref[0] if k == 0 else None
        jobs.append((rows, [(txt_ref, weights_ref.at[span])], None, part_ref.at[span], corner))
    loss_ref[...] = run_tiles(pair, sharp_ref, bias_ref, jobs)


def far_tile_kernel(
    core_ref, sharp_ref, bias_ref, far_ref, received_ref, near_img_ref, near_before_ref,
    txt_ref, img_ref, weights_ref, part_ref, loss_ref,
):
    count = near_img_ref.shape[0]
    pair = count // 2

    def work(is_first):
        txt_ref[...] = far_ref[...] if is_first else received_ref[...]
        img_ref[count:] = received_ref[:pair] if is_first else far_ref[count:]

    by_core(core_ref, work)
    img_ref[:count] = near_img_ref[...]
    jobs = []
    before = row_blocks(near_before_ref, pair) + [None]
    for k, rows in enumerate(row_blocks(img_ref, pair)):
        span = pl.ds(k * pair, pair)
        jobs.append((rows, [(txt_ref, weights_ref.at[span])], before[k], part_ref.at[span], None))
    loss_ref[...] = run_tiles(pair, sharp_ref, bias_ref, jobs)


def middle_tile_kernel(
    core_ref, sharp_ref, bias_ref, img_ref, txt_ref, before_ref, near_weights_ref, weights_ref, part_ref, loss_ref
):
    pair = part_ref.shape[0]
    span = pl.ds(2 * pair, pair)
    weights_ref[: 2 * pair] = near_weights_ref[...]
    job = (img_ref.at[span], [(txt_ref, weights_ref.at[span])], before_ref.at[span], part_ref, None)
    loss_ref[...] = run_tiles(pair, sharp_ref, bias_ref, [job])


def last_tile_kernel(
    core_ref, sharp_ref, bias_ref, last_ref, received_ref, far_ref, far_received_ref, near_txt_ref, far_txt_ref,
    img_ref, before_ref, middle_before_ref,
    weights_ref, part_ref, img_tail_ref, near_tail_ref, far_tail_ref, last_tail_ref, part_tail_ref, loss_ref, txt_ref,
):
    pair = last_ref.shape[0]
    half = pair // 2

    def work(is_first):
        txt_ref[...] = last_ref[...] if is_first else received_ref[...]
        img_tail_ref[:half] = far_received_ref[pair : pair + half] if is_first else far_ref[pair + half : 2 * pair]
        img_tail_ref[half:] = received_ref[:half] if is_first else last_ref[half:]

    by_core(core_ref, work)
    jobs = []
    before = row_blocks(before_ref, pair, 2 * pair) + [middle_before_ref]
    for k, rows in enumerate(row_blocks(img_ref, pair)):
        span = pl.ds(k * pair, pair)
        jobs.append((rows, [(txt_ref, weights_ref.at[span])], before[k], part_ref.at[span], None))
    blocks = [(near_txt_ref, near_tail_ref), (far_txt_ref, far_tail_ref), (txt_ref, last_tail_ref)]
    jobs.append((img_tail_ref, blocks, None, part_tail_ref, None))
    loss_ref[...] = run_tiles(pair, sharp_ref, bias_ref, jobs)


def tile_call(kernel, name, pairs, scalars, arrays, outs, scratch=()):
    features = arrays[0].shape[1]
    return pl.pallas_call(
        kernel,
        out_shape=outs,
        in_specs=[SMEM] + [VMEM] * (len(scalars) - 1 + len(arrays)),
        out_specs=(VMEM,) * len(outs),
        scratch_shapes=[pltpu.VMEM(x.shape, x.dtype) for x in scratch],
        compiler_params=pltpu.CompilerParams(vmem_limit_bytes=16 * MIB),
        cost_estimate=pl.CostEstimate(
            flops=4 * pairs * features,
            bytes_accessed=sum(2 * x.size for x in arrays),
            transcendentals=3 * pairs,
        ),
        name=name,
    )(*scalars, *arrays)


def small_call(kernel, name, core, arrays, outs):
    size = sum(x.size * x.dtype.itemsize for x in (*arrays, *outs))
    return pl.pallas_call(
        kernel,
        out_shape=outs,
        in_specs=[SMEM] + [VMEM] * len(arrays),
        out_specs=(VMEM,) * len(outs),
        compiler_params=pltpu.CompilerParams(vmem_limit_bytes=size + 4 * MIB),
        name=name,
    )(core, *arrays)


CHUNK = 64


def each_chunk(rows, work):
    def step(i, carry):
        first = pl.multiple_of(i * CHUNK, CHUNK)
        work(lambda start=0: pl.ds(start + first, CHUNK))
        return carry

    lax.fori_loop(0, rows // CHUNK, step, 0)


def opposite_kernel(core_ref, txt_ref, img_ref, received_ref, a_ref, b_ref):
    half = a_ref.shape[0]

    def work(is_first):
        def texts(at):
            a_ref[at()] = encode(txt_ref[at()] + decode(received_ref[at()], ONE_CHIP), ONE_CHIP)
            b_ref[at()] = encode(txt_ref[at(half)] + decode(received_ref[at(half)], ONE_CHIP), ONE_CHIP)

        def images(at):
            a_ref[at()] = received_ref[at(half)]
            b_ref[at()] = encode(img_ref[at(half)], ONE_CHIP)

        each_chunk(half, texts if is_first else images)

    by_core(core_ref, work)


def second_kernel(core_ref, txt_ref, received_ref, out_ref):
    pair = out_ref.shape[0]

    def work(is_first):
        def rows(at):
            if is_first:
                value = txt_ref[at()] + decode(received_ref[at()], ONE_CHIP)
            else:
                value = decode(received_ref[at(2 * pair)], ONE_CHIP)
            out_ref[at()] = encode(value, TWO_CHIPS)

        each_chunk(pair, rows)

    by_core(core_ref, work)


def far_kernel(
    core_ref, txt_ref, txt_received_ref, img_ref, img_tail_ref, tail_received_ref, from_a_ref, from_b_ref, x_ref, b_ref
):
    pair = x_ref.shape[0]
    half = pair // 2

    def work(is_first):
        def rows(at):
            def base(i):
                if is_first:
                    return txt_ref[at(i * half)] + decode(txt_received_ref[at(i * half)], ONE_CHIP)
                if i == 2:
                    return decode(tail_received_ref[at()], ONE_CHIP)
                return img_tail_ref[at()] if i == 3 else img_ref[at(i * half)]

            x_ref[at()] = encode(base(2), TWO_CHIPS)
            x_ref[at(half)] = encode(base(3) + decode(from_b_ref[at()], ONE_CHIP), TWO_CHIPS)
            b_ref[at()] = encode(base(4) + decode(from_a_ref[at()], ONE_CHIP), TWO_CHIPS)
            b_ref[at(half)] = encode(base(5), TWO_CHIPS)

        each_chunk(half, rows)

    by_core(core_ref, work)


def base_kernel(core_ref, txt_ref, received_ref, img_ref, img_received_ref, out_ref):
    count = out_ref.shape[0]
    two = count // 2

    def work(is_first):
        def texts(at):
            out_ref[at()] = txt_ref[at()] + decode(received_ref[at()], ONE_CHIP)

        def images(at):
            out_ref[at()] = decode(img_received_ref[at()], ONE_CHIP)

        if is_first:
            each_chunk(count, texts)
        else:
            each_chunk(two, images)
            out_ref[two:] = img_ref[:two]

    by_core(core_ref, work)


def near_kernel(k, core_ref, base_ref, received_ref, out_ref):
    pair = out_ref.shape[0]

    def rows(at):
        value = base_ref[at(k * pair)] + decode(received_ref[at()], TWO_CHIPS)
        out_ref[at()] = encode(value, FOUR_CHIPS)

    each_chunk(pair, rows)


def gather_sums_kernel(core_ref, base_ref, a_ref, b_ref, x_ref, loss_ref, keep_ref, give_ref):
    own = keep_ref.shape[0]
    give_ref[own:] = jnp.zeros((8, give_ref.shape[1]), jnp.float32)
    give_ref[own:, :128] = loss_ref[...]

    def rows(at):
        for start, ref in ((0, keep_ref), (own, give_ref)):
            total = base_ref[at(start)] + decode(x_ref[at(start)], FOUR_CHIPS)
            total = total + decode(a_ref[at(start)], FOUR_CHIPS)
            ref[at()] = total + decode(b_ref[at(start)], FOUR_CHIPS)

    each_chunk(own, rows)


def finish_kernel(batch, core_ref, img_ref, txt_ref, kept_ref, received_ref, loss_parts_ref, loss_ref, grad_img_ref, grad_txt_ref):
    own = kept_ref.shape[0]
    both = loss_parts_ref[...] + received_ref[own:, :128]
    loss_ref[...] = jnp.full((1, 1), jnp.sum(both) * (1.0 / batch), jnp.float32)

    def side(at, raw_ref, sum_ref, grad_ref):
        raw = raw_ref[at()]
        scale = row_scale(raw)
        unit = raw * scale
        summed = sum_ref[at()]
        grad_ref[at()] = (summed - unit * jnp.sum(unit * summed, axis=1, keepdims=True)) * scale

    def work(is_first):
        def rows(at):
            side(at, img_ref, received_ref if is_first else kept_ref, grad_img_ref)
            side(at, txt_ref, kept_ref if is_first else received_ref, grad_txt_ref)

        each_chunk(own, rows)

    by_core(core_ref, work)


def transposed_product(weights, img):
    return lax.dot_general(
        weights, img, (((0,), (0,)), ((), ())), preferred_element_type=jnp.float32
    )


def body(image_embed, text_embed, exponent_of_sharpness, bias):
    own, features = image_embed.shape
    pair = 2 * own
    batch = own * ROWS * COLS
    core = lax.axis_index("row") & 1
    core, on_first = lax.optimization_barrier((core.reshape(1), core == 0))

    def array(rows, dtype, columns=features):
        return jax.ShapeDtypeStruct((rows, columns), dtype)

    low_half, low_piece = array(own, jnp.bfloat16), array(pair, jnp.bfloat16)

    keep, give = normalize(core, image_embed, text_embed)
    low = pack(keep, swap(give))
    slot_x, slot_1, slot_3 = move(low, "x"), move(low, "a"), move(low, "b")
    slot_2, slot_x3, slot_x1 = move(slot_3, "a"), move(slot_x, "b"), move(slot_1, "x")
    near = pack(low, slot_x, slot_1, slot_3)
    near_received = swap(near)
    sharpness = jnp.broadcast_to(exponent_of_sharpness.reshape(1, 1), (8, 128))
    shift = jnp.broadcast_to(bias.reshape(1, 1), (8, 128))

    scalars = (core, sharpness, shift)
    losses = array(8, jnp.float32, 128)
    wide, three, two = 4 * pair, 3 * pair, 2 * pair
    near_img, near_txt, near_weights, near_part, near_loss = tile_call(
        near_tile_kernel,
        "tile_near",
        two * wide,
        scalars,
        (near, near_received),
        (
            array(two, jnp.bfloat16),
            array(wide, jnp.bfloat16),
            array(two, jnp.bfloat16, wide),
            array(two, jnp.float32),
            losses,
        ),
    )
    slot_2, slot_x3, slot_x1, near_part = lax.optimization_barrier((slot_2, slot_x3, slot_x1, near_part))
    last_a = move(half_of(slot_x3, 0), "a")
    last_b = move(half_of(slot_x1, 1), "b")
    far = pack(slot_2, slot_x1, slot_x3)
    far_received = swap(far)
    far_txt, img, far_weights, part, far_loss = tile_call(
        far_tile_kernel,
        "tile_far",
        three * three,
        scalars,
        (far, far_received, near_img, near_part),
        (
            array(three, jnp.bfloat16),
            array(three, jnp.bfloat16),
            array(three, jnp.bfloat16, three),
            array(three, jnp.float32),
            losses,
        ),
    )
    last_a, last_b, part = lax.optimization_barrier((last_a, last_b, part))
    last = pack(last_a, last_b)
    last_received = swap(last)
    near_weights, middle_part, middle_loss = tile_call(
        middle_tile_kernel,
        "tile_middle",
        pair * wide,
        scalars,
        (img, near_txt, part, near_weights),
        (array(three, jnp.bfloat16, wide), array(pair, jnp.float32), losses),
    )
    last_weights, img_part, img_tail, near_tail, far_tail, last_tail, img_part_tail, last_loss = tile_call(
        last_tile_kernel,
        "tile_last",
        three * pair + pair * 2 * wide,
        scalars,
        (last, last_received, far, far_received, near_txt, far_txt, img, part, middle_part),
        (
            array(three, jnp.bfloat16, pair),
            array(three, jnp.float32),
            low_piece,
            array(pair, jnp.bfloat16, wide),
            array(pair, jnp.bfloat16, three),
            array(pair, jnp.bfloat16, pair),
            array(pair, jnp.float32),
            losses,
        ),
        (low_piece,),
    )
    loss = near_loss + middle_loss + far_loss + last_loss

    def text_sums(weights, tail):
        return transposed_product(weights, img) + transposed_product(tail, img_tail)

    loss = loss + swap(loss, 0, 1)
    opposite_part = text_sums(last_weights, last_tail)
    sent = encode(jnp.where(on_first, img_part_tail, opposite_part), ONE_CHIP)
    sent, far_weights, far_tail = lax.optimization_barrier((sent, far_weights, far_tail))
    tail_received = swap(sent)
    far_part = text_sums(far_weights, far_tail)
    sent = encode(jnp.where(on_first, img_part, far_part), ONE_CHIP)
    tail_received, sent, loss = lax.optimization_barrier((tail_received, sent, loss))

    a, b = small_call(
        opposite_kernel, "opposite", core, (opposite_part, img_part_tail, tail_received), (low_half, low_half)
    )
    a, b, sent, near_weights, near_tail = lax.optimization_barrier((a, b, sent, near_weights, near_tail))
    from_a, from_b = move(a, "a"), move(b, "b")
    rest_received = swap(sent)
    near_part = text_sums(near_weights, near_tail)
    sent = encode(near_part, ONE_CHIP)
    loss = loss + swap(loss, 8, 1)
    loss = loss + swap(loss, 0, 2)
    loss = loss + swap(loss, 0, 6)
    (second,) = small_call(
        second_kernel, "second", core, (far_part, rest_received), (low_piece,)
    )
    from_a, from_b, second, sent, loss = lax.optimization_barrier((from_a, from_b, second, sent, loss))

    second_received = move(second, "a")
    x, b = small_call(
        far_kernel,
        "far",
        core,
        (far_part, rest_received, img_part, img_part_tail, tail_received, from_a, from_b),
        (low_piece,) * 2,
    )
    x, b, sent = lax.optimization_barrier((x, b, sent))
    from_x, from_b = move(x, "x"), move(b, "b")
    near_received = swap(sent)
    (base,) = small_call(
        base_kernel, "base", core, (near_part, near_received, img_part, rest_received), (array(wide, jnp.float32),)
    )

    def near_slot(k, received):
        (out,) = small_call(
            lambda *refs: near_kernel(k, *refs), "near", core, (base, received), (low_piece,)
        )
        return out

    from_b, from_x, from_a = (
        move(near_slot(3, second_received), "b"),
        move(near_slot(1, from_b), "x"),
        move(near_slot(2, from_x), "a"),
    )
    loss = loss + swap(loss, 2, 0)
    loss = loss + swap(loss, 6, 0)
    keep, give = small_call(
        gather_sums_kernel,
        "gather_sums",
        core,
        (base, from_a, from_b, from_x, loss),
        (array(own, jnp.float32), array(own + 8, jnp.float32)),
    )
    grad = array(own, jnp.float32)
    loss_value, grad_image, grad_text = small_call(
        lambda *refs: finish_kernel(batch, *refs),
        "finish",
        core,
        (image_embed, text_embed, keep, swap(give), loss),
        (array(1, jnp.float32, 1), grad, grad),
    )
    return (loss_value.reshape(()), grad_image, grad_text)


def solution(mesh):
    in_specs = (P(("row", "col"), None), P(("row", "col"), None), P(), P())
    out_specs = (P(), P(("row", "col"), None), P(("row", "col"), None))
    return jax.shard_map(body, mesh=mesh, in_specs=in_specs, out_specs=out_specs, check_vma=False)
```

```python
import jax
import jax.numpy as jnp
from jax import lax
from jax.experimental import pallas as pl
from jax.experimental.pallas import tpu as pltpu
from jax.sharding import PartitionSpec as P

VMEM = pl.BlockSpec(memory_space=pltpu.VMEM)
SMEM = pl.BlockSpec(memory_space=pltpu.SMEM)
HBM = pl.BlockSpec(memory_space=pltpu.HBM)
MIB = 1024 * 1024
TINY = 1.1754944e-38
AXES = ("row", "col")
ROWS, COLS = 16, 8
ONE_CHIP, TWO_CHIPS, FOUR_CHIPS = 0.5, 0.25, 0.125
PARTNERS = {"x": ((0, 1), (8, 1)), "a": ((0, 2), (2, 0)), "b": ((0, 6), (6, 0))}


def exchange(x, bits_of_core):
    pairs = []
    for row in range(ROWS):
        for col in range(COLS):
            row_bits, col_bits = bits_of_core[row & 1]
            pairs.append((row * COLS + col, (row ^ row_bits) * COLS + (col ^ col_bits)))
    return lax.ppermute(x, AXES, pairs)


def move(x, step):
    return exchange(x, PARTNERS[step])


def swap(x, row_bits=1, col_bits=0):
    return exchange(x, ((row_bits, col_bits),) * 2)


def encode(x, shift):
    y = x * shift
    y2 = y * y
    y4 = y2 * y2
    return (y4 * y2 * (y * jnp.abs(y))).astype(jnp.bfloat16)


def decode(e, shift):
    f = e.astype(jnp.float32)
    size = jnp.exp2(jnp.log2(jnp.maximum(jnp.abs(f), TINY)) * 0.125)
    return jnp.where(f < 0.0, -size, size) * (1.0 / shift)


def row_scale(raw):
    return lax.rsqrt(jnp.sum(raw * raw, axis=1, keepdims=True) + 1e-06)


def by_core(core_ref, work):
    pl.when(core_ref[0] == 0)(lambda: work(True))
    pl.when(core_ref[0] != 0)(lambda: work(False))


def normalize_kernel(core_ref, img_ref, txt_ref, keep_ref, give_ref, raw_ref, sems):
    copies = [
        pltpu.make_async_copy(source, raw_ref.at[k], sems.at[k])
        for k, source in enumerate((txt_ref, img_ref))
    ]
    for copy in copies:
        copy.start()

    def low(k):
        raw = raw_ref[k]
        return (raw * row_scale(raw)).astype(jnp.bfloat16)

    for k, copy in enumerate(copies):
        copy.wait()

        def work(is_first, k=k):
            ref = keep_ref if (k == 0) == is_first else give_ref
            ref[...] = low(k)

        by_core(core_ref, work)


def normalize(core, img, txt):
    low = jax.ShapeDtypeStruct(img.shape, jnp.bfloat16)
    return pl.pallas_call(
        normalize_kernel,
        out_shape=(low, low),
        in_specs=[SMEM, HBM, HBM],
        out_specs=(VMEM, VMEM),
        scratch_shapes=[pltpu.VMEM((2, *img.shape), jnp.float32), pltpu.SemaphoreType.DMA((2,))],
        compiler_params=pltpu.CompilerParams(vmem_limit_bytes=6 * MIB),
        name="normalize",
    )(core, img, txt)


def pack_kernel(*refs):
    out_ref = refs[-1]
    start = 0
    for ref in refs[:-1]:
        out_ref[start : start + ref.shape[0]] = ref[...]
        start += ref.shape[0]


def pack(*pieces):
    shape = (sum(p.shape[0] for p in pieces), pieces[0].shape[1])
    return pl.pallas_call(
        pack_kernel,
        out_shape=jax.ShapeDtypeStruct(shape, pieces[0].dtype),
        in_specs=[VMEM] * len(pieces),
        out_specs=VMEM,
        compiler_params=pltpu.CompilerParams(vmem_limit_bytes=8 * MIB),
        name="pack",
    )(*pieces)


def half_kernel(k, in_ref, out_ref):
    rows = out_ref.shape[0]
    out_ref[...] = in_ref[k * rows : (k + 1) * rows]


def half_of(x, k):
    return pl.pallas_call(
        lambda *refs: half_kernel(k, *refs),
        out_shape=jax.ShapeDtypeStruct((x.shape[0] // 2, x.shape[1]), x.dtype),
        in_specs=[VMEM],
        out_specs=VMEM,
        compiler_params=pltpu.CompilerParams(vmem_limit_bytes=4 * MIB),
        name="half_of",
    )(x)


def run_tiles(pair, sharp_ref, bias_ref, jobs):
    sharp_scalar = jnp.max(sharp_ref[...])
    bias = jnp.max(bias_ref[...])
    steps = [(job, k) for job in jobs for k in range(len(job[1]))]

    def products(step):
        job, k = step
        return lax.dot_general(
            job[0][...], job[1][k][0][...], (((1,), (1,)), ((), ())), preferred_element_type=jnp.float32
        )

    loss = jnp.zeros((8, 128), jnp.float32)
    following = products(steps[0])
    for i, (job, k) in enumerate(steps):
        current = following
        if i + 1 < len(steps):
            following = products(steps[i + 1])
        _, blocks, before, out, corner = job
        texts, weights_out = blocks[k]
        rows, cols = current.shape
        sharp = jnp.exp(jnp.full((1, cols), sharp_scalar, jnp.float32))
        logits = current * sharp + bias
        grown = jnp.exp(logits)
        one_more = 1.0 + grown
        weights = sharp * (grown / one_more)
        weights_out[...] = weights.astype(jnp.bfloat16)
        logs = jnp.log(one_more[: rows // 2] * one_more[rows // 2 :])
        logs = jnp.sum(logs.reshape(rows // 16, 8, cols), axis=0)
        if corner is not None:
            row_ids = lax.broadcasted_iota(jnp.int32, (pair, pair), 0)
            col_ids = lax.broadcasted_iota(jnp.int32, (pair, pair), 1)
            wanted = jnp.where(row_ids < pair // 2, row_ids + pair // 2, row_ids - pair // 2)
            same = (wanted == col_ids) & (corner == 0)
            own = weights[:pair, :pair] - jnp.where(same, sharp[:, :pair], 0.0)
            weights_out[:pair, :pair] = own.astype(jnp.bfloat16)
            matched = jnp.where(same, logits[:pair, :pair], 0.0)
            matched = jnp.sum(matched.reshape(pair // 8, 8, pair), axis=0)
            for start in range(0, pair, 128):
                loss = loss - matched[:, start : start + 128]
        for start in range(0, cols, 128):
            loss = loss + logs[:, start : start + 128]
        part = jnp.dot(weights_out[...], texts[...], preferred_element_type=jnp.float32)
        if k == 0:
            total = part if before is None else part + before[...]
        else:
            total = total + part
        if k == len(blocks) - 1:
            out[...] = total
    return loss


def row_blocks(ref, size, rows=None):
    return [ref.at[pl.ds(start, size)] for start in range(0, rows or ref.shape[0], size)]


def near_tile_kernel(core_ref, sharp_ref, bias_ref, near_ref, received_ref, img_ref, txt_ref, weights_ref, part_ref, loss_ref):
    count = img_ref.shape[0]
    pair = count // 2

    def work(is_first):
        txt_ref[...] = near_ref[...] if is_first else received_ref[...]
        img_ref[...] = received_ref[:count] if is_first else near_ref[count:]

    by_core(core_ref, work)
    jobs = []
    for k, rows in enumerate(row_blocks(img_ref, pair)):
        span = pl.ds(k * pair, pair)
        corner = core_ref[0] if k == 0 else None
        jobs.append((rows, [(txt_ref, weights_ref.at[span])], None, part_ref.at[span], corner))
    loss_ref[...] = run_tiles(pair, sharp_ref, bias_ref, jobs)


def far_tile_kernel(
    core_ref, sharp_ref, bias_ref, far_ref, received_ref, near_img_ref, near_before_ref,
    txt_ref, img_ref, weights_ref, part_ref, loss_ref,
):
    count = near_img_ref.shape[0]
    pair = count // 2

    def work(is_first):
        txt_ref[...] = far_ref[...] if is_first else received_ref[...]
        img_ref[count:] = received_ref[:pair] if is_first else far_ref[count:]

    by_core(core_ref, work)
    img_ref[:count] = near_img_ref[...]
    jobs = []
    before = row_blocks(near_before_ref, pair) + [None]
    for k, rows in enumerate(row_blocks(img_ref, pair)):
        span = pl.ds(k * pair, pair)
        jobs.append((rows, [(txt_ref, weights_ref.at[span])], before[k], part_ref.at[span], None))
    loss_ref[...] = run_tiles(pair, sharp_ref, bias_ref, jobs)


def middle_tile_kernel(
    core_ref, sharp_ref, bias_ref, img_ref, txt_ref, before_ref, near_weights_ref, weights_ref, part_ref, loss_ref
):
    pair = part_ref.shape[0]
    span = pl.ds(2 * pair, pair)
    weights_ref[: 2 * pair] = near_weights_ref[...]
    job = (img_ref.at[span], [(txt_ref, weights_ref.at[span])], before_ref.at[span], part_ref, None)
    loss_ref[...] = run_tiles(pair, sharp_ref, bias_ref, [job])


def last_tile_kernel(
    core_ref, sharp_ref, bias_ref, last_ref, received_ref, far_ref, far_received_ref, near_txt_ref, far_txt_ref,
    img_ref, before_ref, middle_before_ref,
    weights_ref, part_ref, img_tail_ref, near_tail_ref, far_tail_ref, last_tail_ref, part_tail_ref, loss_ref, txt_ref,
):
    pair = last_ref.shape[0]
    half = pair // 2

    def work(is_first):
        txt_ref[...] = last_ref[...] if is_first else received_ref[...]
        img_tail_ref[:half] = far_received_ref[pair : pair + half] if is_first else far_ref[pair + half : 2 * pair]
        img_tail_ref[half:] = received_ref[:half] if is_first else last_ref[half:]

    by_core(core_ref, work)
    jobs = []
    before = row_blocks(before_ref, pair, 2 * pair) + [middle_before_ref]
    for k, rows in enumerate(row_blocks(img_ref, pair)):
        span = pl.ds(k * pair, pair)
        jobs.append((rows, [(txt_ref, weights_ref.at[span])], before[k], part_ref.at[span], None))
    blocks = [(near_txt_ref, near_tail_ref), (far_txt_ref, far_tail_ref), (txt_ref, last_tail_ref)]
    jobs.append((img_tail_ref, blocks, None, part_tail_ref, None))
    loss_ref[...] = run_tiles(pair, sharp_ref, bias_ref, jobs)


def tile_call(kernel, name, pairs, scalars, arrays, outs, scratch=()):
    features = arrays[0].shape[1]
    return pl.pallas_call(
        kernel,
        out_shape=outs,
        in_specs=[SMEM] + [VMEM] * (len(scalars) - 1 + len(arrays)),
        out_specs=(VMEM,) * len(outs),
        scratch_shapes=[pltpu.VMEM(x.shape, x.dtype) for x in scratch],
        compiler_params=pltpu.CompilerParams(vmem_limit_bytes=16 * MIB),
        cost_estimate=pl.CostEstimate(
            flops=4 * pairs * features,
            bytes_accessed=sum(2 * x.size for x in arrays),
            transcendentals=3 * pairs,
        ),
        name=name,
    )(*scalars, *arrays)


def small_call(kernel, name, core, arrays, outs):
    size = sum(x.size * x.dtype.itemsize for x in (*arrays, *outs))
    return pl.pallas_call(
        kernel,
        out_shape=outs,
        in_specs=[SMEM] + [VMEM] * len(arrays),
        out_specs=(VMEM,) * len(outs),
        compiler_params=pltpu.CompilerParams(vmem_limit_bytes=size + 4 * MIB),
        name=name,
    )(core, *arrays)


CHUNK = 64


def each_chunk(rows, work, chunk=CHUNK):
    def step(i, carry):
        first = pl.multiple_of(i * chunk, chunk)
        work(lambda start=0: pl.ds(start + first, chunk))
        return carry

    lax.fori_loop(0, rows // chunk, step, 0)


def opposite_kernel(core_ref, txt_ref, img_ref, received_ref, a_ref, b_ref):
    half = a_ref.shape[0]

    def work(is_first):
        def texts(at):
            a_ref[at()] = encode(txt_ref[at()] + decode(received_ref[at()], ONE_CHIP), ONE_CHIP)
            b_ref[at()] = encode(txt_ref[at(half)] + decode(received_ref[at(half)], ONE_CHIP), ONE_CHIP)

        def images(at):
            a_ref[at()] = received_ref[at(half)]
            b_ref[at()] = encode(img_ref[at(half)], ONE_CHIP)

        each_chunk(half, texts if is_first else images)

    by_core(core_ref, work)


def second_kernel(core_ref, txt_ref, received_ref, out_ref):
    pair = out_ref.shape[0]

    def work(is_first):
        def rows(at):
            if is_first:
                value = txt_ref[at()] + decode(received_ref[at()], ONE_CHIP)
            else:
                value = decode(received_ref[at(2 * pair)], ONE_CHIP)
            out_ref[at()] = encode(value, TWO_CHIPS)

        each_chunk(pair, rows)

    by_core(core_ref, work)


def far_kernel(
    core_ref, txt_ref, txt_received_ref, img_ref, img_tail_ref, tail_received_ref, from_a_ref, from_b_ref, x_ref, b_ref
):
    pair = x_ref.shape[0]
    half = pair // 2

    def work(is_first):
        def rows(at):
            def base(i):
                if is_first:
                    return txt_ref[at(i * half)] + decode(txt_received_ref[at(i * half)], ONE_CHIP)
                if i == 2:
                    return decode(tail_received_ref[at()], ONE_CHIP)
                return img_tail_ref[at()] if i == 3 else img_ref[at(i * half)]

            x_ref[at()] = encode(base(2), TWO_CHIPS)
            x_ref[at(half)] = encode(base(3) + decode(from_b_ref[at()], ONE_CHIP), TWO_CHIPS)
            b_ref[at()] = encode(base(4) + decode(from_a_ref[at()], ONE_CHIP), TWO_CHIPS)
            b_ref[at(half)] = encode(base(5), TWO_CHIPS)

        each_chunk(half, rows)

    by_core(core_ref, work)


def base_kernel(core_ref, txt_ref, received_ref, img_ref, img_received_ref, out_ref):
    count = out_ref.shape[0]
    two = count // 2

    def work(is_first):
        def texts(at):
            out_ref[at()] = txt_ref[at()] + decode(received_ref[at()], ONE_CHIP)

        def images(at):
            out_ref[at()] = decode(img_received_ref[at()], ONE_CHIP)

        if is_first:
            each_chunk(count, texts)
        else:
            each_chunk(two, images)
            out_ref[two:] = img_ref[:two]

    by_core(core_ref, work)


def near_kernel(k, core_ref, base_ref, received_ref, out_ref):
    pair = out_ref.shape[0]

    def rows(at):
        value = base_ref[at(k * pair)] + decode(received_ref[at()], TWO_CHIPS)
        out_ref[at()] = encode(value, FOUR_CHIPS)

    each_chunk(pair, rows, 2 * CHUNK)


def gather_sums_kernel(core_ref, base_ref, a_ref, b_ref, x_ref, loss_ref, keep_ref, give_ref):
    own = keep_ref.shape[0]
    give_ref[own:] = jnp.zeros((8, give_ref.shape[1]), jnp.float32)
    give_ref[own:, :128] = loss_ref[...]

    def rows(at):
        for start, ref in ((0, keep_ref), (own, give_ref)):
            total = base_ref[at(start)] + decode(x_ref[at(start)], FOUR_CHIPS)
            total = total + decode(a_ref[at(start)], FOUR_CHIPS)
            ref[at()] = total + decode(b_ref[at(start)], FOUR_CHIPS)

    each_chunk(own, rows)


def finish_kernel(batch, core_ref, img_ref, txt_ref, kept_ref, received_ref, loss_parts_ref, loss_ref, grad_img_ref, grad_txt_ref):
    own = kept_ref.shape[0]
    both = loss_parts_ref[...] + received_ref[own:, :128]
    loss_ref[...] = jnp.full((1, 1), jnp.sum(both) * (1.0 / batch), jnp.float32)

    def side(at, raw_ref, sum_ref, grad_ref):
        raw = raw_ref[at()]
        scale = row_scale(raw)
        unit = raw * scale
        summed = sum_ref[at()]
        grad_ref[at()] = (summed - unit * jnp.sum(unit * summed, axis=1, keepdims=True)) * scale

    def work(is_first):
        def rows(at):
            side(at, img_ref, received_ref if is_first else kept_ref, grad_img_ref)
            side(at, txt_ref, kept_ref if is_first else received_ref, grad_txt_ref)

        each_chunk(own, rows)

    by_core(core_ref, work)


def transposed_product(weights, img):
    return lax.dot_general(
        weights, img, (((0,), (0,)), ((), ())), preferred_element_type=jnp.float32
    )


def body(image_embed, text_embed, exponent_of_sharpness, bias):
    own, features = image_embed.shape
    pair = 2 * own
    batch = own * ROWS * COLS
    core = lax.axis_index("row") & 1
    core, on_first = lax.optimization_barrier((core.reshape(1), core == 0))

    def array(rows, dtype, columns=features):
        return jax.ShapeDtypeStruct((rows, columns), dtype)

    low_half, low_piece = array(own, jnp.bfloat16), array(pair, jnp.bfloat16)

    keep, give = normalize(core, image_embed, text_embed)
    low = pack(keep, swap(give))
    slot_x, slot_1, slot_3 = move(low, "x"), move(low, "a"), move(low, "b")
    slot_2, slot_x3, slot_x1 = move(slot_3, "a"), move(slot_x, "b"), move(slot_1, "x")
    near = pack(low, slot_x, slot_1, slot_3)
    near_received = swap(near)
    sharpness = jnp.broadcast_to(exponent_of_sharpness.reshape(1, 1), (8, 128))
    shift = jnp.broadcast_to(bias.reshape(1, 1), (8, 128))

    scalars = (core, sharpness, shift)
    losses = array(8, jnp.float32, 128)
    wide, three, two = 4 * pair, 3 * pair, 2 * pair
    near_img, near_txt, near_weights, near_part, near_loss = tile_call(
        near_tile_kernel,
        "tile_near",
        two * wide,
        scalars,
        (near, near_received),
        (
            array(two, jnp.bfloat16),
            array(wide, jnp.bfloat16),
            array(two, jnp.bfloat16, wide),
            array(two, jnp.float32),
            losses,
        ),
    )
    slot_2, slot_x3, slot_x1, near_part = lax.optimization_barrier((slot_2, slot_x3, slot_x1, near_part))
    last_a = move(half_of(slot_x3, 0), "a")
    last_b = move(half_of(slot_x1, 1), "b")
    far = pack(slot_2, slot_x1, slot_x3)
    far_received = swap(far)
    far_txt, img, far_weights, part, far_loss = tile_call(
        far_tile_kernel,
        "tile_far",
        three * three,
        scalars,
        (far, far_received, near_img, near_part),
        (
            array(three, jnp.bfloat16),
            array(three, jnp.bfloat16),
            array(three, jnp.bfloat16, three),
            array(three, jnp.float32),
            losses,
        ),
    )
    last_a, last_b, part = lax.optimization_barrier((last_a, last_b, part))
    last = pack(last_a, last_b)
    last_received = swap(last)
    near_weights, middle_part, middle_loss = tile_call(
        middle_tile_kernel,
        "tile_middle",
        pair * wide,
        scalars,
        (img, near_txt, part, near_weights),
        (array(three, jnp.bfloat16, wide), array(pair, jnp.float32), losses),
    )
    last_weights, img_part, img_tail, near_tail, far_tail, last_tail, img_part_tail, last_loss = tile_call(
        last_tile_kernel,
        "tile_last",
        three * pair + pair * 2 * wide,
        scalars,
        (last, last_received, far, far_received, near_txt, far_txt, img, part, middle_part),
        (
            array(three, jnp.bfloat16, pair),
            array(three, jnp.float32),
            low_piece,
            array(pair, jnp.bfloat16, wide),
            array(pair, jnp.bfloat16, three),
            array(pair, jnp.bfloat16, pair),
            array(pair, jnp.float32),
            losses,
        ),
        (low_piece,),
    )
    loss = near_loss + middle_loss + far_loss + last_loss

    def text_sums(weights, tail):
        return transposed_product(weights, img) + transposed_product(tail, img_tail)

    loss = loss + swap(loss, 0, 1)
    opposite_part = text_sums(last_weights, last_tail)
    sent = encode(jnp.where(on_first, img_part_tail, opposite_part), ONE_CHIP)
    sent, far_weights, far_tail = lax.optimization_barrier((sent, far_weights, far_tail))
    tail_received = swap(sent)
    far_part = text_sums(far_weights, far_tail)
    sent = encode(jnp.where(on_first, img_part, far_part), ONE_CHIP)
    tail_received, sent, loss = lax.optimization_barrier((tail_received, sent, loss))

    a, b = small_call(
        opposite_kernel, "opposite", core, (opposite_part, img_part_tail, tail_received), (low_half, low_half)
    )
    a, b, sent, near_weights, near_tail = lax.optimization_barrier((a, b, sent, near_weights, near_tail))
    from_a, from_b = move(a, "a"), move(b, "b")
    rest_received = swap(sent)
    near_part = text_sums(near_weights, near_tail)
    sent = encode(near_part, ONE_CHIP)
    loss = loss + swap(loss, 8, 1)
    loss = loss + swap(loss, 0, 2)
    (second,) = small_call(
        second_kernel, "second", core, (far_part, rest_received), (low_piece,)
    )
    from_a, from_b, second, sent, loss = lax.optimization_barrier((from_a, from_b, second, sent, loss))

    second_received = move(second, "a")
    x, b = small_call(
        far_kernel,
        "far",
        core,
        (far_part, rest_received, img_part, img_part_tail, tail_received, from_a, from_b),
        (low_piece,) * 2,
    )
    x, b, sent = lax.optimization_barrier((x, b, sent))
    from_x, from_b = move(x, "x"), move(b, "b")
    near_received = swap(sent)
    (base,) = small_call(
        base_kernel, "base", core, (near_part, near_received, img_part, rest_received), (array(wide, jnp.float32),)
    )
    base, loss = lax.optimization_barrier((base, loss))
    loss = loss + swap(loss, 0, 6)
    base, loss = lax.optimization_barrier((base, loss))

    def near_slot(k, received):
        (out,) = small_call(
            lambda *refs: near_kernel(k, *refs), "near", core, (base, received), (low_piece,)
        )
        return out

    from_b, from_x, from_a = (
        move(near_slot(3, second_received), "b"),
        move(near_slot(1, from_b), "x"),
        move(near_slot(2, from_x), "a"),
    )
    loss = loss + swap(loss, 2, 0)
    loss = loss + swap(loss, 6, 0)
    keep, give = small_call(
        gather_sums_kernel,
        "gather_sums",
        core,
        (base, from_a, from_b, from_x, loss),
        (array(own, jnp.float32), array(own + 8, jnp.float32)),
    )
    grad = array(own, jnp.float32)
    loss_value, grad_image, grad_text = small_call(
        lambda *refs: finish_kernel(batch, *refs),
        "finish",
        core,
        (image_embed, text_embed, keep, swap(give), loss),
        (array(1, jnp.float32, 1), grad, grad),
    )
    return (loss_value.reshape(()), grad_image, grad_text)


def solution(mesh):
    in_specs = (P(("row", "col"), None), P(("row", "col"), None), P(), P())
    out_specs = (P(), P(("row", "col"), None), P(("row", "col"), None))
    return jax.shard_map(body, mesh=mesh, in_specs=in_specs, out_specs=out_specs, check_vma=False)
```
